32 devices in a mesh: row: 8 (over z, y), col: 4 (over x, core).
Axes of the slice: x: 2, y: 2, z: 4, core: 2. Of those that a mesh axis runs over, the one named last changes fastest.
Arguments:
- load_currents: float32 [16, 64, 64, 128], P(None, 'row', 'col'), may hold values from -24 to 24
- block_library: float32 [8, 128, 128], replicated, may hold values from -4.0625 to 24.1, as said below
- strap_conductance: float32 [2, 128], replicated, may hold values from 0.5 to 4
- block_types: int32 [64, 64], P('row', 'col'), may hold values from 0 to 7
- aggregate_map: int32 [64, 64], P('row', 'col'), may hold values from 0 to 63, as said below
Outputs:
- node_voltage: float32 [16, 64, 64, 128], P(None, 'row', 'col')
- residual: float32 [16, 64, 64, 128], P(None, 'row', 'col')
The draws below stay inside these ranges and needn't reach their ends.
Inputs may be any that keep to these rules, and one draw needn't show every extreme that they name: `aggregate_map`: each aggregate id names an aggregate of one column group of 16 block columns; the same id in another column group is another aggregate. Every aggregate of every column group holds at least one block. `block_library`: each library block is symmetric positive definite, with nonpositive off-diagonal entries and positive row sums.
All inputs are finite; a program needn't handle non-finite values.
Results may differ from the reference program's by a relative error of at most 0.0003.
Values sent between devices are 32-bit elements; how exact they have to be, the bound alone decides.
No kernel may reach another device: no remote copies, remote signals or barrier semaphores. Data moves between devices by JAX's collectives and lax.ppermute only.
A program may use at most 64 MiB of HBM per device.

```python
import math
import jax
import jax.numpy as jnp
from jax import lax

NODE = 128
LAYERS = 8
SIZ = 16
BC = 16
NT = 8
SWEEPS = 3
ITERS = 2
AGR = 4
AGC = 4
GR = 64
GC = 64
NAGG = 64
N_COL = 4


def draw_load_currents(key, part):
    first, second, third = jax.random.split(key, 3)
    grow = jnp.arange(GR, dtype=jnp.float32)[:, None]
    ramp = 1.0 + 2.0 * grow / max(GR - 1, 1)
    block_scale = 10.0 ** (jax.random.uniform(second, (GR, GC), dtype=jnp.float32) - 1.0) * ramp
    sizing_scale = jax.random.uniform(third, (SIZ, 1, 1, 1), dtype=jnp.float32, minval=0.5, maxval=2.0)
    rough = jnp.clip(jax.random.normal(first, (SIZ, GR, GC, NODE), dtype=jnp.float32), -4.0, 4.0)
    return (rough * block_scale[None, :, :, None] * sizing_scale).astype(jnp.float32)


def log_uniform(key, shape, low, high):
    exponent = jax.random.uniform(key, shape, dtype=jnp.float32, minval=math.log(low), maxval=math.log(high))
    return jnp.exp(exponent)


def draw_block_library(key, part):
    key_lateral, key_via, key_pad, key_leak, key_distant = jax.random.split(key, 5)
    per_layer = NODE // LAYERS
    lateral_wire = log_uniform(key_lateral, (NT, LAYERS, per_layer), 0.5, 4.0)
    via_wire = log_uniform(key_via, (NT, LAYERS, per_layer), 0.5, 4.0)
    pad_ground = log_uniform(key_pad, (NT, 1, per_layer), 0.5, 2.0)
    leakage = log_uniform(key_leak, (NT, NODE), 0.02, 0.1)
    position = jnp.arange(per_layer, dtype=jnp.int32)[None, None, :]
    layer_index = jnp.arange(LAYERS, dtype=jnp.int32)[None, :, None]
    lateral_wire = jnp.where(position < per_layer - 1, lateral_wire, 0.0)
    via_wire = jnp.where(layer_index < LAYERS - 1, via_wire, 0.0)
    lateral_before = jnp.concatenate([jnp.zeros((NT, LAYERS, 1), jnp.float32), lateral_wire[:, :, :-1]], axis=2)
    via_before = jnp.concatenate([jnp.zeros((NT, 1, per_layer), jnp.float32), via_wire[:, :-1, :]], axis=1)
    degree = (lateral_wire + lateral_before + via_wire + via_before).reshape(NT, NODE)
    ground = leakage + jnp.concatenate([pad_ground, jnp.zeros((NT, LAYERS - 1, per_layer), jnp.float32)], axis=1).reshape(NT, NODE)
    lateral_flat = lateral_wire.reshape(NT, NODE)
    via_flat = via_wire.reshape(NT, NODE)
    row_index = jnp.arange(NODE, dtype=jnp.int32)[:, None]
    col_index = jnp.arange(NODE, dtype=jnp.int32)[None, :]
    right_next = (col_index == row_index + 1).astype(jnp.float32)
    left_next = (row_index == col_index + 1).astype(jnp.float32)
    layer_below = (col_index == row_index + per_layer).astype(jnp.float32)
    layer_above = (row_index == col_index + per_layer).astype(jnp.float32)
    sparse_part = lateral_flat[:, :, None] * right_next + lateral_flat[:, None, :] * left_next + via_flat[:, :, None] * layer_below + via_flat[:, None, :] * layer_above
    integer_counts = jax.random.randint(key_distant, (NT, NODE, NODE), 0, 65)
    paired = integer_counts + jnp.swapaxes(integer_counts, 1, 2)
    paired = jnp.where(row_index == col_index, 0, paired)
    far_unit = 1.0 / 2048.0
    distant = paired.astype(jnp.float32) * far_unit
    distant_total = jnp.sum(paired, axis=2).astype(jnp.float32) * far_unit
    identity = (row_index == col_index).astype(jnp.float32)
    centre = degree + distant_total + ground
    return (identity * centre[:, :, None] - sparse_part - distant).astype(jnp.float32)


def draw_aggregate_map(key, part):
    first, second = jax.random.split(key, 2)
    grow = jnp.arange(GR, dtype=jnp.int32)[:, None]
    gcol = jnp.arange(GC, dtype=jnp.int32)[None, :]
    leading = (grow % AGR != 0).astype(jnp.int32)
    jitter = jax.random.randint(first, (GR, GC), 0, 2) * leading
    bands = GR // AGR
    half_span = bands // 2
    band = (grow // AGR + jitter * half_span) % bands
    region = band * (BC // AGC) + gcol % BC // AGC
    labels = jax.random.permutation(second, NAGG)
    return labels[region].astype(jnp.int32)


def touch_ends(values, own_key, least, top_value):
    longest = values.shape.index(max(values.shape))
    spots = []
    for shift in (0, 1):
        where = [jax.random.randint(jax.random.fold_in(own_key, axis), (), 0, length) for axis, length in enumerate(values.shape)]
        where[longest] = (where[longest] + shift) % values.shape[longest]
        spots.append(tuple(where))
    return values.at[spots[0]].set(least).at[spots[1]].set(top_value)


def setup_inputs(seed: int = 0) -> dict:
    arg_keys = jax.random.split(jax.random.key(seed), 6)
    return {
        "load_currents": draw_load_currents(jax.random.fold_in(arg_keys[5], 71), 0),
        "block_library": draw_block_library(jax.random.fold_in(arg_keys[5], 71), 0),
        "strap_conductance": jnp.clip(jnp.exp(jax.random.uniform(arg_keys[2], (2, NODE), jnp.float32, math.log(0.5), math.log(4.0))), 0.5, 4.0),
        "block_types": touch_ends(jax.random.randint(arg_keys[3], (GR, GC), 0, NT), jax.random.fold_in(arg_keys[3], 1), 0, NT - 1).astype(jnp.int32),
        "aggregate_map": draw_aggregate_map(jax.random.fold_in(arg_keys[5], 71), 0),
    }


def block_products(block_library, block_types, field):

    def one_row(pair):
        row_field, row_types = pair
        picked = block_library[row_types]
        return jnp.einsum('cij,scj->sci', picked, row_field, precision=lax.Precision.HIGHEST)
    rows = lax.map(one_row, (jnp.moveaxis(field, 1, 0), block_types))
    return jnp.moveaxis(rows, 0, 1)

def operator(block_library, block_types, strap_conductance, field):
    padded = jnp.pad(field, ((0, 0), (1, 1), (1, 1), (0, 0)))
    north = padded[:, :-2, 1:-1]
    south = padded[:, 2:, 1:-1]
    west = padded[:, 1:-1, :-2]
    east = padded[:, 1:-1, 2:]
    lateral = strap_conductance[0] * (2.0 * field - north - south) + strap_conductance[1] * (2.0 * field - west - east)
    return block_products(block_library, block_types, field) + lateral

def coarse_terms(group_ids, group_types, block_sums, north_weight, east_weight, count):
    centre = block_sums[group_types] + 2.0 * north_weight + 2.0 * east_weight
    flat = group_ids.reshape(-1)
    upper = group_ids[:-1].reshape(-1)
    lower = group_ids[1:].reshape(-1)
    left = group_ids[:, :-1].reshape(-1)
    right = group_ids[:, 1:].reshape(-1)
    index = jnp.concatenate([flat * count + flat, upper * count + lower, lower * count + upper, left * count + right, right * count + left]).astype(jnp.int32)
    values = jnp.concatenate([centre.reshape(-1), -north_weight * jnp.ones((2 * upper.shape[0],), jnp.float32), -east_weight * jnp.ones((2 * left.shape[0],), jnp.float32)])
    return jax.ops.segment_sum(values, index, num_segments=count * count).reshape(count, count)

def reference(load_currents, block_library, strap_conductance, block_types, aggregate_map):
    couple = 2.0 * strap_conductance[0] + 2.0 * strap_conductance[1]
    diag_library = jnp.diagonal(block_library, axis1=1, axis2=2)
    diagonal = diag_library[block_types] + couple
    block_sums = jnp.sum(block_library, axis=(1, 2))
    north_weight = jnp.sum(strap_conductance[0])
    east_weight = jnp.sum(strap_conductance[1])
    factors = []
    for group in range(N_COL):
        group_ids = aggregate_map[:, group * BC:(group + 1) * BC]
        group_types = block_types[:, group * BC:(group + 1) * BC]
        matrix = coarse_terms(group_ids, group_types, block_sums, north_weight, east_weight, NAGG)
        factors.append(jnp.linalg.cholesky(matrix))

    def smooth(residual):
        result = residual / diagonal
        for sweep in range(SWEEPS - 1):
            image = block_products(block_library, block_types, result) + couple * result
            result = result + (residual - image) / diagonal
        return result

    def coarse_part(residual):
        sums = residual.sum(-1)
        pieces = []
        for group in range(N_COL):
            group_ids = aggregate_map[:, group * BC:(group + 1) * BC].reshape(-1)
            local = sums[:, :, group * BC:(group + 1) * BC].reshape(SIZ, -1).T
            gathered = jax.ops.segment_sum(local, group_ids, num_segments=NAGG)
            solved = jax.scipy.linalg.cho_solve((factors[group], True), gathered)
            pieces.append(solved[group_ids].T.reshape(SIZ, GR, BC))
        return jnp.concatenate(pieces, axis=2)[..., None]

    def precondition(residual):
        return smooth(residual) + coarse_part(residual)
    node_voltage = jnp.zeros_like(load_currents)
    residual = load_currents
    zeta = precondition(residual)
    direction = zeta
    aligned = jnp.sum(residual * zeta, axis=(1, 2, 3))
    for iteration in range(ITERS):
        image = operator(block_library, block_types, strap_conductance, direction)
        curvature = jnp.sum(direction * image, axis=(1, 2, 3))
        step_size = (aligned / curvature)[:, None, None, None]
        node_voltage = node_voltage + step_size * direction
        residual = residual - step_size * image
        if iteration + 1 < ITERS:
            zeta = precondition(residual)
            fresh = jnp.sum(residual * zeta, axis=(1, 2, 3))
            blend = (fresh / aligned)[:, None, None, None]
            direction = zeta + blend * direction
            aligned = fresh
    return (node_voltage, residual)
```

```python
import functools

import jax
import jax.numpy as jnp
from jax import lax
from jax.experimental import pallas as pl
from jax.experimental.pallas import tpu as pltpu
from jax.sharding import PartitionSpec as P

AGR = 4
AGC = 4
TILE = 8
GROUP = 2
F32 = jnp.float32
BF16 = jnp.bfloat16
HIGHEST = lax.Precision.HIGHEST
VMEM = pl.BlockSpec(memory_space=pltpu.VMEM)
SMEM = pl.BlockSpec(memory_space=pltpu.SMEM)
PARAMS = pltpu.CompilerParams(vmem_limit_bytes=56 * 1024 * 1024)


def iota(shape, dim):
    return lax.broadcasted_iota(jnp.int32, shape, dim)


def pack(values, count):
    if count < 128:
        fold = 128 // count
        height = values.shape[0] // fold
        return jnp.concatenate(
            [values[p * height : (p + 1) * height, :count] for p in range(fold)], axis=1
        )
    return jnp.concatenate([values[:, j : j + 128] for j in range(0, count, 128)], axis=0)


def unpack(rows, count, sizings):
    if count < 128:
        return jnp.concatenate(
            [rows[:, j : j + count] for j in range(0, 128, count)], axis=0
        )
    return jnp.concatenate(
        [rows[j : j + sizings] for j in range(0, rows.shape[0], sizings)], axis=1
    )


def split3(values):
    first = values.astype(BF16)
    rest = values - first.astype(F32)
    second = rest.astype(BF16)
    third = (rest - second.astype(F32)).astype(BF16)
    return first, second, third


def sums_kernel(dims, ids, ids_row, types_row, load, blocks, top, bottom, pay):
    sizings, rows, cols, nodes, count = dims
    many = rows * cols
    lanes = iota((sizings, max(count, 128)), 1)

    def step(r, sums):
        for c in range(cols):
            b = r * cols + c
            block = load[pl.ds(b, sizings, stride=many), :]
            blocks[pl.ds(pl.multiple_of(b * sizings, sizings), sizings), :] = block
            total = jnp.sum(block, axis=1, keepdims=True)
            sums = sums + jnp.where(lanes == ids[b], total, 0.0)
        return sums

    sums = lax.fori_loop(0, rows, step, jnp.zeros(lanes.shape, F32))
    edge = 2 * cols * sizings
    top[...] = blocks[0:edge, :]
    bottom[...] = blocks[many * sizings - edge : many * sizings, :]
    height = sizings * count // 128
    packed = pack(sums, count)
    spare = jnp.zeros((pay.shape[1] - height - 2, 128), F32)
    whole = jnp.concatenate([packed, ids_row[...], types_row[...], spare], axis=0)

    def copy(d, carry):
        pay[d] = whole
        return carry

    lax.fori_loop(0, pay.shape[0], copy, 0)


def weights_kernel(library, strap, stacked, low, row_sums):
    kinds, nodes, _ = library.shape
    eye = iota((nodes, nodes), 0) == iota((nodes, nodes), 1)
    couple_row = 2.0 * strap[0:1, :] + 2.0 * strap[1:2, :]
    couple_col = jnp.sum(jnp.where(eye, couple_row, 0.0), axis=1, keepdims=True)

    def step(t, carry):
        block = library[t]
        on = jnp.where(eye, block, 0.0)
        inv_row = 1.0 / (jnp.sum(on, axis=0, keepdims=True) + couple_row)
        inv_col = 1.0 / (jnp.sum(on, axis=1, keepdims=True) + couple_col)
        off = jnp.where(eye, 0.0, -block)
        once = inv_col * off * inv_row
        twice = jnp.dot(once, off, precision=HIGHEST, preferred_element_type=F32) * inv_row
        smoother = jnp.where(eye, inv_row, 0.0) + once + twice
        product = jnp.dot(smoother, block, precision=HIGHEST, preferred_element_type=F32)
        both = jnp.concatenate([smoother, product], axis=1)
        high = both.astype(BF16)
        stacked[t] = jnp.concatenate([high, high], axis=0)
        low[t] = (both - high.astype(F32)).astype(BF16)
        row_sums[pl.ds(t, 1), :] = jnp.sum(block, axis=0, keepdims=True)
        return carry

    lax.fori_loop(0, kinds, step, 0)


def sides_kernel(dims, blocks, above, below, west, east):
    sizings, rows, cols, nodes, count = dims
    for out, first in ((west, 0), (east, cols - 2)):
        for side in range(2):
            c = first + side
            for k in range(rows + 2):
                if k == 0:
                    src, at = above, cols + c
                elif k == rows + 1:
                    src, at = below, c
                else:
                    src, at = blocks, (k - 1) * cols + c
                to = (k * 2 + side) * sizings
                out[to : to + sizings, :] = src[at * sizings : (at + 1) * sizings, :]


def sorted_products(order, kinds, pairs, source, stacked, low, sizings, store):
    def step(it, carry):
        for one in range(GROUP):
            tile = it * GROUP + one
            kind = kinds[tile]
            places = [
                pl.ds(pl.multiple_of(order[tile * TILE + j] * sizings, sizings), sizings)
                for j in range(TILE)
            ]
            field = jnp.concatenate([source[place, :] for place in places], axis=0)
            high = field.astype(BF16)
            rest = (field - high.astype(F32)).astype(BF16)
            out = jnp.dot(
                jnp.concatenate([high, rest], axis=1), stacked[kind], preferred_element_type=F32
            ) + jnp.dot(high, low[kind], preferred_element_type=F32)
            store(kind, places, out)
        return carry

    lax.fori_loop(0, pairs, step, 0)


def neighbour_ids(ids, cols):
    height, many = ids.shape
    lane, row = iota(ids.shape, 1), iota(ids.shape, 0)
    down = pltpu.roll(ids, many - cols, 1)
    south = jnp.where(lane < many - cols, down, pltpu.roll(down, height - 1, 0))
    south = jnp.where((lane >= many - cols) & (row == height - 1), -1.0, south)
    up = pltpu.roll(ids, cols, 1)
    north = jnp.where(lane >= cols, up, pltpu.roll(up, 1, 0))
    north = jnp.where((lane < cols) & (row == 0), -1.0, north)
    east = jnp.where(lane % cols == cols - 1, -1.0, pltpu.roll(ids, many - 1, 1))
    west = jnp.where(lane % cols == 0, -1.0, pltpu.roll(ids, 1, 1))
    return south, north, east, west


def invert_unrolled(matrix, count):
    width = matrix.shape[1]
    lane = iota((1, width), 1) % count
    row = iota((count, 1), 0)
    tile_lane = iota((count, 128), 1)
    for k in range(count):
        parts = []
        for base in range(0, width, 128):
            part = jnp.broadcast_to(matrix[:, base + k : base + k + 1], (count, 128))
            for j in range(1, 128 // count):
                at = base + j * count + k
                part = jnp.where(tile_lane >= j * count, matrix[:, at : at + 1], part)
            parts.append(part)
        column = jnp.concatenate(parts, axis=1)
        inverse = 1.0 / column[k : k + 1, :]
        scaled = jnp.where(lane == k, 1.0, matrix[k : k + 1, :]) * inverse
        column = jnp.where(row == k, -1.0, column)
        matrix = jnp.where((lane == k) | (row == k), 0.0, matrix) - column * scaled
    return matrix


def invert_looped(ref, count):
    def step(k, carry):
        for base in range(0, ref.shape[1], count):
            here = slice(base, base + count)
            lane = iota((1, count), 1)
            row = iota((count, 1), 0)
            pivot_row = ref[pl.ds(k, 1), here]
            part = ref[:, here]
            column = jnp.sum(jnp.where(lane == k, part, 0.0), axis=1, keepdims=True)
            inverse = 1.0 / jnp.sum(jnp.where(lane == k, pivot_row, 0.0), axis=1, keepdims=True)
            scaled = jnp.where(lane == k, 1.0, pivot_row) * inverse
            column = jnp.where(row == k, -1.0, column)
            ref[:, here] = jnp.where((lane == k) | (row == k), 0.0, part) - column * scaled
        return carry

    lax.fori_loop(0, count, step, 0)


def coarse_matrices(dims, mesh_dims, gathered, row_sums, strap, inverses, cross, nearby):
    sizings, rows, cols, nodes, count = dims
    n_row, n_col = mesh_dims
    many = rows * cols
    height = sizings * count // 128
    kinds = row_sums.shape[0]
    north_weight = jnp.sum(strap[0:1, :], axis=1, keepdims=True)
    east_weight = jnp.sum(strap[1:2, :], axis=1, keepdims=True)
    block_sums = jnp.sum(row_sums[...], axis=1, keepdims=True)
    names = iota((count, many), 0).astype(F32)
    lane = iota((n_row, many), 1)

    def rows_of(g, at):
        return jnp.concatenate(
            [gathered[i * n_col + g, at : at + 1, :] for i in range(n_row)], axis=0
        )

    all_ids = [rows_of(g, height) for g in range(n_col)]
    eye = iota((count, count), 0) == iota((count, count), 1)
    contract = (((1,), (1,)), ((), ()))
    for g in range(n_col):
        ids = all_ids[g]
        types = rows_of(g, height + 1)
        centre = jnp.zeros(ids.shape, F32) + 2.0 * north_weight + 2.0 * east_weight
        for t in range(kinds):
            centre = centre + jnp.where(types == float(t), block_sums[t : t + 1, :], 0.0)
        beyond = all_ids[min(g + 1, n_col - 1)]
        beyond = jnp.where(lane % cols == cols - 1, pltpu.roll(beyond, cols - 1, 1), -1.0)
        for slot, value in enumerate((ids, *neighbour_ids(ids, cols), beyond, centre)):
            nearby[slot] = value

        def step(i, carry):
            pairs, crossed, diagonal = carry
            hot = [names == nearby[slot, pl.ds(i, 1), :] for slot in range(6)]
            soft = [h.astype(F32).astype(BF16) for h in hot]
            around = jnp.concatenate([soft[1] + soft[2], soft[3] + soft[4], soft[5]], axis=0)
            pairs = pairs + lax.dot_general(
                soft[0], around, contract, preferred_element_type=F32
            )
            diagonal = diagonal + jnp.where(hot[0], nearby[6, pl.ds(i, 1), :], 0.0)
            return pairs, crossed, diagonal

        start = (
            jnp.zeros((count, 3 * count), F32),
            0,
            jnp.zeros((count, many), F32),
        )
        pairs, _, diagonal = lax.fori_loop(0, n_row, step, start, unroll=n_row <= 8)
        diagonal = jnp.sum(diagonal, axis=1, keepdims=True)
        matrix = jnp.where(eye, diagonal, 0.0) - (
            north_weight * pairs[:, :count] + east_weight * pairs[:, count : 2 * count]
        )
        inverses[:, g * count : (g + 1) * count] = matrix
        cross[g] = pairs[:, 2 * count :]


def coarse_solve(gathered, first, height, mesh_dims, count, sizings, inverses, g):
    n_row, n_col = mesh_dims
    total = gathered[g, first : first + height, :]
    for i in range(1, n_row):
        total = total + gathered[i * n_col + g, first : first + height, :]
    sums = unpack(total, count, sizings)
    solved = jnp.dot(
        sums, inverses[:, g * count : (g + 1) * count], precision=HIGHEST,
        preferred_element_type=F32,
    )
    return sums, solved


def spread(solved, col, keys, out, count, sizings, nodes, many):
    three = jnp.concatenate([solved[col], solved[col + 1], solved[col + 2]], axis=1)
    hot = (iota((3 * count, keys.shape[1]), 0) == keys[...]).astype(F32).astype(BF16)
    parts = jnp.concatenate(split3(three), axis=0)
    values = jnp.dot(parts, hot, preferred_element_type=F32)
    values = (
        values[2 * sizings : 3 * sizings] + values[sizings : 2 * sizings] + values[:sizings]
    )
    for e in range(many):
        out[e * sizings : (e + 1) * sizings, :] = jnp.broadcast_to(
            values[:, e : e + 1], (sizings, nodes)
        )


def middle_kernel(
    dims, mesh_dims,
    order_1, kinds_1, order_2, kinds_2, info, ids,
    gathered, keys, blocks, above, below, west, east, stacked, low, row_sums, strap,
    z_out, q_out, u_out, au_out, inverses, cross, pay,
    field, level, z, bz, q, u, bu, solved, nearby,
):
    sizings, rows, cols, nodes, count = dims
    n_row, n_col = mesh_dims
    wide = cols + 4
    many = (rows + 4) * wide
    height = sizings * count // 128

    def at(er, ec):
        return pl.ds(pl.multiple_of((er * wide + ec) * sizings, sizings), sizings)

    span = cols * sizings
    for r in range(rows):
        to = ((r + 2) * wide + 2) * sizings
        field[to : to + span, :] = blocks[r * span : (r + 1) * span, :]
    for r in range(2):
        to = (r * wide + 2) * sizings
        field[to : to + span, :] = above[r * span : (r + 1) * span, :]
        to = ((rows + 2 + r) * wide + 2) * sizings
        field[to : to + span, :] = below[r * span : (r + 1) * span, :]
    for k in range(rows + 2):
        pair = 2 * sizings
        to = (k + 1) * wide * sizings
        field[to : to + pair, :] = west[k * pair : (k + 1) * pair, :]
        to = to + (cols + 2) * sizings
        field[to : to + pair, :] = east[k * pair : (k + 1) * pair, :]
    field[many * sizings :, :] = jnp.zeros((sizings, nodes), F32)
    level[many * sizings :, :] = jnp.zeros((sizings, nodes), F32)
    q[many * sizings :, :] = jnp.zeros((sizings, nodes), F32)

    coarse_matrices(dims, mesh_dims, gathered, row_sums, strap, inverses, cross, nearby)
    if count <= 64:
        inverses[...] = invert_unrolled(inverses[...], count)
    else:
        invert_looped(inverses, count)
    solved[0] = jnp.zeros((sizings, count), F32)
    solved[n_col + 1] = jnp.zeros((sizings, count), F32)
    for g in range(n_col):
        _, solved[g + 1] = coarse_solve(
            gathered, 0, height, mesh_dims, count, sizings, inverses, g
        )
    spread(solved, info[2], keys, level, count, sizings, nodes, many)

    def store_z(kind, places, out):
        sums = row_sums[pl.ds(kind, 1), :]
        for j, place in enumerate(places):
            here = level[place, :]
            z[place, :] = out[j * sizings : (j + 1) * sizings, :nodes] + here
            bz[place, :] = out[j * sizings : (j + 1) * sizings, nodes:] + sums * here

    sorted_products(order_1, kinds_1, info[0], field, stacked, low, sizings, store_z)

    north, east_strap = strap[0:1, :], strap[1:2, :]
    couple = 2.0 * north + 2.0 * east_strap

    def operator(v, bv, er, ec):
        here = v[at(er, ec), :]
        image = (
            bv[at(er, ec), :]
            + couple * here
            - north * (v[at(er - 1, ec), :] + v[at(er + 1, ec), :])
            - east_strap * (v[at(er, ec - 1), :] + v[at(er, ec + 1), :])
        )
        return here, image

    for er, flag in ((1, info[3]), (rows + 2, info[4])):
        inside = flag.astype(F32)

        def across(ec, carry):
            q[at(er, ec), :] = operator(z, bz, er, ec)[1] * inside
            return carry

        lax.fori_loop(2, cols + 2, across, 0)
    for ec, flag in ((1, info[5]), (cols + 2, info[6])):
        inside = flag.astype(F32)

        def along(er, carry):
            q[at(er, ec), :] = operator(z, bz, er, ec)[1] * inside
            return carry

        lax.fori_loop(2, rows + 2, along, 0)

    lanes = iota((sizings, max(count, 128)), 1)
    blank = jnp.zeros((sizings, nodes), F32)
    zero_sums = jnp.zeros(lanes.shape, F32)

    def first_row(r, carry):
        rz, zq, sums = carry
        for c in range(cols):
            here, image = operator(z, bz, r + 2, c + 2)
            q[at(r + 2, c + 2), :] = image
            b = r * cols + c
            own = pl.ds(pl.multiple_of(b * sizings, sizings), sizings)
            z_out[own, :] = here
            q_out[own, :] = image
            rz = rz + blocks[own, :] * here
            zq = zq + here * image
            total = jnp.sum(image, axis=1, keepdims=True)
            sums = sums + jnp.where(lanes == ids[b], total, 0.0)
        return rz, zq, sums

    rz, zq, sums_q = lax.fori_loop(0, rows, first_row, (blank, blank, zero_sums))

    def store_u(kind, places, out):
        for j, place in enumerate(places):
            u[place, :] = out[j * sizings : (j + 1) * sizings, :nodes]
            bu[place, :] = out[j * sizings : (j + 1) * sizings, nodes:]

    sorted_products(order_2, kinds_2, info[1], q, stacked, low, sizings, store_u)

    def second_row(r, carry):
        qu, uau, sums = carry
        for c in range(cols):
            here, image = operator(u, bu, r + 2, c + 2)
            b = r * cols + c
            own = pl.ds(pl.multiple_of(b * sizings, sizings), sizings)
            u_out[own, :] = here
            au_out[own, :] = image
            qu = qu + q[at(r + 2, c + 2), :] * here
            uau = uau + here * image
            total = jnp.sum(image, axis=1, keepdims=True)
            sums = sums + jnp.where(lanes == ids[b], total, 0.0)
        return qu, uau, sums

    qu, uau, sums_u = lax.fori_loop(0, rows, second_row, (blank, blank, zero_sums))

    lane = iota((sizings, 128), 1)
    dots = jnp.zeros((sizings, 128), F32)
    for j, one in enumerate((rz, zq, qu, uau)):
        dots = jnp.where(lane % 4 == j, jnp.sum(one, axis=1, keepdims=True), dots)
    dots = jnp.where(lane // 4 == iota((sizings, 128), 0), dots, 0.0)
    dots = jnp.sum(dots, axis=0, keepdims=True)
    whole = jnp.concatenate([pack(sums_q, count), pack(sums_u, count), dots], axis=0)

    def copy(d, carry):
        pay[d] = whole
        return carry

    lax.fori_loop(0, pay.shape[0], copy, 0)


def last_kernel(
    dims, mesh_dims,
    types, info,
    gathered, keys, inverses, cross, z, q, u, au, blocks, row_sums, strap,
    voltage, residual,
    level, solved,
):
    sizings, rows, cols, nodes, count = dims
    n_row, n_col = mesh_dims
    wide = cols + 4
    many = (rows + 4) * wide
    height = sizings * count // 128
    mesh_args = (mesh_dims, count, sizings)

    solved[0] = jnp.zeros((sizings, count), F32)
    solved[n_col + 1] = jnp.zeros((sizings, count), F32)
    with_q = jnp.zeros((sizings, count), F32)
    with_u = jnp.zeros((sizings, count), F32)
    crossed = jnp.zeros((sizings, count), F32)
    before = None
    for g in range(n_col):
        sums, one = coarse_solve(gathered, 0, height, *mesh_args, inverses, g)
        solved[g + 1] = one
        image = gathered[g, height : 2 * height, :]
        for i in range(1, n_row):
            image = image + gathered[i * n_col + g, height : 2 * height, :]
        with_q = with_q + sums * one
        with_u = with_u + unpack(image, count, sizings) * one
        if before is not None:
            crossed = crossed + one * jnp.dot(
                before, cross[g - 1], precision=HIGHEST, preferred_element_type=F32
            )
        before = one
    spread(solved, info[2], keys, level, count, sizings, nodes, many)

    dots = gathered[0, 2 * height : 2 * height + 1, :]
    for d in range(1, n_row * n_col):
        dots = dots + gathered[d, 2 * height : 2 * height + 1, :]
    lane = iota((sizings, 128), 1)
    dots = jnp.where(lane // 4 == iota((sizings, 128), 0), dots, 0.0)
    rz, zq, qu, uau = [
        jnp.sum(jnp.where(lane % 4 == j, dots, 0.0), axis=1, keepdims=True) for j in range(4)
    ]
    east_weight = jnp.sum(strap[1:2, :], axis=1, keepdims=True)
    total = functools.partial(jnp.sum, axis=1, keepdims=True)
    qw = qu + total(with_q)
    wp = uau + 2.0 * total(with_u) + total(with_q) - 2.0 * east_weight * total(crossed)
    step_1 = rz / zq
    fresh = step_1 * step_1 * qw - rz
    grown = 1.0 + fresh / rz
    step_2 = fresh / (grown * grown * zq - 2.0 * grown * step_1 * qw + step_1 * step_1 * wp)
    alpha = jnp.broadcast_to(step_1 + step_2 * grown, (sizings, nodes))
    gamma = jnp.broadcast_to(-step_2 * step_1, (sizings, nodes))

    north, east_strap = strap[0:1, :], strap[1:2, :]
    couple = 2.0 * north + 2.0 * east_strap

    def step(r, carry):
        for c in range(cols):
            b = r * cols + c
            own = pl.ds(pl.multiple_of(b * sizings, sizings), sizings)

            def value(dr, dc):
                e = (r + 2 + dr) * wide + c + 2 + dc
                return level[pl.ds(pl.multiple_of(e * sizings, sizings), sizings), :]

            here = value(0, 0)
            lift = (
                (row_sums[pl.ds(types[b], 1), :] + couple) * here
                - north * (value(-1, 0) + value(1, 0))
                - east_strap * (value(0, -1) + value(0, 1))
            )
            voltage[pl.ds(b, sizings, stride=rows * cols), :] = alpha * z[own, :] + gamma * (
                u[own, :] + here
            )
            residual[pl.ds(b, sizings, stride=rows * cols), :] = (
                blocks[own, :] - alpha * q[own, :] - gamma * (au[own, :] + lift)
            )
        return carry

    lax.fori_loop(0, rows, step, 0)


def tile_plan(types, needed, kinds, many):
    n = sum(needed)
    most = (n + (TILE - 1) * kinds) // TILE
    most = -(-most // GROUP) * GROUP
    flat = jnp.where(jnp.array(needed), types.reshape(-1), kinds)
    hot = (flat[None, :] == jnp.arange(kinds)[:, None]).astype(jnp.int32)
    index = jnp.arange(many)
    rank = jnp.dot(
        hot.astype(BF16), (index[:, None] < index[None, :]).astype(BF16),
        preferred_element_type=F32,
    ).astype(jnp.int32)
    tiles = (jnp.sum(hot, axis=1) + TILE - 1) // TILE
    below = jnp.arange(kinds)[:, None] >= jnp.arange(kinds)[None, :]
    ends = jnp.sum(jnp.where(below, tiles[None, :], 0), axis=1)
    starts = ends - tiles
    place = jnp.sum(hot * (starts[:, None] * TILE + rank + 1), axis=0) - 1
    slots = jnp.arange(most * TILE)
    order = many + jnp.sum(
        jnp.where(place[None, :] == slots[:, None], index[None, :] - many, 0), axis=1
    )
    tile_kinds = jnp.sum(jnp.arange(most)[:, None] >= ends[None, :], axis=1)
    tile_kinds = jnp.minimum(tile_kinds, kinds - 1)
    groups = (ends[-1] + GROUP - 1) // GROUP
    return order.astype(jnp.int32), tile_kinds.astype(jnp.int32), groups.astype(jnp.int32)


def call(kernel, in_specs, out_shape, scratch, cost):
    return pl.pallas_call(
        kernel,
        in_specs=in_specs,
        out_specs=jax.tree.map(lambda _: VMEM, out_shape),
        out_shape=out_shape,
        scratch_shapes=scratch,
        compiler_params=PARAMS,
        cost_estimate=pl.CostEstimate(flops=cost, bytes_accessed=4_000_000, transcendentals=0),
    )


def on_device(load_currents, block_library, strap_conductance, block_types, aggregate_map):
    sizings, rows, cols, nodes = load_currents.shape
    kinds = block_library.shape[0]
    n_row, n_col = lax.axis_size("row"), lax.axis_size("col")
    n_dev = n_row * n_col
    row, col = lax.axis_index("row"), lax.axis_index("col")
    count = rows * n_row // AGR * (cols // AGC)
    dims, mesh_dims = (sizings, rows, cols, nodes, count), (n_row, n_col)
    block_rows = rows * cols * sizings
    wide, tall = cols + 4, rows + 4
    many = wide * tall
    height = sizings * count // 128
    shape = jax.ShapeDtypeStruct

    edge = shape((2 * cols * sizings, nodes), F32)
    own = shape((block_rows, nodes), F32)
    ids = aggregate_map.reshape(-1)
    types = block_types.reshape(-1)
    pay_rows = -(-(height + 2) // 8) * 8
    blocks, top, bottom, pay = call(
        functools.partial(sums_kernel, dims),
        [SMEM] + [VMEM] * 3,
        [own, edge, edge, shape((n_dev, pay_rows, 128), F32)],
        [],
        1_000_000,
    )(
        ids,
        ids.reshape(1, -1).astype(F32),
        types.reshape(1, -1).astype(F32),
        load_currents.reshape(-1, nodes),
    )
    forth = [(i, i + 1) for i in range(n_row - 1)]
    above = lax.ppermute(bottom, "row", forth)
    below = lax.ppermute(top, "row", [(j, i) for i, j in forth])
    gathered = lax.all_to_all(pay, ("row", "col"), 0, 0)
    stacked, low, row_sums = call(
        weights_kernel,
        [VMEM, VMEM],
        [
            shape((kinds, 2 * nodes, 2 * nodes), BF16),
            shape((kinds, nodes, 2 * nodes), BF16),
            shape((kinds, nodes), F32),
        ],
        [],
        1_000_000_000,
    )(block_library, strap_conductance)
    side = shape(((rows + 2) * 2 * sizings, nodes), F32)
    to_west, to_east = call(
        functools.partial(sides_kernel, dims), [VMEM] * 3, [side, side], [], 1_000_000
    )(blocks, above, below)
    forth = [(i, i + 1) for i in range(n_col - 1)]
    west = lax.ppermute(to_east, "col", forth)
    east = lax.ppermute(to_west, "col", [(j, i) for i, j in forth])

    def die(at):
        whole = gathered[:, at, :].astype(jnp.int32).reshape(n_row, n_col, rows, cols)
        whole = whole.transpose(0, 2, 1, 3).reshape(n_row * rows, n_col * cols)
        whole = jnp.pad(whole, 2, constant_values=-1)
        return lax.dynamic_slice(whole, (row * rows, col * cols), (tall, wide))

    place = jnp.arange(wide)
    relative = (place >= 2).astype(jnp.int32) + (place >= cols + 2).astype(jnp.int32)
    near_ids, near_types = die(height), jnp.maximum(die(height + 1), 0)
    keys = jnp.where(near_ids >= 0, near_ids + relative[None, :] * count, -1).reshape(1, -1)
    keys = jnp.pad(keys, ((0, 0), (0, -many % 128)), constant_values=-1)

    def ring(er, ec):
        down = max(2 - er, er - (rows + 1), 0)
        over = max(2 - ec, ec - (cols + 1), 0)
        return down, over

    rings = [ring(er, ec) for er in range(tall) for ec in range(wide)]
    needed_1 = [down + over <= 2 for down, over in rings]
    needed_2 = [down + over <= 1 for down, over in rings]
    order_1, kinds_1, groups_1 = tile_plan(near_types, needed_1, kinds, many)
    order_2, kinds_2, groups_2 = tile_plan(near_types, needed_2, kinds, many)
    info = jnp.stack(
        [
            groups_1,
            groups_2,
            col,
            (row > 0).astype(jnp.int32),
            (row < n_row - 1).astype(jnp.int32),
            (col > 0).astype(jnp.int32),
            (col < n_col - 1).astype(jnp.int32),
        ]
    )
    big = pltpu.VMEM(((many + 1) * sizings, nodes), F32)
    coarse = pltpu.VMEM((n_col + 2, sizings, count), F32)
    z, q, u, au, inverses, cross, pay = call(
        functools.partial(middle_kernel, dims, mesh_dims),
        [SMEM] * 6 + [VMEM] * 11,
        [own] * 4
        + [
            shape((count, n_col * count), F32),
            shape((n_col, count, count), F32),
            shape((n_dev, 2 * height + 1, 128), F32),
        ],
        [big] * 7 + [coarse, pltpu.VMEM((7, n_row, rows * cols), F32)],
        1_000_000_000,
    )(
        order_1, kinds_1, order_2, kinds_2, info, ids,
        gathered, keys, blocks, above, below, west, east, stacked, low, row_sums,
        strap_conductance,
    )
    gathered = lax.all_to_all(pay, ("row", "col"), 0, 0)
    out = shape((sizings * rows * cols, nodes), F32)
    voltage, residual = call(
        functools.partial(last_kernel, dims, mesh_dims),
        [SMEM] * 2 + [VMEM] * 11,
        [out, out],
        [big, coarse],
        1_000_000_000,
    )(
        types, info,
        gathered, keys, inverses, cross, z, q, u, au, blocks, row_sums, strap_conductance,
    )
    return voltage.reshape(load_currents.shape), residual.reshape(load_currents.shape)


def solution(mesh):
    placed = (P(None, "row", "col", None), P(), P(), P("row", "col"), P("row", "col"))
    return jax.shard_map(
        on_device,
        mesh=mesh,
        in_specs=placed,
        out_specs=(P(None, "row", "col", None), P(None, "row", "col", None)),
        check_vma=False,
    )
```

```python
import functools

import jax
import jax.numpy as jnp
from jax import lax
from jax.experimental import pallas as pl
from jax.experimental.pallas import tpu as pltpu
from jax.sharding import PartitionSpec as P
import numpy as np

AGR = 4
AGC = 4
TILE = 8
GROUP = 2
PANEL = 8
F32 = jnp.float32
BF16 = jnp.bfloat16
HIGHEST = lax.Precision.HIGHEST
VMEM = pl.BlockSpec(memory_space=pltpu.VMEM)
SMEM = pl.BlockSpec(memory_space=pltpu.SMEM)


def iota(shape, dim):
    return lax.broadcasted_iota(jnp.int32, shape, dim)


def pack(values, count):
    if count < 128:
        fold = 128 // count
        height = values.shape[0] // fold
        return jnp.concatenate(
            [values[p * height : (p + 1) * height, :count] for p in range(fold)], axis=1
        )
    return jnp.concatenate([values[:, j : j + 128] for j in range(0, count, 128)], axis=0)


def unpack(rows, count, sizings):
    if count < 128:
        return jnp.concatenate(
            [rows[:, j : j + count] for j in range(0, 128, count)], axis=0
        )
    return jnp.concatenate(
        [rows[j : j + sizings] for j in range(0, rows.shape[0], sizings)], axis=1
    )


def split3(values):
    first = values.astype(BF16)
    rest = values - first.astype(F32)
    second = rest.astype(BF16)
    third = (rest - second.astype(F32)).astype(BF16)
    return first, second, third


def flat_row(table, many):
    rows, cols = table.shape
    repeat = (iota((cols, many), 1) % cols == iota((cols, many), 0)).astype(F32).astype(BF16)
    wide = jnp.dot(table.astype(F32).astype(BF16), repeat, preferred_element_type=F32)
    own = iota((rows, many), 1) // cols == iota((rows, many), 0)
    return jnp.sum(jnp.where(own, wide, 0.0), axis=0, keepdims=True)


def meta_rows(types, ids, many, height):
    rows = [flat_row(types[...], many), flat_row(ids[...], many) + 1.0]
    return jnp.concatenate(rows + [jnp.zeros((height - 2, many), F32)], axis=0)


def edges_kernel(dims, load, types, ids, top, bottom, sems):
    sizings, rows, cols, nodes, count = dims
    many = rows * cols
    copies = [
        pltpu.make_async_copy(
            load.at[:, pl.ds(first, 2)], out.at[pl.ds(0, sizings)], sems.at[i]
        )
        for i, (out, first) in enumerate(((top, 0), (bottom, rows - 2)))
    ]
    for copy in copies:
        copy.start()
    meta = meta_rows(types, ids, many, cols)
    blank = jnp.zeros((cols, nodes), F32)
    top[sizings, 0] = meta
    top[sizings, 1] = blank
    bottom[sizings, 0] = pltpu.roll(meta, 2 * cols, 1)
    bottom[sizings, 1] = blank
    for copy in copies:
        copy.wait()


def sums_kernel(dims, ids_smem, types, ids, load, blocks, pay):
    sizings, rows, cols, nodes, count = dims
    many = rows * cols
    lanes = iota((sizings, max(count, 128)), 1)

    def step(r, sums):
        for c in range(cols):
            b = r * cols + c
            block = load[pl.ds(b, sizings, stride=many), :]
            blocks[pl.ds(pl.multiple_of(b * sizings, sizings), sizings), :] = block
            total = jnp.sum(block, axis=1, keepdims=True)
            sums = sums + jnp.where(lanes == ids_smem[r, c], total, 0.0)
        return sums

    sums = lax.fori_loop(0, rows, step, jnp.zeros(lanes.shape, F32))
    height = sizings * count // 128
    meta = meta_rows(types, ids, many, pay.shape[1] - height)
    whole = jnp.concatenate([pack(sums, count), meta], axis=0)

    def copy(d, carry):
        pay[d] = whole
        return carry

    lax.fori_loop(0, pay.shape[0], copy, 0)


def weights_kernel(library, strap, stacked, low, row_sums):
    kinds, nodes, _ = library.shape
    eye = iota((nodes, nodes), 0) == iota((nodes, nodes), 1)
    couple_row = 2.0 * strap[0:1, :] + 2.0 * strap[1:2, :]
    couple_col = jnp.sum(jnp.where(eye, couple_row, 0.0), axis=1, keepdims=True)

    def step(t, carry):
        block = library[t]
        on = jnp.where(eye, block, 0.0)
        inv_row = 1.0 / (jnp.sum(on, axis=0, keepdims=True) + couple_row)
        inv_col = 1.0 / (jnp.sum(on, axis=1, keepdims=True) + couple_col)
        off = jnp.where(eye, 0.0, -block)
        once = inv_col * off * inv_row
        twice = jnp.dot(once, off, precision=HIGHEST, preferred_element_type=F32) * inv_row
        smoother = jnp.where(eye, inv_row, 0.0) + once + twice
        product = jnp.dot(smoother, block, precision=HIGHEST, preferred_element_type=F32)
        both = jnp.concatenate([smoother, product], axis=1)
        high = both.astype(BF16)
        stacked[t] = jnp.concatenate([high, high], axis=0)
        low[t] = (both - high.astype(F32)).astype(BF16)
        row_sums[pl.ds(t, 1), :] = jnp.sum(block, axis=0, keepdims=True)
        return carry

    lax.fori_loop(0, kinds, step, 0, unroll=True)


def sides_kernel(dims, types, ids, blocks, above, below, west, east):
    sizings, rows, cols, nodes, count = dims
    last = sizings * 2 * cols
    own = meta_rows(types, ids, rows * cols, 8)
    metas = [own, above[last : last + 8, :], below[last : last + 8, :]]
    metas = jnp.concatenate(metas, axis=1).astype(BF16)
    shape = (metas.shape[1], 128)
    slot, lane = iota(shape, 0), iota(shape, 1)
    for out, first in ((west, 0), (east, cols - 2)):
        for side in range(2):
            c = first + side
            for k in range(rows + 2):
                to = (k * 2 + side) * sizings
                if k == 0:
                    block = above[pl.ds(cols + c, sizings, stride=2 * cols), :]
                elif k == rows + 1:
                    block = below[pl.ds(c, sizings, stride=2 * cols), :]
                else:
                    at = ((k - 1) * cols + c) * sizings
                    block = blocks[at : at + sizings, :]
                out[to : to + sizings, :] = block
        k = lane // 2
        place = (k - 1) * cols
        place = jnp.where(k == 0, rows * cols + cols, place)
        place = jnp.where(k == rows + 1, 2 * rows * cols, place) + first + lane % 2
        pick = (slot == place) & (k < rows + 2)
        picked = jnp.dot(metas, pick.astype(F32).astype(BF16), preferred_element_type=F32)
        out[(rows + 2) * 2 * sizings :, :] = picked


def order_kernel(dims, kinds, lengths, maps, types, ids, above, below, west, east, plan, keys):
    sizings, rows, cols, nodes, count = dims
    many = rows * cols
    own = meta_rows(types, ids, many, 8)
    metas = jnp.concatenate([own, above[...], below[...], west[...], east[...]], axis=1)
    shape = (metas.shape[1], maps.shape[1])
    pick = (iota(shape, 0) == maps[0:1, :]).astype(F32).astype(BF16)
    near = jnp.dot(metas.astype(BF16), pick, preferred_element_type=F32)
    near_types, near_ids = near[0:1, :], near[1:2, :]
    keys[...] = jnp.where(
        near_ids > 0.0, near_ids - 1.0 + maps[3:4, :].astype(F32), -1.0
    ).astype(jnp.int32)

    length = maps.shape[1]
    total = (rows + 4) * (cols + 4)
    before = (iota((length, length), 0) < iota((length, length), 1)).astype(F32).astype(BF16)
    upto = (iota((kinds, kinds), 0) >= iota((kinds, kinds), 1)).astype(F32).astype(BF16)
    slot = iota((plan.shape[1], length), 0).astype(F32)
    slot_row = iota((kinds, plan.shape[1]), 1).astype(F32)
    side = iota((8, length), 0)
    index = jnp.where(side == 0, iota((8, length), 1), jnp.where(side == 1, 1, 0))
    index = index.astype(F32).astype(BF16)
    orders, tile_kinds, groups = [], [], []
    for which in (1, 2):
        needed = maps[which : which + 1, :] > 0
        hot = (iota((kinds, length), 0).astype(F32) == near_types) & needed
        hot = hot.astype(F32)
        rank = jnp.dot(hot.astype(BF16), before, preferred_element_type=F32)
        tiles = jnp.floor((jnp.sum(hot, axis=1, keepdims=True) + (TILE - 1)) * (1.0 / TILE))
        tiles = jnp.broadcast_to(tiles, (kinds, 128))
        ends = jnp.dot(upto, tiles.astype(BF16), preferred_element_type=F32)
        starts = (ends - tiles)[:, :1]
        place = jnp.sum(hot * (starts * TILE + rank + 1.0), axis=0, keepdims=True) - 1.0
        hit = (slot == place).astype(F32).astype(BF16)
        found = lax.dot_general(
            index, hit, (((1,), (1,)), ((), ())), preferred_element_type=F32
        )
        orders.append(found[0:1, :] + float(total) * (1.0 - found[1:2, :]))
        kind = jnp.sum(jnp.where(slot_row >= ends[:, :1], 1.0, 0.0), axis=0, keepdims=True)
        tile_kinds.append(jnp.minimum(kind, kinds - 1.0))
        last = jnp.floor((ends[kinds - 1 : kinds, :1] + (GROUP - 1)) * (1.0 / GROUP))
        groups.append(jnp.broadcast_to(last, (1, plan.shape[1])))
    rest = jnp.zeros((2, plan.shape[1]), F32)
    whole = jnp.concatenate(orders + tile_kinds + groups + [rest], axis=0)
    plan[...] = whole.astype(jnp.int32)


def sorted_products(plan, which, source, stacked, low, sizings, store):
    def step(it, carry):
        for one in range(GROUP):
            tile = it * GROUP + one
            kind = plan[2 + which, tile]
            places = [
                pl.ds(pl.multiple_of(plan[which, tile * TILE + j] * sizings, sizings), sizings)
                for j in range(TILE)
            ]
            field = jnp.concatenate([source[place, :] for place in places], axis=0)
            high = field.astype(BF16)
            rest = (field - high.astype(F32)).astype(BF16)
            out = jnp.dot(
                jnp.concatenate([high, rest], axis=1), stacked[kind], preferred_element_type=F32
            ) + jnp.dot(high, low[kind], preferred_element_type=F32)
            store(kind, places, out)
        return carry

    lax.fori_loop(0, plan[4 + which, 0], step, 0)


def neighbour_ids(ids, cols):
    height, many = ids.shape
    lane, row = iota(ids.shape, 1), iota(ids.shape, 0)
    down = pltpu.roll(ids, many - cols, 1)
    south = jnp.where(lane < many - cols, down, pltpu.roll(down, height - 1, 0))
    south = jnp.where((lane >= many - cols) & (row == height - 1), -1.0, south)
    up = pltpu.roll(ids, cols, 1)
    north = jnp.where(lane >= cols, up, pltpu.roll(up, 1, 0))
    north = jnp.where((lane < cols) & (row == 0), -1.0, north)
    east = jnp.where(lane % cols == cols - 1, -1.0, pltpu.roll(ids, many - 1, 1))
    west = jnp.where(lane % cols == 0, -1.0, pltpu.roll(ids, 1, 1))
    return south, north, east, west


def invert_unrolled(ref, count):
    width = ref.shape[1]
    fold = 128 // count
    lane = iota((8, width), 1) % count
    row = iota((8, width), 0)
    tile_lane = iota((8, 128), 1)
    many = count // 8
    tiles = [ref[i * 8 : (i + 1) * 8, :] for i in range(many)]

    def column(tile, k):
        parts = []
        for base in range(0, width, 128):
            part = jnp.broadcast_to(tile[:, base + k : base + k + 1], (8, 128))
            for j in range(1, fold):
                at = base + j * count + k
                part = jnp.where(tile_lane >= j * count, tile[:, at : at + 1], part)
            parts.append(part)
        return jnp.concatenate(parts, axis=1)

    for first in range(0, count, PANEL):
        columns = [[column(t, first + j) for t in tiles] for j in range(PANEL)]
        for j in range(PANEL):
            k = first + j
            at, within = k // 8, k % 8
            here = columns[j]
            inverse = 1.0 / here[at][within : within + 1, :]
            scaled = jnp.where(
                lane[:1] == k, inverse, tiles[at][within : within + 1, :] * inverse
            )
            pivot = row == within
            for i in range(many):
                new = jnp.where(lane == k, 0.0, tiles[i]) - here[i] * scaled
                tiles[i] = jnp.where(pivot, scaled, new) if i == at else new
            for later in range(j + 1, PANEL):
                other = columns[later]
                factor = other[at][within : within + 1, :] * inverse
                for i in range(many):
                    new = other[i] - here[i] * factor
                    other[i] = jnp.where(pivot, factor, new) if i == at else new
    for i in range(many):
        ref[i * 8 : (i + 1) * 8, :] = tiles[i]


def invert_looped(ref, count):
    def step(k, carry):
        for base in range(0, ref.shape[1], count):
            here = slice(base, base + count)
            lane = iota((1, count), 1)
            row = iota((count, 1), 0)
            pivot_row = ref[pl.ds(k, 1), here]
            part = ref[:, here]
            column = jnp.sum(jnp.where(lane == k, part, 0.0), axis=1, keepdims=True)
            inverse = 1.0 / jnp.sum(jnp.where(lane == k, pivot_row, 0.0), axis=1, keepdims=True)
            scaled = jnp.where(lane == k, 1.0, pivot_row) * inverse
            column = jnp.where(row == k, -1.0, column)
            ref[:, here] = jnp.where((lane == k) | (row == k), 0.0, part) - column * scaled
        return carry

    lax.fori_loop(0, count, step, 0)


def coarse_matrices(dims, mesh_dims, gathered, row_sums, strap, inverses, cross):
    sizings, rows, cols, nodes, count = dims
    n_row, n_col = mesh_dims
    many = rows * cols
    height = sizings * count // 128
    kinds = row_sums.shape[0]
    north_weight = jnp.sum(strap[0:1, :], axis=1, keepdims=True)
    east_weight = jnp.sum(strap[1:2, :], axis=1, keepdims=True)
    names = iota((count, many), 0).astype(F32).astype(BF16)
    kind_names = iota((16, many), 0).astype(F32).astype(BF16)
    lane = iota((n_row, many), 1)
    eye = iota((count, count), 0) == iota((count, count), 1)
    contract = (((1,), (1,)), ((), ()))
    spot = iota((kinds, 16), 0) == iota((kinds, 16), 1)
    centre = jnp.sum(row_sums[...], axis=1, keepdims=True) + 2.0 * north_weight
    centre = centre + 2.0 * east_weight
    centre = jnp.sum(jnp.where(spot, centre, 0.0), axis=0, keepdims=True)

    def rows_of(g, at):
        return jnp.concatenate(
            [gathered[i * n_col + g, at : at + 1, :] for i in range(n_row)], axis=0
        )

    def hot(values, labels):
        rows_bf = values.astype(BF16)
        one, zero = jnp.ones(labels.shape, BF16), jnp.zeros(labels.shape, BF16)
        return [
            jnp.where(labels == rows_bf[i : i + 1, :], one, zero) for i in range(n_row)
        ]

    all_ids = [rows_of(g, height + 1) - 1.0 for g in range(n_col)]
    for g in range(n_col):
        ids = all_ids[g]
        beyond = all_ids[min(g + 1, n_col - 1)]
        beyond = jnp.where(lane % cols == cols - 1, pltpu.roll(beyond, cols - 1, 1), -1.0)
        south, north, east, west = [hot(v, names) for v in neighbour_ids(ids, cols)]
        own, over = hot(ids, names), hot(beyond, names)
        types = hot(rows_of(g, height), kind_names)
        right = jnp.concatenate(
            [
                jnp.concatenate([south[i] + north[i], east[i] + west[i], over[i], types[i]], axis=0)
                for i in range(n_row)
            ],
            axis=1,
        )
        pairs = lax.dot_general(
            jnp.concatenate(own, axis=1), right, contract, preferred_element_type=F32
        )
        diagonal = jnp.sum(pairs[:, 3 * count :] * centre, axis=1, keepdims=True)
        inverses[:, g * count : (g + 1) * count] = jnp.where(eye, diagonal, 0.0) - (
            north_weight * pairs[:, :count] + east_weight * pairs[:, count : 2 * count]
        )
        cross[g] = pairs[:, 2 * count : 3 * count]


def coarse_solve(gathered, first, height, mesh_dims, count, sizings, inverses, g):
    n_row, n_col = mesh_dims
    total = gathered[g, first : first + height, :]
    for i in range(1, n_row):
        total = total + gathered[i * n_col + g, first : first + height, :]
    sums = unpack(total, count, sizings)
    solved = jnp.dot(
        sums, inverses[:, g * count : (g + 1) * count], precision=HIGHEST,
        preferred_element_type=F32,
    )
    return sums, solved


def spread(solved, col, keys, out, count, sizings, nodes, many):
    three = jnp.concatenate([solved[col], solved[col + 1], solved[col + 2]], axis=1)
    hot = (iota((3 * count, keys.shape[1]), 0) == keys[...]).astype(F32).astype(BF16)
    parts = jnp.concatenate(split3(three), axis=0)
    values = jnp.dot(parts, hot, preferred_element_type=F32)
    values = (
        values[2 * sizings : 3 * sizings] + values[sizings : 2 * sizings] + values[:sizings]
    )
    for e in range(many):
        out[e * sizings : (e + 1) * sizings, :] = jnp.broadcast_to(
            values[:, e : e + 1], (sizings, nodes)
        )


def middle_kernel(
    dims, mesh_dims,
    plan, info, ids,
    gathered, keys, blocks, above, below, west, east, stacked, low, row_sums, strap,
    z_out, q_out, u_out, au_out, inverses, cross, pay,
    field, level, z, bz, q, u, bu, solved,
):
    sizings, rows, cols, nodes, count = dims
    n_row, n_col = mesh_dims
    wide = cols + 4
    many = (rows + 4) * wide
    height = sizings * count // 128

    def at(er, ec):
        return pl.ds(pl.multiple_of((er * wide + ec) * sizings, sizings), sizings)

    span = cols * sizings
    for r in range(rows):
        to = ((r + 2) * wide + 2) * sizings
        field[to : to + span, :] = blocks[r * span : (r + 1) * span, :]
    for r in range(2):
        for c in range(cols):
            from_edge = pl.ds(r * cols + c, sizings, stride=2 * cols)
            to = (r * wide + 2 + c) * sizings
            field[to : to + sizings, :] = above[from_edge, :]
            to = ((rows + 2 + r) * wide + 2 + c) * sizings
            field[to : to + sizings, :] = below[from_edge, :]
    for k in range(rows + 2):
        pair = 2 * sizings
        to = (k + 1) * wide * sizings
        field[to : to + pair, :] = west[k * pair : (k + 1) * pair, :]
        to = to + (cols + 2) * sizings
        field[to : to + pair, :] = east[k * pair : (k + 1) * pair, :]
    field[many * sizings :, :] = jnp.zeros((sizings, nodes), F32)
    level[many * sizings :, :] = jnp.zeros((sizings, nodes), F32)
    q[many * sizings :, :] = jnp.zeros((sizings, nodes), F32)

    coarse_matrices(dims, mesh_dims, gathered, row_sums, strap, inverses, cross)
    if count <= 64:
        invert_unrolled(inverses, count)
    else:
        invert_looped(inverses, count)
    solved[0] = jnp.zeros((sizings, count), F32)
    solved[n_col + 1] = jnp.zeros((sizings, count), F32)
    for g in range(n_col):
        _, solved[g + 1] = coarse_solve(
            gathered, 0, height, mesh_dims, count, sizings, inverses, g
        )
    spread(solved, info[0], keys, level, count, sizings, nodes, many)

    def store_z(kind, places, out):
        sums = row_sums[pl.ds(kind, 1), :]
        for j, place in enumerate(places):
            here = level[place, :]
            z[place, :] = out[j * sizings : (j + 1) * sizings, :nodes] + here
            bz[place, :] = out[j * sizings : (j + 1) * sizings, nodes:] + sums * here

    sorted_products(plan, 0, field, stacked, low, sizings, store_z)

    north, east_strap = strap[0:1, :], strap[1:2, :]
    couple = 2.0 * north + 2.0 * east_strap

    def operator(v, bv, er, ec):
        here = v[at(er, ec), :]
        image = (
            bv[at(er, ec), :]
            + couple * here
            - north * (v[at(er - 1, ec), :] + v[at(er + 1, ec), :])
            - east_strap * (v[at(er, ec - 1), :] + v[at(er, ec + 1), :])
        )
        return here, image

    for er, flag in ((1, info[1]), (rows + 2, info[2])):
        inside = flag.astype(F32)

        def across(ec, carry):
            q[at(er, ec), :] = operator(z, bz, er, ec)[1] * inside
            return carry

        lax.fori_loop(2, cols + 2, across, 0)
    for ec, flag in ((1, info[3]), (cols + 2, info[4])):
        inside = flag.astype(F32)

        def along(er, carry):
            q[at(er, ec), :] = operator(z, bz, er, ec)[1] * inside
            return carry

        lax.fori_loop(2, rows + 2, along, 0)

    lanes = iota((sizings, max(count, 128)), 1)
    blank = jnp.zeros((sizings, nodes), F32)
    zero_sums = jnp.zeros(lanes.shape, F32)

    def first_row(r, carry):
        rz, zq, sums = carry
        for c in range(cols):
            here, image = operator(z, bz, r + 2, c + 2)
            q[at(r + 2, c + 2), :] = image
            b = r * cols + c
            own = pl.ds(pl.multiple_of(b * sizings, sizings), sizings)
            z_out[own, :] = here
            q_out[own, :] = image
            rz = rz + blocks[own, :] * here
            zq = zq + here * image
            total = jnp.sum(image, axis=1, keepdims=True)
            sums = sums + jnp.where(lanes == ids[r, c], total, 0.0)
        return rz, zq, sums

    rz, zq, sums_q = lax.fori_loop(0, rows, first_row, (blank, blank, zero_sums))

    def store_u(kind, places, out):
        for j, place in enumerate(places):
            u[place, :] = out[j * sizings : (j + 1) * sizings, :nodes]
            bu[place, :] = out[j * sizings : (j + 1) * sizings, nodes:]

    sorted_products(plan, 1, q, stacked, low, sizings, store_u)

    def second_row(r, carry):
        qu, uau, sums = carry
        for c in range(cols):
            here, image = operator(u, bu, r + 2, c + 2)
            b = r * cols + c
            own = pl.ds(pl.multiple_of(b * sizings, sizings), sizings)
            u_out[own, :] = here
            au_out[own, :] = image
            qu = qu + q[at(r + 2, c + 2), :] * here
            uau = uau + here * image
            total = jnp.sum(image, axis=1, keepdims=True)
            sums = sums + jnp.where(lanes == ids[r, c], total, 0.0)
        return qu, uau, sums

    qu, uau, sums_u = lax.fori_loop(0, rows, second_row, (blank, blank, zero_sums))

    lane = iota((sizings, 128), 1)
    dots = jnp.zeros((sizings, 128), F32)
    for j, one in enumerate((rz, zq, qu, uau)):
        dots = jnp.where(lane % 4 == j, jnp.sum(one, axis=1, keepdims=True), dots)
    dots = jnp.where(lane // 4 == iota((sizings, 128), 0), dots, 0.0)
    dots = jnp.sum(dots, axis=0, keepdims=True)
    whole = jnp.concatenate([pack(sums_q, count), pack(sums_u, count), dots], axis=0)

    def copy(d, carry):
        pay[d] = whole
        return carry

    lax.fori_loop(0, pay.shape[0], copy, 0)


def last_kernel(
    dims, mesh_dims,
    types, info,
    gathered, keys, inverses, cross, z, q, u, au, blocks, row_sums, strap,
    voltage, residual,
    level, solved,
):
    sizings, rows, cols, nodes, count = dims
    n_row, n_col = mesh_dims
    wide = cols + 4
    many = (rows + 4) * wide
    height = sizings * count // 128
    mesh_args = (mesh_dims, count, sizings)

    solved[0] = jnp.zeros((sizings, count), F32)
    solved[n_col + 1] = jnp.zeros((sizings, count), F32)
    with_q = jnp.zeros((sizings, count), F32)
    with_u = jnp.zeros((sizings, count), F32)
    crossed = jnp.zeros((sizings, count), F32)
    before = None
    for g in range(n_col):
        sums, one = coarse_solve(gathered, 0, height, *mesh_args, inverses, g)
        solved[g + 1] = one
        image = gathered[g, height : 2 * height, :]
        for i in range(1, n_row):
            image = image + gathered[i * n_col + g, height : 2 * height, :]
        with_q = with_q + sums * one
        with_u = with_u + unpack(image, count, sizings) * one
        if before is not None:
            crossed = crossed + one * jnp.dot(
                before, cross[g - 1], precision=HIGHEST, preferred_element_type=F32
            )
        before = one
    spread(solved, info[0], keys, level, count, sizings, nodes, many)

    dots = gathered[0, 2 * height : 2 * height + 1, :]
    for d in range(1, n_row * n_col):
        dots = dots + gathered[d, 2 * height : 2 * height + 1, :]
    lane = iota((sizings, 128), 1)
    dots = jnp.where(lane // 4 == iota((sizings, 128), 0), dots, 0.0)
    rz, zq, qu, uau = [
        jnp.sum(jnp.where(lane % 4 == j, dots, 0.0), axis=1, keepdims=True) for j in range(4)
    ]
    east_weight = jnp.sum(strap[1:2, :], axis=1, keepdims=True)
    total = functools.partial(jnp.sum, axis=1, keepdims=True)
    qw = qu + total(with_q)
    wp = uau + 2.0 * total(with_u) + total(with_q) - 2.0 * east_weight * total(crossed)
    step_1 = rz / zq
    fresh = step_1 * step_1 * qw - rz
    grown = 1.0 + fresh / rz
    step_2 = fresh / (grown * grown * zq - 2.0 * grown * step_1 * qw + step_1 * step_1 * wp)
    alpha = jnp.broadcast_to(step_1 + step_2 * grown, (sizings, nodes))
    gamma = jnp.broadcast_to(-step_2 * step_1, (sizings, nodes))

    north, east_strap = strap[0:1, :], strap[1:2, :]
    couple = 2.0 * north + 2.0 * east_strap

    def step(r, carry):
        for c in range(cols):
            b = r * cols + c
            own = pl.ds(pl.multiple_of(b * sizings, sizings), sizings)

            def value(dr, dc):
                e = (r + 2 + dr) * wide + c + 2 + dc
                return level[pl.ds(pl.multiple_of(e * sizings, sizings), sizings), :]

            here = value(0, 0)
            lift = (
                (row_sums[pl.ds(types[r, c], 1), :] + couple) * here
                - north * (value(-1, 0) + value(1, 0))
                - east_strap * (value(0, -1) + value(0, 1))
            )
            voltage[pl.ds(b, sizings, stride=rows * cols), :] = alpha * z[own, :] + gamma * (
                u[own, :] + here
            )
            residual[pl.ds(b, sizings, stride=rows * cols), :] = (
                blocks[own, :] - alpha * q[own, :] - gamma * (au[own, :] + lift)
            )
        return carry

    lax.fori_loop(0, rows, step, 0)


def ring_maps(rows, cols, count):
    tall, wide = rows + 4, cols + 4
    many = rows * cols
    length = -(-tall * wide // 128) * 128
    maps = np.zeros((8, length), np.int32)
    maps[0] = -1
    for er in range(tall):
        for ec in range(wide):
            e = er * wide + ec
            down = max(2 - er, er - (rows + 1), 0)
            over = max(2 - ec, ec - (cols + 1), 0)
            maps[1, e] = down + over <= 2
            maps[2, e] = down + over <= 1
            maps[3, e] = count * ((ec >= 2) + (ec >= cols + 2))
            if not down and not over:
                maps[0, e] = (er - 2) * cols + ec - 2
            elif not over:
                south = er > 1
                maps[0, e] = (1 + south) * many + (er - (rows + 2 if south else 0)) * cols + ec - 2
            elif down <= 1:
                right = ec > 1
                maps[0, e] = (3 + right) * many + (er - 1) * 2 + ec - (cols + 2 if right else 0)
    return maps


def call(kernel, in_specs, out_shape, scratch, cost, megabytes, **more):
    return pl.pallas_call(
        kernel,
        in_specs=in_specs,
        out_specs=jax.tree.map(lambda _: VMEM, out_shape),
        out_shape=out_shape,
        scratch_shapes=scratch,
        compiler_params=pltpu.CompilerParams(vmem_limit_bytes=megabytes * 1024 * 1024),
        cost_estimate=pl.CostEstimate(flops=cost, bytes_accessed=4_000_000, transcendentals=0),
        **more,
    )


def on_device(load_currents, block_library, strap_conductance, block_types, aggregate_map):
    sizings, rows, cols, nodes = load_currents.shape
    kinds = block_library.shape[0]
    n_row, n_col = lax.axis_size("row"), lax.axis_size("col")
    n_dev = n_row * n_col
    row, col = lax.axis_index("row"), lax.axis_index("col")
    count = rows * n_row // AGR * (cols // AGC)
    dims, mesh_dims = (sizings, rows, cols, nodes, count), (n_row, n_col)
    block_rows = rows * cols * sizings
    many = (rows + 4) * (cols + 4)
    height = sizings * count // 128
    shape = jax.ShapeDtypeStruct
    own = shape((block_rows, nodes), F32)

    edge = shape((sizings + 1, 2, cols, nodes), F32)
    top, bottom = call(
        functools.partial(edges_kernel, dims),
        [pl.BlockSpec(memory_space=pl.ANY), VMEM, VMEM],
        [edge, edge],
        [pltpu.SemaphoreType.DMA((2,))],
        1_000_000,
        8,
    )(load_currents, block_types, aggregate_map)
    forth = [(i, i + 1) for i in range(n_row - 1)]
    edge_rows = (sizings + 1) * 2 * cols
    above = lax.ppermute(bottom.reshape(edge_rows, nodes), "row", forth)
    below = lax.ppermute(top.reshape(edge_rows, nodes), "row", [(j, i) for i, j in forth])

    pay_rows = -(-(height + 2) // 8) * 8
    blocks, pay = call(
        functools.partial(sums_kernel, dims),
        [SMEM] + [VMEM] * 3,
        [own, shape((n_dev, pay_rows, 128), F32)],
        [],
        1_000_000,
        16,
    )(aggregate_map, block_types, aggregate_map, load_currents.reshape(-1, nodes))
    gathered = lax.all_to_all(pay, ("row", "col"), 0, 0)
    stacked, low, row_sums = call(
        weights_kernel,
        [VMEM, VMEM],
        [
            shape((kinds, 2 * nodes, 2 * nodes), BF16),
            shape((kinds, nodes, 2 * nodes), BF16),
            shape((kinds, nodes), F32),
        ],
        [],
        1_000_000_000,
        16,
    )(block_library, strap_conductance)
    side_rows = (rows + 2) * 2 * sizings
    side = shape((side_rows + 8, nodes), F32)
    to_west, to_east = call(
        functools.partial(sides_kernel, dims), [VMEM] * 5, [side, side], [], 1_000_000, 16
    )(block_types, aggregate_map, blocks, above, below)
    forth = [(i, i + 1) for i in range(n_col - 1)]
    west = lax.ppermute(to_east, "col", forth)
    east = lax.ppermute(to_west, "col", [(j, i) for i, j in forth])

    maps = ring_maps(rows, cols, count)
    longest = int(max(maps[1].sum(), maps[2].sum())) + (TILE - 1) * kinds + GROUP * TILE
    longest = -(-longest // 128) * 128
    edge_meta = pl.BlockSpec((8, 128), lambda i: (sizings * 2 * cols // 8, 0))
    side_meta = pl.BlockSpec((8, 128), lambda i: (side_rows // 8, 0))
    plan, keys = call(
        functools.partial(order_kernel, dims, kinds, longest),
        [VMEM] * 3 + [edge_meta, edge_meta, side_meta, side_meta],
        [shape((8, longest), jnp.int32), shape((1, maps.shape[1]), jnp.int32)],
        [],
        1_000_000,
        16,
        grid=(1,),
    )(jnp.asarray(maps), block_types, aggregate_map, above, below, west, east)
    info = jnp.stack(
        [
            col,
            (row > 0).astype(jnp.int32),
            (row < n_row - 1).astype(jnp.int32),
            (col > 0).astype(jnp.int32),
            (col < n_col - 1).astype(jnp.int32),
        ]
    )
    big = pltpu.VMEM(((many + 1) * sizings, nodes), F32)
    coarse = pltpu.VMEM((n_col + 2, sizings, count), F32)
    z, q, u, au, inverses, cross, pay = call(
        functools.partial(middle_kernel, dims, mesh_dims),
        [SMEM] * 3 + [VMEM] * 11,
        [own] * 4
        + [
            shape((count, n_col * count), F32),
            shape((n_col, count, count), F32),
            shape((n_dev, 2 * height + 1, 128), F32),
        ],
        [big] * 7 + [coarse],
        1_000_000_000,
        32 if count <= 64 else 56,
    )(
        plan, info, aggregate_map,
        gathered, keys, blocks, above, below, west, east, stacked, low, row_sums,
        strap_conductance,
    )
    gathered = lax.all_to_all(pay, ("row", "col"), 0, 0)
    out = shape((sizings * rows * cols, nodes), F32)
    voltage, residual = call(
        functools.partial(last_kernel, dims, mesh_dims),
        [SMEM] * 2 + [VMEM] * 11,
        [out, out],
        [big, coarse],
        1_000_000_000,
        16 if count <= 64 else 32,
    )(
        block_types, info,
        gathered, keys, inverses, cross, z, q, u, au, blocks, row_sums, strap_conductance,
    )
    return voltage.reshape(load_currents.shape), residual.reshape(load_currents.shape)


def solution(mesh):
    placed = (P(None, "row", "col", None), P(), P(), P("row", "col"), P("row", "col"))
    return jax.shard_map(
        on_device,
        mesh=mesh,
        in_specs=placed,
        out_specs=(P(None, "row", "col", None), P(None, "row", "col", None)),
        check_vma=False,
    )
```

```python
import functools

import jax
import jax.numpy as jnp
from jax import lax
from jax.experimental import pallas as pl
from jax.experimental.pallas import tpu as pltpu
from jax.sharding import PartitionSpec as P
import numpy as np

AGR = 4
AGC = 4
TILE = 8
GROUP = 2
PANEL = 8
F32 = jnp.float32
BF16 = jnp.bfloat16
HIGHEST = lax.Precision.HIGHEST
VMEM = pl.BlockSpec(memory_space=pltpu.VMEM)
SMEM = pl.BlockSpec(memory_space=pltpu.SMEM)


def iota(shape, dim):
    return lax.broadcasted_iota(jnp.int32, shape, dim)


def pack(values, count):
    if count < 128:
        fold = 128 // count
        height = values.shape[0] // fold
        return jnp.concatenate(
            [values[p * height : (p + 1) * height, :count] for p in range(fold)], axis=1
        )
    return jnp.concatenate([values[:, j : j + 128] for j in range(0, count, 128)], axis=0)


def unpack(rows, count, sizings):
    if count < 128:
        return jnp.concatenate(
            [rows[:, j : j + count] for j in range(0, 128, count)], axis=0
        )
    return jnp.concatenate(
        [rows[j : j + sizings] for j in range(0, rows.shape[0], sizings)], axis=1
    )


def split3(values):
    first = values.astype(BF16)
    rest = values - first.astype(F32)
    second = rest.astype(BF16)
    third = (rest - second.astype(F32)).astype(BF16)
    return first, second, third


def flat_row(table, many):
    rows, cols = table.shape
    repeat = (iota((cols, many), 1) % cols == iota((cols, many), 0)).astype(F32).astype(BF16)
    wide = jnp.dot(table.astype(F32).astype(BF16), repeat, preferred_element_type=F32)
    own = iota((rows, many), 1) // cols == iota((rows, many), 0)
    return jnp.sum(jnp.where(own, wide, 0.0), axis=0, keepdims=True)


def meta_rows(types, ids, many, height):
    rows = [flat_row(types[...], many), flat_row(ids[...], many) + 1.0]
    return jnp.concatenate(rows + [jnp.zeros((height - 2, many), F32)], axis=0)


def edges_kernel(dims, load, types, ids, top, bottom, sems):
    sizings, rows, cols, nodes, count = dims
    many = rows * cols
    copies = [
        pltpu.make_async_copy(
            load.at[:, pl.ds(first, 2)], out.at[pl.ds(0, sizings)], sems.at[i]
        )
        for i, (out, first) in enumerate(((top, 0), (bottom, rows - 2)))
    ]
    for copy in copies:
        copy.start()
    meta = meta_rows(types, ids, many, cols)
    blank = jnp.zeros((cols, nodes), F32)
    top[sizings, 0] = meta
    top[sizings, 1] = blank
    bottom[sizings, 0] = pltpu.roll(meta, 2 * cols, 1)
    bottom[sizings, 1] = blank
    for copy in copies:
        copy.wait()


def sums_kernel(dims, ids_smem, types, ids, load, blocks, pay):
    sizings, rows, cols, nodes, count = dims
    many = rows * cols
    lanes = iota((sizings, max(count, 128)), 1)

    def step(r, sums):
        for c in range(cols):
            b = r * cols + c
            block = load[pl.ds(b, sizings, stride=many), :]
            blocks[pl.ds(pl.multiple_of(b * sizings, sizings), sizings), :] = block
            total = jnp.sum(block, axis=1, keepdims=True)
            sums = sums + jnp.where(lanes == ids_smem[r, c], total, 0.0)
        return sums

    sums = lax.fori_loop(0, rows, step, jnp.zeros(lanes.shape, F32))
    height = sizings * count // 128
    meta = meta_rows(types, ids, many, pay.shape[1] - height)
    whole = jnp.concatenate([pack(sums, count), meta], axis=0)

    def copy(d, carry):
        pay[d] = whole
        return carry

    lax.fori_loop(0, pay.shape[0], copy, 0)


def weights_kernel(library, strap, stacked, low, row_sums):
    kinds, nodes, _ = library.shape
    eye = iota((nodes, nodes), 0) == iota((nodes, nodes), 1)
    couple_row = 2.0 * strap[0:1, :] + 2.0 * strap[1:2, :]
    couple_col = jnp.sum(jnp.where(eye, couple_row, 0.0), axis=1, keepdims=True)

    def step(t, carry):
        block = library[t]
        on = jnp.where(eye, block, 0.0)
        inv_row = 1.0 / (jnp.sum(on, axis=0, keepdims=True) + couple_row)
        inv_col = 1.0 / (jnp.sum(on, axis=1, keepdims=True) + couple_col)
        off = jnp.where(eye, 0.0, -block)
        once = inv_col * off * inv_row
        twice = jnp.dot(once, off, precision=HIGHEST, preferred_element_type=F32) * inv_row
        smoother = jnp.where(eye, inv_row, 0.0) + once + twice
        product = jnp.dot(smoother, block, precision=HIGHEST, preferred_element_type=F32)
        both = jnp.concatenate([smoother, product], axis=1)
        high = both.astype(BF16)
        stacked[t] = jnp.concatenate([high, high], axis=0)
        low[t] = (both - high.astype(F32)).astype(BF16)
        row_sums[pl.ds(t, 1), :] = jnp.sum(block, axis=0, keepdims=True)
        return carry

    lax.fori_loop(0, kinds, step, 0, unroll=True)


def sides_kernel(dims, types, ids, blocks, above, below, west, east):
    sizings, rows, cols, nodes, count = dims
    last = sizings * 2 * cols
    own = meta_rows(types, ids, rows * cols, 8)
    metas = [own, above[last : last + 8, :], below[last : last + 8, :]]
    metas = jnp.concatenate(metas, axis=1).astype(BF16)
    shape = (metas.shape[1], 128)
    slot, lane = iota(shape, 0), iota(shape, 1)
    for out, first in ((west, 0), (east, cols - 2)):
        for side in range(2):
            c = first + side
            for k in range(rows + 2):
                to = (k * 2 + side) * sizings
                if k == 0:
                    block = above[pl.ds(cols + c, sizings, stride=2 * cols), :]
                elif k == rows + 1:
                    block = below[pl.ds(c, sizings, stride=2 * cols), :]
                else:
                    at = ((k - 1) * cols + c) * sizings
                    block = blocks[at : at + sizings, :]
                out[to : to + sizings, :] = block
        k = lane // 2
        place = (k - 1) * cols
        place = jnp.where(k == 0, rows * cols + cols, place)
        place = jnp.where(k == rows + 1, 2 * rows * cols, place) + first + lane % 2
        pick = (slot == place) & (k < rows + 2)
        picked = jnp.dot(metas, pick.astype(F32).astype(BF16), preferred_element_type=F32)
        out[(rows + 2) * 2 * sizings :, :] = picked


def order_kernel(dims, kinds, lengths, maps, types, ids, above, below, west, east, plan, keys):
    sizings, rows, cols, nodes, count = dims
    many = rows * cols
    own = meta_rows(types, ids, many, 8)
    metas = jnp.concatenate([own, above[...], below[...], west[...], east[...]], axis=1)
    shape = (metas.shape[1], maps.shape[1])
    pick = (iota(shape, 0) == maps[0:1, :]).astype(F32).astype(BF16)
    near = jnp.dot(metas.astype(BF16), pick, preferred_element_type=F32)
    near_types, near_ids = near[0:1, :], near[1:2, :]
    keys[...] = jnp.where(
        near_ids > 0.0, near_ids - 1.0 + maps[3:4, :].astype(F32), -1.0
    ).astype(jnp.int32)

    length = maps.shape[1]
    total = (rows + 4) * (cols + 4)
    before = (iota((length, length), 0) < iota((length, length), 1)).astype(F32).astype(BF16)
    upto = (iota((kinds, kinds), 0) >= iota((kinds, kinds), 1)).astype(F32).astype(BF16)
    slot = iota((plan.shape[1], length), 0).astype(F32)
    slot_row = iota((kinds, plan.shape[1]), 1).astype(F32)
    side = iota((8, length), 0)
    index = jnp.where(side == 0, iota((8, length), 1), jnp.where(side == 1, 1, 0))
    index = index.astype(F32).astype(BF16)
    orders, tile_kinds, groups = [], [], []
    for which in (1, 2):
        needed = maps[which : which + 1, :] > 0
        hot = (iota((kinds, length), 0).astype(F32) == near_types) & needed
        hot = hot.astype(F32)
        rank = jnp.dot(hot.astype(BF16), before, preferred_element_type=F32)
        tiles = jnp.floor((jnp.sum(hot, axis=1, keepdims=True) + (TILE - 1)) * (1.0 / TILE))
        tiles = jnp.broadcast_to(tiles, (kinds, 128))
        ends = jnp.dot(upto, tiles.astype(BF16), preferred_element_type=F32)
        starts = (ends - tiles)[:, :1]
        place = jnp.sum(hot * (starts * TILE + rank + 1.0), axis=0, keepdims=True) - 1.0
        hit = (slot == place).astype(F32).astype(BF16)
        found = lax.dot_general(
            index, hit, (((1,), (1,)), ((), ())), preferred_element_type=F32
        )
        orders.append(found[0:1, :] + float(total) * (1.0 - found[1:2, :]))
        kind = jnp.sum(jnp.where(slot_row >= ends[:, :1], 1.0, 0.0), axis=0, keepdims=True)
        tile_kinds.append(jnp.minimum(kind, kinds - 1.0))
        last = jnp.floor((ends[kinds - 1 : kinds, :1] + (GROUP - 1)) * (1.0 / GROUP))
        groups.append(jnp.broadcast_to(last, (1, plan.shape[1])))
    rest = jnp.zeros((2, plan.shape[1]), F32)
    whole = jnp.concatenate(orders + tile_kinds + groups + [rest], axis=0)
    plan[...] = whole.astype(jnp.int32)


def sorted_products(plan, which, source, stacked, low, sizings, store):
    def step(it, carry):
        for one in range(GROUP):
            tile = it * GROUP + one
            kind = plan[2 + which, tile]
            places = [
                pl.ds(pl.multiple_of(plan[which, tile * TILE + j] * sizings, sizings), sizings)
                for j in range(TILE)
            ]
            field = jnp.concatenate([source[place, :] for place in places], axis=0)
            high = field.astype(BF16)
            rest = (field - high.astype(F32)).astype(BF16)
            out = jnp.dot(
                jnp.concatenate([high, rest], axis=1), stacked[kind], preferred_element_type=F32
            ) + jnp.dot(high, low[kind], preferred_element_type=F32)
            store(kind, places, out)
        return carry

    lax.fori_loop(0, plan[4 + which, 0], step, 0)


def neighbour_ids(ids, cols):
    height, many = ids.shape
    lane, row = iota(ids.shape, 1), iota(ids.shape, 0)
    down = pltpu.roll(ids, many - cols, 1)
    south = jnp.where(lane < many - cols, down, pltpu.roll(down, height - 1, 0))
    south = jnp.where((lane >= many - cols) & (row == height - 1), -1.0, south)
    up = pltpu.roll(ids, cols, 1)
    north = jnp.where(lane >= cols, up, pltpu.roll(up, 1, 0))
    north = jnp.where((lane < cols) & (row == 0), -1.0, north)
    east = jnp.where(lane % cols == cols - 1, -1.0, pltpu.roll(ids, many - 1, 1))
    west = jnp.where(lane % cols == 0, -1.0, pltpu.roll(ids, 1, 1))
    return south, north, east, west


def invert_unrolled(ref, count):
    width = ref.shape[1]
    fold = 128 // count
    lane = iota((8, width), 1) % count
    row = iota((8, width), 0)
    tile_lane = iota((8, 128), 1)
    many = count // 8
    tiles = [ref[i * 8 : (i + 1) * 8, :] for i in range(many)]

    def column(tile, k):
        parts = []
        for base in range(0, width, 128):
            part = jnp.broadcast_to(tile[:, base + k : base + k + 1], (8, 128))
            for j in range(1, fold):
                at = base + j * count + k
                part = jnp.where(tile_lane >= j * count, tile[:, at : at + 1], part)
            parts.append(part)
        return jnp.concatenate(parts, axis=1)

    for first in range(0, count, PANEL):
        columns = [[column(t, first + j) for t in tiles] for j in range(PANEL)]
        for j in range(PANEL):
            k = first + j
            at, within = k // 8, k % 8
            here = columns[j]
            inverse = 1.0 / here[at][within : within + 1, :]
            scaled = jnp.where(
                lane[:1] == k, inverse, tiles[at][within : within + 1, :] * inverse
            )
            pivot = row == within
            for i in range(many):
                new = jnp.where(lane == k, 0.0, tiles[i]) - here[i] * scaled
                tiles[i] = jnp.where(pivot, scaled, new) if i == at else new
            for later in range(j + 1, PANEL):
                other = columns[later]
                factor = other[at][within : within + 1, :] * inverse
                for i in range(many):
                    new = other[i] - here[i] * factor
                    other[i] = jnp.where(pivot, factor, new) if i == at else new
    for i in range(many):
        ref[i * 8 : (i + 1) * 8, :] = tiles[i]


def invert_looped(ref, count):
    def step(k, carry):
        for base in range(0, ref.shape[1], count):
            here = slice(base, base + count)
            lane = iota((1, count), 1)
            row = iota((count, 1), 0)
            pivot_row = ref[pl.ds(k, 1), here]
            part = ref[:, here]
            column = jnp.sum(jnp.where(lane == k, part, 0.0), axis=1, keepdims=True)
            inverse = 1.0 / jnp.sum(jnp.where(lane == k, pivot_row, 0.0), axis=1, keepdims=True)
            scaled = jnp.where(lane == k, 1.0, pivot_row) * inverse
            column = jnp.where(row == k, -1.0, column)
            ref[:, here] = jnp.where((lane == k) | (row == k), 0.0, part) - column * scaled
        return carry

    lax.fori_loop(0, count, step, 0)


def coarse_matrices(dims, mesh_dims, gathered, row_sums, strap, inverses, cross):
    sizings, rows, cols, nodes, count = dims
    n_row, n_col = mesh_dims
    many = rows * cols
    height = sizings * count // 128
    kinds = row_sums.shape[0]
    north_weight = jnp.sum(strap[0:1, :], axis=1, keepdims=True)
    east_weight = jnp.sum(strap[1:2, :], axis=1, keepdims=True)
    names = iota((count, many), 0).astype(F32).astype(BF16)
    kind_names = iota((16, many), 0).astype(F32).astype(BF16)
    lane = iota((n_row, many), 1)
    eye = iota((count, count), 0) == iota((count, count), 1)
    contract = (((1,), (1,)), ((), ()))
    spot = iota((kinds, 16), 0) == iota((kinds, 16), 1)
    centre = jnp.sum(row_sums[...], axis=1, keepdims=True) + 2.0 * north_weight
    centre = centre + 2.0 * east_weight
    centre = jnp.sum(jnp.where(spot, centre, 0.0), axis=0, keepdims=True)

    def rows_of(g, at):
        return jnp.concatenate(
            [gathered[i * n_col + g, at : at + 1, :] for i in range(n_row)], axis=0
        )

    def hot(values, labels):
        rows_bf = values.astype(BF16)
        one, zero = jnp.ones(labels.shape, BF16), jnp.zeros(labels.shape, BF16)
        return [
            jnp.where(labels == rows_bf[i : i + 1, :], one, zero) for i in range(n_row)
        ]

    all_ids = [rows_of(g, height + 1) - 1.0 for g in range(n_col)]
    for g in range(n_col):
        ids = all_ids[g]
        beyond = all_ids[min(g + 1, n_col - 1)]
        beyond = jnp.where(lane % cols == cols - 1, pltpu.roll(beyond, cols - 1, 1), -1.0)
        south, north, east, west = [hot(v, names) for v in neighbour_ids(ids, cols)]
        own, over = hot(ids, names), hot(beyond, names)
        types = hot(rows_of(g, height), kind_names)
        right = jnp.concatenate(
            [
                jnp.concatenate([south[i] + north[i], east[i] + west[i], over[i], types[i]], axis=0)
                for i in range(n_row)
            ],
            axis=1,
        )
        pairs = lax.dot_general(
            jnp.concatenate(own, axis=1), right, contract, preferred_element_type=F32
        )
        diagonal = jnp.sum(pairs[:, 3 * count :] * centre, axis=1, keepdims=True)
        inverses[:, g * count : (g + 1) * count] = jnp.where(eye, diagonal, 0.0) - (
            north_weight * pairs[:, :count] + east_weight * pairs[:, count : 2 * count]
        )
        cross[g] = pairs[:, 2 * count : 3 * count]


def coarse_solve(gathered, first, height, mesh_dims, count, sizings, inverses, g):
    n_row, n_col = mesh_dims
    total = gathered[g, first : first + height, :]
    for i in range(1, n_row):
        total = total + gathered[i * n_col + g, first : first + height, :]
    sums = unpack(total, count, sizings)
    solved = jnp.dot(
        sums, inverses[:, g * count : (g + 1) * count], precision=HIGHEST,
        preferred_element_type=F32,
    )
    return sums, solved


def spread(solved, col, keys, out, count, sizings, nodes, many):
    three = jnp.concatenate([solved[col], solved[col + 1], solved[col + 2]], axis=1)
    hot = (iota((3 * count, keys.shape[1]), 0) == keys[...]).astype(F32).astype(BF16)
    parts = jnp.concatenate(split3(three), axis=0)
    values = jnp.dot(parts, hot, preferred_element_type=F32)
    values = (
        values[2 * sizings : 3 * sizings] + values[sizings : 2 * sizings] + values[:sizings]
    )
    for e in range(many):
        out[e * sizings : (e + 1) * sizings, :] = jnp.broadcast_to(
            values[:, e : e + 1], (sizings, nodes)
        )


def middle_kernel(
    dims, mesh_dims,
    plan, info, ids,
    gathered, keys, blocks, above, below, west, east, stacked, low, row_sums, strap,
    z_out, q_out, u_out, au_out, inverses, cross, pay,
    field, level, z, bz, q, u, bu, solved,
):
    sizings, rows, cols, nodes, count = dims
    n_row, n_col = mesh_dims
    wide = cols + 4
    many = (rows + 4) * wide
    height = sizings * count // 128

    def at(er, ec):
        return pl.ds(pl.multiple_of((er * wide + ec) * sizings, sizings), sizings)

    span = cols * sizings
    for r in range(rows):
        to = ((r + 2) * wide + 2) * sizings
        field[to : to + span, :] = blocks[r * span : (r + 1) * span, :]
    for r in range(2):
        for c in range(cols):
            from_edge = pl.ds(r * cols + c, sizings, stride=2 * cols)
            to = (r * wide + 2 + c) * sizings
            field[to : to + sizings, :] = above[from_edge, :]
            to = ((rows + 2 + r) * wide + 2 + c) * sizings
            field[to : to + sizings, :] = below[from_edge, :]
    for k in range(rows + 2):
        pair = 2 * sizings
        to = (k + 1) * wide * sizings
        field[to : to + pair, :] = west[k * pair : (k + 1) * pair, :]
        to = to + (cols + 2) * sizings
        field[to : to + pair, :] = east[k * pair : (k + 1) * pair, :]
    field[many * sizings :, :] = jnp.zeros((sizings, nodes), F32)
    level[many * sizings :, :] = jnp.zeros((sizings, nodes), F32)
    q[many * sizings :, :] = jnp.zeros((sizings, nodes), F32)

    coarse_matrices(dims, mesh_dims, gathered, row_sums, strap, inverses, cross)
    if count <= 64:
        invert_unrolled(inverses, count)
    else:
        invert_looped(inverses, count)
    solved[0] = jnp.zeros((sizings, count), F32)
    solved[n_col + 1] = jnp.zeros((sizings, count), F32)
    for g in range(n_col):
        _, solved[g + 1] = coarse_solve(
            gathered, 0, height, mesh_dims, count, sizings, inverses, g
        )
    spread(solved, info[0], keys, level, count, sizings, nodes, many)

    def store_z(kind, places, out):
        sums = row_sums[pl.ds(kind, 1), :]
        for j, place in enumerate(places):
            here = level[place, :]
            z[place, :] = out[j * sizings : (j + 1) * sizings, :nodes] + here
            bz[place, :] = out[j * sizings : (j + 1) * sizings, nodes:] + sums * here

    sorted_products(plan, 0, field, stacked, low, sizings, store_z)

    north, east_strap = strap[0:1, :], strap[1:2, :]
    couple = 2.0 * north + 2.0 * east_strap

    def operator(v, bv, er, ec):
        here = v[at(er, ec), :]
        image = (
            bv[at(er, ec), :]
            + couple * here
            - north * (v[at(er - 1, ec), :] + v[at(er + 1, ec), :])
            - east_strap * (v[at(er, ec - 1), :] + v[at(er, ec + 1), :])
        )
        return here, image

    for er, flag in ((1, info[1]), (rows + 2, info[2])):
        inside = flag.astype(F32)

        def across(ec, carry):
            q[at(er, ec), :] = operator(z, bz, er, ec)[1] * inside
            return carry

        lax.fori_loop(2, cols + 2, across, 0)
    for ec, flag in ((1, info[3]), (cols + 2, info[4])):
        inside = flag.astype(F32)

        def along(er, carry):
            q[at(er, ec), :] = operator(z, bz, er, ec)[1] * inside
            return carry

        lax.fori_loop(2, rows + 2, along, 0)

    lanes = iota((sizings, max(count, 128)), 1)
    blank = jnp.zeros((sizings, nodes), F32)
    zero_sums = jnp.zeros(lanes.shape, F32)

    def first_row(r, carry):
        rz, zq, sums = carry
        for c in range(cols):
            here, image = operator(z, bz, r + 2, c + 2)
            q[at(r + 2, c + 2), :] = image
            b = r * cols + c
            own = pl.ds(pl.multiple_of(b * sizings, sizings), sizings)
            z_out[own, :] = here
            q_out[own, :] = image
            rz = rz + blocks[own, :] * here
            zq = zq + here * image
            total = jnp.sum(image, axis=1, keepdims=True)
            sums = sums + jnp.where(lanes == ids[r, c], total, 0.0)
        return rz, zq, sums

    rz, zq, sums_q = lax.fori_loop(0, rows, first_row, (blank, blank, zero_sums))

    def store_u(kind, places, out):
        for j, place in enumerate(places):
            u[place, :] = out[j * sizings : (j + 1) * sizings, :nodes]
            bu[place, :] = out[j * sizings : (j + 1) * sizings, nodes:]

    sorted_products(plan, 1, q, stacked, low, sizings, store_u)

    def second_row(r, carry):
        qu, uau, sums = carry
        for c in range(cols):
            here, image = operator(u, bu, r + 2, c + 2)
            b = r * cols + c
            own = pl.ds(pl.multiple_of(b * sizings, sizings), sizings)
            u_out[own, :] = here
            au_out[own, :] = image
            qu = qu + q[at(r + 2, c + 2), :] * here
            uau = uau + here * image
            total = jnp.sum(image, axis=1, keepdims=True)
            sums = sums + jnp.where(lanes == ids[r, c], total, 0.0)
        return qu, uau, sums

    qu, uau, sums_u = lax.fori_loop(0, rows, second_row, (blank, blank, zero_sums))

    lane = iota((sizings, 128), 1)
    dots = jnp.zeros((sizings, 128), F32)
    for j, one in enumerate((rz, zq, qu, uau)):
        dots = jnp.where(lane % 4 == j, jnp.sum(one, axis=1, keepdims=True), dots)
    dots = jnp.where(lane // 4 == iota((sizings, 128), 0), dots, 0.0)
    dots = jnp.sum(dots, axis=0, keepdims=True)
    whole = jnp.concatenate([pack(sums_q, count), pack(sums_u, count), dots], axis=0)

    def copy(d, carry):
        pay[d] = whole
        return carry

    lax.fori_loop(0, pay.shape[0], copy, 0)


def last_kernel(
    dims, mesh_dims,
    types, info,
    gathered, keys, inverses, cross, z, q, u, au, blocks, row_sums, strap,
    voltage, residual,
    level, solved,
):
    sizings, rows, cols, nodes, count = dims
    n_row, n_col = mesh_dims
    wide = cols + 4
    many = (rows + 4) * wide
    height = sizings * count // 128
    mesh_args = (mesh_dims, count, sizings)

    solved[0] = jnp.zeros((sizings, count), F32)
    solved[n_col + 1] = jnp.zeros((sizings, count), F32)
    with_q = jnp.zeros((sizings, count), F32)
    with_u = jnp.zeros((sizings, count), F32)
    crossed = jnp.zeros((sizings, count), F32)
    before = None
    for g in range(n_col):
        sums, one = coarse_solve(gathered, 0, height, *mesh_args, inverses, g)
        solved[g + 1] = one
        image = gathered[g, height : 2 * height, :]
        for i in range(1, n_row):
            image = image + gathered[i * n_col + g, height : 2 * height, :]
        with_q = with_q + sums * one
        with_u = with_u + unpack(image, count, sizings) * one
        if before is not None:
            crossed = crossed + one * jnp.dot(
                before, cross[g - 1], precision=HIGHEST, preferred_element_type=F32
            )
        before = one
    spread(solved, info[0], keys, level, count, sizings, nodes, many)

    dots = gathered[0, 2 * height : 2 * height + 1, :]
    for d in range(1, n_row * n_col):
        dots = dots + gathered[d, 2 * height : 2 * height + 1, :]
    lane = iota((sizings, 128), 1)
    dots = jnp.where(lane // 4 == iota((sizings, 128), 0), dots, 0.0)
    rz, zq, qu, uau = [
        jnp.sum(jnp.where(lane % 4 == j, dots, 0.0), axis=1, keepdims=True) for j in range(4)
    ]
    east_weight = jnp.sum(strap[1:2, :], axis=1, keepdims=True)
    total = functools.partial(jnp.sum, axis=1, keepdims=True)
    qw = qu + total(with_q)
    wp = uau + 2.0 * total(with_u) + total(with_q) - 2.0 * east_weight * total(crossed)
    step_1 = rz / zq
    fresh = step_1 * step_1 * qw - rz
    grown = 1.0 + fresh / rz
    step_2 = fresh / (grown * grown * zq - 2.0 * grown * step_1 * qw + step_1 * step_1 * wp)
    alpha = jnp.broadcast_to(step_1 + step_2 * grown, (sizings, nodes))
    gamma = jnp.broadcast_to(-step_2 * step_1, (sizings, nodes))

    north, east_strap = strap[0:1, :], strap[1:2, :]
    couple = 2.0 * north + 2.0 * east_strap

    def step(r, carry):
        for c in range(cols):
            b = r * cols + c
            own = pl.ds(pl.multiple_of(b * sizings, sizings), sizings)

            def value(dr, dc):
                e = (r + 2 + dr) * wide + c + 2 + dc
                return level[pl.ds(pl.multiple_of(e * sizings, sizings), sizings), :]

            here = value(0, 0)
            lift = (
                (row_sums[pl.ds(types[r, c], 1), :] + couple) * here
                - north * (value(-1, 0) + value(1, 0))
                - east_strap * (value(0, -1) + value(0, 1))
            )
            voltage[pl.ds(b, sizings, stride=rows * cols), :] = alpha * z[own, :] + gamma * (
                u[own, :] + here
            )
            residual[pl.ds(b, sizings, stride=rows * cols), :] = (
                blocks[own, :] - alpha * q[own, :] - gamma * (au[own, :] + lift)
            )
        return carry

    lax.fori_loop(0, rows, step, 0)


def ring_maps(rows, cols, count):
    tall, wide = rows + 4, cols + 4
    many = rows * cols
    length = -(-tall * wide // 128) * 128
    maps = np.zeros((8, length), np.int32)
    maps[0] = -1
    for er in range(tall):
        for ec in range(wide):
            e = er * wide + ec
            down = max(2 - er, er - (rows + 1), 0)
            over = max(2 - ec, ec - (cols + 1), 0)
            maps[1, e] = down + over <= 2
            maps[2, e] = down + over <= 1
            maps[3, e] = count * ((ec >= 2) + (ec >= cols + 2))
            if not down and not over:
                maps[0, e] = (er - 2) * cols + ec - 2
            elif not over:
                south = er > 1
                maps[0, e] = (1 + south) * many + (er - (rows + 2 if south else 0)) * cols + ec - 2
            elif down <= 1:
                right = ec > 1
                maps[0, e] = (3 + right) * many + (er - 1) * 2 + ec - (cols + 2 if right else 0)
    return maps


def call(kernel, in_specs, out_shape, scratch, cost, megabytes, **more):
    return pl.pallas_call(
        kernel,
        in_specs=in_specs,
        out_specs=jax.tree.map(lambda _: VMEM, out_shape),
        out_shape=out_shape,
        scratch_shapes=scratch,
        compiler_params=pltpu.CompilerParams(vmem_limit_bytes=megabytes * 1024 * 1024),
        cost_estimate=pl.CostEstimate(flops=cost, bytes_accessed=4_000_000, transcendentals=0),
        **more,
    )


def on_device(load_currents, block_library, strap_conductance, block_types, aggregate_map):
    sizings, rows, cols, nodes = load_currents.shape
    kinds = block_library.shape[0]
    n_row, n_col = lax.axis_size("row"), lax.axis_size("col")
    n_dev = n_row * n_col
    row, col = lax.axis_index("row"), lax.axis_index("col")
    count = rows * n_row // AGR * (cols // AGC)
    dims, mesh_dims = (sizings, rows, cols, nodes, count), (n_row, n_col)
    block_rows = rows * cols * sizings
    many = (rows + 4) * (cols + 4)
    height = sizings * count // 128
    shape = jax.ShapeDtypeStruct
    own = shape((block_rows, nodes), F32)

    edge = shape((sizings + 1, 2, cols, nodes), F32)
    top, bottom = call(
        functools.partial(edges_kernel, dims),
        [pl.BlockSpec(memory_space=pl.ANY), VMEM, VMEM],
        [edge, edge],
        [pltpu.SemaphoreType.DMA((2,))],
        1_000_000,
        8,
    )(load_currents, block_types, aggregate_map)
    forth = [(i, i + 1) for i in range(n_row - 1)]
    edge_rows = (sizings + 1) * 2 * cols
    above = lax.ppermute(bottom.reshape(edge_rows, nodes), "row", forth)
    below = lax.ppermute(top.reshape(edge_rows, nodes), "row", [(j, i) for i, j in forth])

    pay_rows = -(-(height + 2) // 8) * 8
    blocks, pay = call(
        functools.partial(sums_kernel, dims),
        [SMEM] + [VMEM] * 3,
        [own, shape((n_dev, pay_rows, 128), F32)],
        [],
        1_000_000,
        16,
    )(aggregate_map, block_types, aggregate_map, load_currents.reshape(-1, nodes))
    gathered = lax.all_to_all(pay, ("row", "col"), 0, 0)
    stacked, low, row_sums = call(
        weights_kernel,
        [VMEM, VMEM],
        [
            shape((kinds, 2 * nodes, 2 * nodes), BF16),
            shape((kinds, nodes, 2 * nodes), BF16),
            shape((kinds, nodes), F32),
        ],
        [],
        40_000_000_000,
        16,
    )(block_library, strap_conductance)
    side_rows = (rows + 2) * 2 * sizings
    side = shape((side_rows + 8, nodes), F32)
    to_west, to_east = call(
        functools.partial(sides_kernel, dims), [VMEM] * 5, [side, side], [], 1_000_000, 16
    )(block_types, aggregate_map, blocks, above, below)
    forth = [(i, i + 1) for i in range(n_col - 1)]
    west = lax.ppermute(to_east, "col", forth)
    east = lax.ppermute(to_west, "col", [(j, i) for i, j in forth])

    maps = ring_maps(rows, cols, count)
    longest = int(max(maps[1].sum(), maps[2].sum())) + (TILE - 1) * kinds + GROUP * TILE
    longest = -(-longest // 128) * 128
    edge_meta = pl.BlockSpec((8, 128), lambda i: (sizings * 2 * cols // 8, 0))
    side_meta = pl.BlockSpec((8, 128), lambda i: (side_rows // 8, 0))
    plan, keys = call(
        functools.partial(order_kernel, dims, kinds, longest),
        [VMEM] * 3 + [edge_meta, edge_meta, side_meta, side_meta],
        [shape((8, longest), jnp.int32), shape((1, maps.shape[1]), jnp.int32)],
        [],
        1_000_000,
        16,
        grid=(1,),
    )(jnp.asarray(maps), block_types, aggregate_map, above, below, west, east)
    info = jnp.stack(
        [
            col,
            (row > 0).astype(jnp.int32),
            (row < n_row - 1).astype(jnp.int32),
            (col > 0).astype(jnp.int32),
            (col < n_col - 1).astype(jnp.int32),
        ]
    )
    big = pltpu.VMEM(((many + 1) * sizings, nodes), F32)
    coarse = pltpu.VMEM((n_col + 2, sizings, count), F32)
    z, q, u, au, inverses, cross, pay = call(
        functools.partial(middle_kernel, dims, mesh_dims),
        [SMEM] * 3 + [VMEM] * 11,
        [own] * 4
        + [
            shape((count, n_col * count), F32),
            shape((n_col, count, count), F32),
            shape((n_dev, 2 * height + 1, 128), F32),
        ],
        [big] * 7 + [coarse],
        1_000_000_000,
        32 if count <= 64 else 56,
    )(
        plan, info, aggregate_map,
        gathered, keys, blocks, above, below, west, east, stacked, low, row_sums,
        strap_conductance,
    )
    gathered = lax.all_to_all(pay, ("row", "col"), 0, 0)
    out = shape((sizings * rows * cols, nodes), F32)
    voltage, residual = call(
        functools.partial(last_kernel, dims, mesh_dims),
        [SMEM] * 2 + [VMEM] * 11,
        [out, out],
        [big, coarse],
        1_000_000_000,
        16 if count <= 64 else 32,
    )(
        block_types, info,
        gathered, keys, inverses, cross, z, q, u, au, blocks, row_sums, strap_conductance,
    )
    return voltage.reshape(load_currents.shape), residual.reshape(load_currents.shape)


def solution(mesh):
    placed = (P(None, "row", "col", None), P(), P(), P("row", "col"), P("row", "col"))
    return jax.shard_map(
        on_device,
        mesh=mesh,
        in_specs=placed,
        out_specs=(P(None, "row", "col", None), P(None, "row", "col", None)),
        check_vma=False,
    )
```

```python
import functools

import jax
import jax.numpy as jnp
from jax import lax
from jax.experimental import pallas as pl
from jax.experimental.pallas import tpu as pltpu
from jax.sharding import PartitionSpec as P
import numpy as np

AGR = 4
AGC = 4
TILE = 8
GROUP = 4
PANEL = 8
F32 = jnp.float32
BF16 = jnp.bfloat16
HIGHEST = lax.Precision.HIGHEST
VMEM = pl.BlockSpec(memory_space=pltpu.VMEM)
SMEM = pl.BlockSpec(memory_space=pltpu.SMEM)
HBM = pl.BlockSpec(memory_space=pltpu.HBM)


def iota(shape, dim):
    return lax.broadcasted_iota(jnp.int32, shape, dim)


def pack(values, count):
    if count < 128:
        fold = 128 // count
        height = values.shape[0] // fold
        return jnp.concatenate(
            [values[p * height : (p + 1) * height, :count] for p in range(fold)], axis=1
        )
    return jnp.concatenate([values[:, j : j + 128] for j in range(0, count, 128)], axis=0)


def unpack(rows, count, sizings):
    if count < 128:
        return jnp.concatenate(
            [rows[:, j : j + count] for j in range(0, 128, count)], axis=0
        )
    return jnp.concatenate(
        [rows[j : j + sizings] for j in range(0, rows.shape[0], sizings)], axis=1
    )


def split3(values):
    first = values.astype(BF16)
    rest = values - first.astype(F32)
    second = rest.astype(BF16)
    third = (rest - second.astype(F32)).astype(BF16)
    return first, second, third


def flat_row(table, many):
    rows, cols = table.shape
    repeat = (iota((cols, many), 1) % cols == iota((cols, many), 0)).astype(F32).astype(BF16)
    wide = jnp.dot(table.astype(F32).astype(BF16), repeat, preferred_element_type=F32)
    own = iota((rows, many), 1) // cols == iota((rows, many), 0)
    return jnp.sum(jnp.where(own, wide, 0.0), axis=0, keepdims=True)


def meta_rows(types, ids, many, height):
    rows = [flat_row(types[...], many), flat_row(ids[...], many) + 1.0]
    spare = [jnp.zeros((height - 2, many), F32)] if height > 2 else []
    return jnp.concatenate(rows + spare, axis=0)


def either(odd, if_even, if_odd):
    return jnp.where(odd == 1, if_odd, if_even)


def edges_kernel(
    dims, info, load, types_hbm, ids_hbm, first, second, types, ids, sems
):
    sizings, rows, cols, nodes, count = dims
    many = rows * cols
    odd = info[5]
    copies = [
        pltpu.make_async_copy(types_hbm, types, sems.at[0]),
        pltpu.make_async_copy(ids_hbm, ids, sems.at[1]),
        pltpu.make_async_copy(
            load.at[:, pl.ds(either(odd, rows - 2, 0), 2)],
            first.at[pl.ds(0, sizings)],
            sems.at[2],
        ),
        pltpu.make_async_copy(
            load.at[:, pl.ds(either(odd, 0, rows - 2), 2)],
            second.at[pl.ds(0, sizings)],
            sems.at[3],
        ),
    ]
    for copy in copies:
        copy.start()
    copies[0].wait()
    copies[1].wait()
    meta = meta_rows(types, ids, many, cols)
    blank = jnp.zeros((cols, nodes), F32)
    top, bottom = meta, pltpu.roll(meta, 2 * cols, 1)
    first[sizings, 0] = either(odd, bottom, top)
    first[sizings, 1] = blank
    second[sizings, 0] = either(odd, top, bottom)
    second[sizings, 1] = blank
    copies[2].wait()
    copies[3].wait()


def sums_kernel(dims, ids_smem, types, ids, load, pay):
    sizings, rows, cols, nodes, count = dims
    many = rows * cols
    width = max(count, 128)
    lane, side = iota((cols, width), 1), iota((cols, width), 0)
    hots = []
    for r in range(rows):
        names = jnp.zeros((cols, width), jnp.int32)
        for c in range(cols):
            names = jnp.where(side == c, ids_smem[r, c], names)
        hots.append((names == lane).astype(F32))
    sums = []
    for s in range(sizings):
        total = jnp.zeros((cols, width), F32)
        for r in range(rows):
            at = s * many + r * cols
            total = total + hots[r] * jnp.sum(load[at : at + cols, :], axis=1, keepdims=True)
        sums.append(jnp.sum(total, axis=0, keepdims=True))
    height = sizings * count // 128
    meta = meta_rows(types, ids, many, pay.shape[1] - height)
    whole = jnp.concatenate([pack(jnp.concatenate(sums, axis=0), count), meta], axis=0)
    send_all(pay, whole)


def send_all(pay, whole):
    def copy(d, carry):
        pay[d] = whole.reshape(pay.shape[1:])
        return carry

    lax.fori_loop(0, pay.shape[0], copy, 0)


def blocks_kernel(dims, load, blocks):
    sizings, rows, cols, nodes, count = dims
    many = rows * cols

    def step(r, carry):
        for c in range(cols):
            b = r * cols + c
            at = pl.ds(pl.multiple_of(b * sizings, sizings), sizings)
            blocks[at, :] = load[pl.ds(b, sizings, stride=many), :]
        return carry

    lax.fori_loop(0, rows, step, 0)


def weights_kernel(library, strap, stacked, low, row_sums):
    kinds, nodes, _ = library.shape
    eye = iota((nodes, nodes), 0) == iota((nodes, nodes), 1)
    couple_row = 2.0 * strap[0:1, :] + 2.0 * strap[1:2, :]
    couple_col = jnp.sum(jnp.where(eye, couple_row, 0.0), axis=1, keepdims=True)

    def step(t, carry):
        block = library[t]
        on = jnp.where(eye, block, 0.0)
        inv_row = 1.0 / (jnp.sum(on, axis=0, keepdims=True) + couple_row)
        inv_col = 1.0 / (jnp.sum(on, axis=1, keepdims=True) + couple_col)
        off = jnp.where(eye, 0.0, -block)
        once = inv_col * off * inv_row
        twice = jnp.dot(once, off, precision=HIGHEST, preferred_element_type=F32) * inv_row
        smoother = jnp.where(eye, inv_row, 0.0) + once + twice
        product = jnp.dot(smoother, block, precision=HIGHEST, preferred_element_type=F32)
        both = jnp.concatenate([smoother, product], axis=1)
        high = both.astype(BF16)
        stacked[t] = jnp.concatenate([high, high], axis=0)
        low[t] = (both - high.astype(F32)).astype(BF16)
        row_sums[pl.ds(t, 1), :] = jnp.sum(block, axis=0, keepdims=True)
        return carry

    lax.fori_loop(0, kinds, step, 0, unroll=True)


def sides_kernel(
    dims, info, types, ids, blocks, row_first, row_second, row_sums, first, second
):
    sizings, rows, cols, nodes, count = dims
    last = sizings * 2 * cols
    row_odd, odd = info[5], info[6]
    own = meta_rows(types, ids, rows * cols, 8)
    one, two = row_first[last : last + 8, :], row_second[last : last + 8, :]
    metas = [own, either(row_odd, two, one), either(row_odd, one, two)]
    metas = jnp.concatenate(metas, axis=1).astype(BF16)
    shape = (metas.shape[1], 128)
    slot, lane = iota(shape, 0), iota(shape, 1)
    for out, begin in ((first, either(odd, cols - 2, 0)), (second, either(odd, 0, cols - 2))):
        for side in range(2):
            c = begin + side
            above = pl.ds(cols + c, sizings, stride=2 * cols)
            below = pl.ds(c, sizings, stride=2 * cols)
            to = side * sizings
            out[to : to + sizings, :] = either(row_odd, row_second[above, :], row_first[above, :])
            to = ((rows + 1) * 2 + side) * sizings
            out[to : to + sizings, :] = either(row_odd, row_first[below, :], row_second[below, :])
            for r in range(rows):
                at = pl.multiple_of((r * cols + c) * sizings, sizings)
                to = ((r + 1) * 2 + side) * sizings
                out[to : to + sizings, :] = blocks[pl.ds(at, sizings), :]
        k = lane // 2
        place = (k - 1) * cols
        place = jnp.where(k == 0, rows * cols + cols, place)
        place = jnp.where(k == rows + 1, 2 * rows * cols, place) + begin + lane % 2
        pick = (slot == place) & (k < rows + 2)
        picked = jnp.dot(metas, pick.astype(F32).astype(BF16), preferred_element_type=F32)
        out[(rows + 2) * 2 * sizings :, :] = picked


def order_kernel(
    dims, kinds, info, maps, types, ids, row_first, row_second, col_first, col_second, solved, plan, keys
):
    sizings, rows, cols, nodes, count = dims
    many = rows * cols
    own = meta_rows(types, ids, many, 8)
    metas = [own]
    for odd, one, two in ((info[5], row_first, row_second), (info[6], col_first, col_second)):
        metas += [either(odd, two[...], one[...]), either(odd, one[...], two[...])]
    metas = jnp.concatenate(metas, axis=1)
    shape = (metas.shape[1], maps.shape[1])
    pick = (iota(shape, 0) == maps[0:1, :]).astype(F32).astype(BF16)
    near = jnp.dot(metas.astype(BF16), pick, preferred_element_type=F32)
    near_types, near_ids = near[0:1, :], near[1:2, :]
    keys[...] = jnp.where(
        near_ids > 0.0, near_ids - 1.0 + maps[3:4, :].astype(F32), -1.0
    ).astype(jnp.int32)

    length = maps.shape[1]
    total = (rows + 4) * (cols + 4)
    before = (iota((length, length), 0) < iota((length, length), 1)).astype(F32).astype(BF16)
    upto = (iota((kinds, kinds), 0) >= iota((kinds, kinds), 1)).astype(F32).astype(BF16)
    slot = iota((plan.shape[1], length), 0).astype(F32)
    slot_row = iota((kinds, plan.shape[1]), 1).astype(F32)
    side = iota((8, length), 0)
    index = jnp.where(side == 0, iota((8, length), 1), jnp.where(side == 1, 1, 0))
    index = index.astype(F32).astype(BF16)
    orders, tile_kinds, groups = [], [], []
    for which in (1, 2):
        needed = maps[which : which + 1, :] > 0
        hot = (iota((kinds, length), 0).astype(F32) == near_types) & needed
        hot = hot.astype(F32)
        rank = jnp.dot(hot.astype(BF16), before, preferred_element_type=F32)
        tiles = jnp.floor((jnp.sum(hot, axis=1, keepdims=True) + (TILE - 1)) * (1.0 / TILE))
        tiles = jnp.broadcast_to(tiles, (kinds, 128))
        ends = jnp.dot(upto, tiles.astype(BF16), preferred_element_type=F32)
        starts = (ends - tiles)[:, :1]
        place = jnp.sum(hot * (starts * TILE + rank + 1.0), axis=0, keepdims=True) - 1.0
        hit = (slot == place).astype(F32).astype(BF16)
        found = lax.dot_general(
            index, hit, (((1,), (1,)), ((), ())), preferred_element_type=F32
        )
        orders.append(found[0:1, :] + float(total) * (1.0 - found[1:2, :]))
        kind = jnp.sum(jnp.where(slot_row >= ends[:, :1], 1.0, 0.0), axis=0, keepdims=True)
        tile_kinds.append(jnp.minimum(kind, kinds - 1.0))
        last = jnp.floor((ends[kinds - 1 : kinds, :1] + (GROUP - 1)) * (1.0 / GROUP))
        groups.append(jnp.broadcast_to(last, (1, plan.shape[1])))
    rest = jnp.zeros((2, plan.shape[1]), F32)
    whole = jnp.concatenate(orders + tile_kinds + groups + [rest], axis=0)
    plan[...] = whole.astype(jnp.int32)


def sorted_products(plan, which, source, stacked, low, sizings, store):
    def step(it, carry):
        for one in range(GROUP):
            tile = it * GROUP + one
            kind = plan[2 + which, tile]
            places = [
                pl.ds(pl.multiple_of(plan[which, tile * TILE + j] * sizings, sizings), sizings)
                for j in range(TILE)
            ]
            field = jnp.concatenate([source[place, :] for place in places], axis=0)
            high = field.astype(BF16)
            rest = (field - high.astype(F32)).astype(BF16)
            out = jnp.dot(
                jnp.concatenate([high, rest], axis=1), stacked[kind], preferred_element_type=F32
            ) + jnp.dot(high, low[kind], preferred_element_type=F32)
            store(kind, places, out)
        return carry

    lax.fori_loop(0, plan[4 + which, 0], step, 0)


def neighbour_ids(ids, cols):
    height, many = ids.shape
    lane, row = iota(ids.shape, 1), iota(ids.shape, 0)
    down = pltpu.roll(ids, many - cols, 1)
    south = jnp.where(lane < many - cols, down, pltpu.roll(down, height - 1, 0))
    south = jnp.where((lane >= many - cols) & (row == height - 1), -1.0, south)
    up = pltpu.roll(ids, cols, 1)
    north = jnp.where(lane >= cols, up, pltpu.roll(up, 1, 0))
    north = jnp.where((lane < cols) & (row == 0), -1.0, north)
    east = jnp.where(lane % cols == cols - 1, -1.0, pltpu.roll(ids, many - 1, 1))
    west = jnp.where(lane % cols == 0, -1.0, pltpu.roll(ids, 1, 1))
    return south, north, east, west


def invert_unrolled(ref, count):
    width = ref.shape[1]
    fold = 128 // count
    lane = iota((8, width), 1) % count
    row = iota((8, width), 0)
    tile_lane = iota((8, 128), 1)
    many = count // 8
    tiles = [ref[i * 8 : (i + 1) * 8, :] for i in range(many)]

    def column(tile, k):
        parts = []
        for base in range(0, width, 128):
            part = jnp.broadcast_to(tile[:, base + k : base + k + 1], (8, 128))
            for j in range(1, fold):
                at = base + j * count + k
                part = jnp.where(tile_lane >= j * count, tile[:, at : at + 1], part)
            parts.append(part)
        return jnp.concatenate(parts, axis=1)

    for first in range(0, count, PANEL):
        columns = [[column(t, first + j) for t in tiles] for j in range(PANEL)]
        for j in range(PANEL):
            k = first + j
            at, within = k // 8, k % 8
            here = columns[j]
            inverse = 1.0 / here[at][within : within + 1, :]
            scaled = jnp.where(
                lane[:1] == k, inverse, tiles[at][within : within + 1, :] * inverse
            )
            pivot = row == within
            for i in range(many):
                new = jnp.where(lane == k, 0.0, tiles[i]) - here[i] * scaled
                tiles[i] = jnp.where(pivot, scaled, new) if i == at else new
            for later in range(j + 1, PANEL):
                other = columns[later]
                factor = other[at][within : within + 1, :] * inverse
                for i in range(many):
                    new = other[i] - here[i] * factor
                    other[i] = jnp.where(pivot, factor, new) if i == at else new
    for i in range(many):
        ref[i * 8 : (i + 1) * 8, :] = tiles[i]


def invert_looped(ref, count):
    def step(k, carry):
        for base in range(0, ref.shape[1], count):
            here = slice(base, base + count)
            lane = iota((1, count), 1)
            row = iota((count, 1), 0)
            pivot_row = ref[pl.ds(k, 1), here]
            part = ref[:, here]
            column = jnp.sum(jnp.where(lane == k, part, 0.0), axis=1, keepdims=True)
            inverse = 1.0 / jnp.sum(jnp.where(lane == k, pivot_row, 0.0), axis=1, keepdims=True)
            scaled = jnp.where(lane == k, 1.0, pivot_row) * inverse
            column = jnp.where(row == k, -1.0, column)
            ref[:, here] = jnp.where((lane == k) | (row == k), 0.0, part) - column * scaled
        return carry

    lax.fori_loop(0, count, step, 0)


def coarse_matrices(dims, mesh_dims, gathered, row_sums, strap, inverses, cross):
    sizings, rows, cols, nodes, count = dims
    n_row, n_col = mesh_dims
    many = rows * cols
    height = sizings * count // 128
    kinds = row_sums.shape[0]
    north_weight = jnp.sum(strap[0:1, :], axis=1, keepdims=True)
    east_weight = jnp.sum(strap[1:2, :], axis=1, keepdims=True)
    names = iota((count, many), 0).astype(F32).astype(BF16)
    kind_names = iota((16, many), 0).astype(F32).astype(BF16)
    lane = iota((n_row, many), 1)
    eye = iota((count, count), 0) == iota((count, count), 1)
    contract = (((1,), (1,)), ((), ()))
    spot = iota((kinds, 16), 0) == iota((kinds, 16), 1)
    centre = jnp.sum(row_sums[...], axis=1, keepdims=True) + 2.0 * north_weight
    centre = centre + 2.0 * east_weight
    centre = jnp.sum(jnp.where(spot, centre, 0.0), axis=0, keepdims=True)

    def rows_of(g, at):
        return jnp.concatenate(
            [gathered[i * n_col + g, at : at + 1, 0, :] for i in range(n_row)], axis=0
        )

    def hot(values, labels):
        rows_bf = values.astype(BF16)
        one, zero = jnp.ones(labels.shape, BF16), jnp.zeros(labels.shape, BF16)
        return [
            jnp.where(labels == rows_bf[i : i + 1, :], one, zero) for i in range(n_row)
        ]

    all_ids = [rows_of(g, height + 1) - 1.0 for g in range(n_col)]
    for g in range(n_col):
        ids = all_ids[g]
        beyond = all_ids[min(g + 1, n_col - 1)]
        beyond = jnp.where(lane % cols == cols - 1, pltpu.roll(beyond, cols - 1, 1), -1.0)
        south, north, east, west = [hot(v, names) for v in neighbour_ids(ids, cols)]
        own, over = hot(ids, names), hot(beyond, names)
        types = hot(rows_of(g, height), kind_names)
        right = jnp.concatenate(
            [
                jnp.concatenate([south[i] + north[i], east[i] + west[i], over[i], types[i]], axis=0)
                for i in range(n_row)
            ],
            axis=1,
        )
        pairs = lax.dot_general(
            jnp.concatenate(own, axis=1), right, contract, preferred_element_type=F32
        )
        diagonal = jnp.sum(pairs[:, 3 * count :] * centre, axis=1, keepdims=True)
        inverses[:, g * count : (g + 1) * count] = jnp.where(eye, diagonal, 0.0) - (
            north_weight * pairs[:, :count] + east_weight * pairs[:, count : 2 * count]
        )
        cross[g] = pairs[:, 2 * count : 3 * count]


def total_of(gathered, first, height, mesh_dims, g):
    n_row, n_col = mesh_dims
    total = gathered[g, first : first + height]
    for i in range(1, n_row):
        total = total + gathered[i * n_col + g, first : first + height]
    return total.reshape(height, 128)


def coarse_solve(gathered, first, height, mesh_dims, count, sizings, inverses, g):
    sums = unpack(total_of(gathered, first, height, mesh_dims, g), count, sizings)
    solved = jnp.dot(
        sums, inverses[:, g * count : (g + 1) * count], precision=HIGHEST,
        preferred_element_type=F32,
    )
    return sums, solved


def spread(solved, col, keys, out, count, sizings, nodes, many):
    three = jnp.concatenate([solved[col], solved[col + 1], solved[col + 2]], axis=1)
    hot = (iota((3 * count, keys.shape[1]), 0) == keys[...]).astype(F32).astype(BF16)
    parts = jnp.concatenate(split3(three), axis=0)
    values = jnp.dot(parts, hot, preferred_element_type=F32)
    values = (
        values[2 * sizings : 3 * sizings] + values[sizings : 2 * sizings] + values[:sizings]
    )
    for e in range(many):
        out[e * sizings : (e + 1) * sizings, :] = jnp.broadcast_to(
            values[:, e : e + 1], (sizings, nodes)
        )


def coarse_kernel(dims, mesh_dims, gathered, row_sums, strap, inverses, cross, solved):
    sizings, rows, cols, nodes, count = dims
    n_col = mesh_dims[1]
    height = sizings * count // 128
    coarse_matrices(dims, mesh_dims, gathered, row_sums, strap, inverses, cross)
    if count <= 64:
        invert_unrolled(inverses, count)
    else:
        invert_looped(inverses, count)
    solved[0] = jnp.zeros((sizings, count), F32)
    solved[n_col + 1] = jnp.zeros((sizings, count), F32)
    for g in range(n_col):
        _, solved[g + 1] = coarse_solve(
            gathered, 0, height, mesh_dims, count, sizings, inverses, g
        )


def middle_kernel(
    dims,
    plan, info, ids,
    solved, keys, blocks, row_first, row_second, col_first, col_second,
    stacked, low, row_sums, strap,
    z_out, q_out, u_out, au_out, pay,
    field, level, z, bz, q, u, bu,
):
    sizings, rows, cols, nodes, count = dims
    wide = cols + 4
    many = (rows + 4) * wide

    def at(er, ec):
        return pl.ds(pl.multiple_of((er * wide + ec) * sizings, sizings), sizings)

    row_odd, col_odd = info[5], info[6]
    span = cols * sizings
    for r in range(rows):
        to = ((r + 2) * wide + 2) * sizings
        field[to : to + span, :] = blocks[r * span : (r + 1) * span, :]
    for r in range(2):
        for c in range(cols):
            edge = pl.ds(r * cols + c, sizings, stride=2 * cols)
            one, two = row_first[edge, :], row_second[edge, :]
            to = (r * wide + 2 + c) * sizings
            field[to : to + sizings, :] = either(row_odd, two, one)
            to = ((rows + 2 + r) * wide + 2 + c) * sizings
            field[to : to + sizings, :] = either(row_odd, one, two)
    for k in range(rows + 2):
        pair = 2 * sizings
        one, two = [ref[k * pair : (k + 1) * pair, :] for ref in (col_first, col_second)]
        to = (k + 1) * wide * sizings
        field[to : to + pair, :] = either(col_odd, two, one)
        to = to + (cols + 2) * sizings
        field[to : to + pair, :] = either(col_odd, one, two)
    field[many * sizings :, :] = jnp.zeros((sizings, nodes), F32)
    level[many * sizings :, :] = jnp.zeros((sizings, nodes), F32)
    q[many * sizings :, :] = jnp.zeros((sizings, nodes), F32)
    spread(solved, info[0], keys, level, count, sizings, nodes, many)

    def store_z(kind, places, out):
        sums = row_sums[pl.ds(kind, 1), :]
        for j, place in enumerate(places):
            here = level[place, :]
            z[place, :] = out[j * sizings : (j + 1) * sizings, :nodes] + here
            bz[place, :] = out[j * sizings : (j + 1) * sizings, nodes:] + sums * here

    sorted_products(plan, 0, field, stacked, low, sizings, store_z)

    north, east_strap = strap[0:1, :], strap[1:2, :]
    couple = 2.0 * north + 2.0 * east_strap

    def operator(v, bv, er, ec, row=None):
        row = row or [v[at(er, ec + j), :] for j in (-1, 0, 1)]
        image = (
            bv[at(er, ec), :]
            + couple * row[1]
            - north * (v[at(er - 1, ec), :] + v[at(er + 1, ec), :])
            - east_strap * (row[0] + row[2])
        )
        return row[1], image

    for er, flag in ((1, info[1]), (rows + 2, info[2])):
        inside = flag.astype(F32)

        def across(ec, carry):
            q[at(er, ec), :] = operator(z, bz, er, ec)[1] * inside
            return carry

        lax.fori_loop(2, cols + 2, across, 0)
    for ec, flag in ((1, info[3]), (cols + 2, info[4])):
        inside = flag.astype(F32)

        def along(er, carry):
            q[at(er, ec), :] = operator(z, bz, er, ec)[1] * inside
            return carry

        lax.fori_loop(2, rows + 2, along, 0)

    lanes = iota((sizings, max(count, 128)), 1)
    blank = jnp.zeros((sizings, nodes), F32)
    zero_sums = jnp.zeros(lanes.shape, F32)

    def first_row(r, carry):
        rz, zq, sums = carry
        line = [z[at(r + 2, 1), :], z[at(r + 2, 2), :]]
        for c in range(cols):
            line.append(z[at(r + 2, c + 3), :])
            here, image = operator(z, bz, r + 2, c + 2, line[c : c + 3])
            q[at(r + 2, c + 2), :] = image
            b = r * cols + c
            own = pl.ds(pl.multiple_of(b * sizings, sizings), sizings)
            z_out[own, :] = here
            q_out[own, :] = image
            rz = rz + blocks[own, :] * here
            zq = zq + here * image
            total = jnp.sum(image, axis=1, keepdims=True)
            sums = sums + jnp.where(lanes == ids[r, c], total, 0.0)
        return rz, zq, sums

    rz, zq, sums_q = lax.fori_loop(0, rows, first_row, (blank, blank, zero_sums))

    def store_u(kind, places, out):
        for j, place in enumerate(places):
            u[place, :] = out[j * sizings : (j + 1) * sizings, :nodes]
            bu[place, :] = out[j * sizings : (j + 1) * sizings, nodes:]

    sorted_products(plan, 1, q, stacked, low, sizings, store_u)

    def second_row(r, carry):
        qu, uau, sums = carry
        line = [u[at(r + 2, 1), :], u[at(r + 2, 2), :]]
        for c in range(cols):
            line.append(u[at(r + 2, c + 3), :])
            here, image = operator(u, bu, r + 2, c + 2, line[c : c + 3])
            b = r * cols + c
            own = pl.ds(pl.multiple_of(b * sizings, sizings), sizings)
            u_out[own, :] = here
            au_out[own, :] = image
            qu = qu + q[at(r + 2, c + 2), :] * here
            uau = uau + here * image
            total = jnp.sum(image, axis=1, keepdims=True)
            sums = sums + jnp.where(lanes == ids[r, c], total, 0.0)
        return qu, uau, sums

    qu, uau, sums_u = lax.fori_loop(0, rows, second_row, (blank, blank, zero_sums))

    lane = iota((sizings, 128), 1)
    dots = jnp.zeros((sizings, 128), F32)
    for j, one in enumerate((rz, zq, qu, uau)):
        dots = jnp.where(lane % 4 == j, jnp.sum(one, axis=1, keepdims=True), dots)
    dots = jnp.where(lane // 4 == iota((sizings, 128), 0), dots, 0.0)
    dots = jnp.sum(dots, axis=0, keepdims=True)
    whole = jnp.concatenate([pack(sums_q, count), pack(sums_u, count), dots], axis=0)

    send_all(pay, whole)


def last_kernel(
    dims, mesh_dims,
    types, info,
    gathered, keys, inverses, cross, z, q, u, au, blocks, row_sums, strap,
    voltage, residual,
    level, solved,
):
    sizings, rows, cols, nodes, count = dims
    n_row, n_col = mesh_dims
    wide = cols + 4
    many = (rows + 4) * wide
    height = sizings * count // 128
    mesh_args = (mesh_dims, count, sizings)

    solved[0] = jnp.zeros((sizings, count), F32)
    solved[n_col + 1] = jnp.zeros((sizings, count), F32)
    with_q = jnp.zeros((sizings, count), F32)
    with_u = jnp.zeros((sizings, count), F32)
    crossed = jnp.zeros((sizings, count), F32)
    before = None
    for g in range(n_col):
        sums, one = coarse_solve(gathered, 0, height, *mesh_args, inverses, g)
        solved[g + 1] = one
        image = total_of(gathered, height, height, mesh_dims, g)
        with_q = with_q + sums * one
        with_u = with_u + unpack(image, count, sizings) * one
        if before is not None:
            crossed = crossed + one * jnp.dot(
                before, cross[g - 1], precision=HIGHEST, preferred_element_type=F32
            )
        before = one
    spread(solved, info[0], keys, level, count, sizings, nodes, many)

    dots = gathered[0, 2 * height]
    for d in range(1, n_row * n_col):
        dots = dots + gathered[d, 2 * height]
    lane = iota((sizings, 128), 1)
    dots = jnp.where(lane // 4 == iota((sizings, 128), 0), dots, 0.0)
    rz, zq, qu, uau = [
        jnp.sum(jnp.where(lane % 4 == j, dots, 0.0), axis=1, keepdims=True) for j in range(4)
    ]
    east_weight = jnp.sum(strap[1:2, :], axis=1, keepdims=True)
    total = functools.partial(jnp.sum, axis=1, keepdims=True)
    qw = qu + total(with_q)
    wp = uau + 2.0 * total(with_u) + total(with_q) - 2.0 * east_weight * total(crossed)
    step_1 = rz / zq
    fresh = step_1 * step_1 * qw - rz
    grown = 1.0 + fresh / rz
    step_2 = fresh / (grown * grown * zq - 2.0 * grown * step_1 * qw + step_1 * step_1 * wp)
    alpha = jnp.broadcast_to(step_1 + step_2 * grown, (sizings, nodes))
    gamma = jnp.broadcast_to(-step_2 * step_1, (sizings, nodes))

    north, east_strap = strap[0:1, :], strap[1:2, :]
    couple = 2.0 * north + 2.0 * east_strap

    def step(r, carry):
        for c in range(cols):
            b = r * cols + c
            own = pl.ds(pl.multiple_of(b * sizings, sizings), sizings)

            def value(dr, dc):
                e = (r + 2 + dr) * wide + c + 2 + dc
                return level[pl.ds(pl.multiple_of(e * sizings, sizings), sizings), :]

            here = value(0, 0)
            lift = (
                (row_sums[pl.ds(types[r, c], 1), :] + couple) * here
                - north * (value(-1, 0) + value(1, 0))
                - east_strap * (value(0, -1) + value(0, 1))
            )
            voltage[pl.ds(b, sizings, stride=rows * cols), :] = alpha * z[own, :] + gamma * (
                u[own, :] + here
            )
            residual[pl.ds(b, sizings, stride=rows * cols), :] = (
                blocks[own, :] - alpha * q[own, :] - gamma * (au[own, :] + lift)
            )
        return carry

    lax.fori_loop(0, rows, step, 0)


def ring_maps(rows, cols, count):
    tall, wide = rows + 4, cols + 4
    many = rows * cols
    length = -(-tall * wide // 128) * 128
    maps = np.zeros((8, length), np.int32)
    maps[0] = -1
    for er in range(tall):
        for ec in range(wide):
            e = er * wide + ec
            down = max(2 - er, er - (rows + 1), 0)
            over = max(2 - ec, ec - (cols + 1), 0)
            maps[1, e] = down + over <= 2
            maps[2, e] = down + over <= 1
            maps[3, e] = count * ((ec >= 2) + (ec >= cols + 2))
            if not down and not over:
                maps[0, e] = (er - 2) * cols + ec - 2
            elif not over:
                south = er > 1
                maps[0, e] = (1 + south) * many + (er - (rows + 2 if south else 0)) * cols + ec - 2
            elif down <= 1:
                right = ec > 1
                maps[0, e] = (3 + right) * many + (er - 1) * 2 + ec - (cols + 2 if right else 0)
    return maps


def call(kernel, in_specs, out_shape, scratch, cost, megabytes, **more):
    return pl.pallas_call(
        kernel,
        in_specs=in_specs,
        out_specs=jax.tree.map(lambda _: VMEM, out_shape),
        out_shape=out_shape,
        scratch_shapes=scratch,
        compiler_params=pltpu.CompilerParams(vmem_limit_bytes=megabytes * 1024 * 1024),
        cost_estimate=pl.CostEstimate(flops=cost, bytes_accessed=4_000_000, transcendentals=0),
        **more,
    )


def swap(payload, axis, begin):
    pairs = [(i, i + 1) for i in range(begin, lax.axis_size(axis) - 1, 2)]
    return lax.ppermute(payload, axis, pairs + [(j, i) for i, j in pairs])


def on_device(load_currents, block_library, strap_conductance, block_types, aggregate_map):
    sizings, rows, cols, nodes = load_currents.shape
    kinds = block_library.shape[0]
    n_row, n_col = lax.axis_size("row"), lax.axis_size("col")
    n_dev = n_row * n_col
    row, col = lax.axis_index("row"), lax.axis_index("col")
    count = rows * n_row // AGR * (cols // AGC)
    dims, mesh_dims = (sizings, rows, cols, nodes, count), (n_row, n_col)
    block_rows = rows * cols * sizings
    many = (rows + 4) * (cols + 4)
    height = sizings * count // 128
    shape = jax.ShapeDtypeStruct
    own = shape((block_rows, nodes), F32)

    info = jnp.stack(
        [
            col,
            (row > 0).astype(jnp.int32),
            (row < n_row - 1).astype(jnp.int32),
            (col > 0).astype(jnp.int32),
            (col < n_col - 1).astype(jnp.int32),
            row % 2,
            col % 2,
        ]
    )
    edge = shape((sizings + 1, 2, cols, nodes), F32)
    first, second = call(
        functools.partial(edges_kernel, dims),
        [SMEM] + [HBM] * 3,
        [edge, edge],
        [pltpu.VMEM((rows, cols), jnp.int32)] * 2 + [pltpu.SemaphoreType.DMA((4,))],
        1_000_000,
        4,
    )(info, load_currents, block_types, aggregate_map)
    edge_rows = (sizings + 1) * 2 * cols
    row_first = swap(first.reshape(edge_rows, nodes), "row", 0)
    row_second = swap(second.reshape(edge_rows, nodes), "row", 1)

    pay_rows = height + 2
    flat_load = load_currents.reshape(-1, nodes)
    (pay,) = call(
        functools.partial(sums_kernel, dims),
        [SMEM] + [VMEM] * 3,
        [shape((n_dev, pay_rows, 1, 128), F32)],
        [],
        20_000_000_000,
        4 if count <= 64 else 16,
    )(aggregate_map, block_types, aggregate_map, flat_load)
    gathered = lax.all_to_all(pay, ("row", "col"), 0, 0)
    stacked, low, row_sums = call(
        weights_kernel,
        [VMEM, VMEM],
        [
            shape((kinds, 2 * nodes, 2 * nodes), BF16),
            shape((kinds, nodes, 2 * nodes), BF16),
            shape((kinds, nodes), F32),
        ],
        [],
        1_000_000,
        8,
    )(block_library, strap_conductance)
    (blocks,) = call(
        functools.partial(blocks_kernel, dims), [VMEM], [own], [], 1_000_000, 4
    )(flat_load)
    side_rows = (rows + 2) * 2 * sizings
    side = shape((side_rows + 8, nodes), F32)
    first, second = call(
        functools.partial(sides_kernel, dims),
        [SMEM] + [VMEM] * 6,
        [side, side],
        [],
        40_000_000_000,
        4,
    )(info, block_types, aggregate_map, blocks, row_first, row_second, row_sums)
    col_first, col_second = swap(first, "col", 0), swap(second, "col", 1)

    big = pltpu.VMEM(((many + 1) * sizings, nodes), F32)
    coarse_shape = (n_col + 2, sizings, count)
    inverses, cross, solved = call(
        functools.partial(coarse_kernel, dims, mesh_dims),
        [VMEM] * 3,
        [
            shape((count, n_col * count), F32),
            shape((n_col, count, count), F32),
            shape(coarse_shape, F32),
        ],
        [],
        10_000_000_000,
        8 if count <= 64 else 48,
    )(gathered, row_sums, strap_conductance)
    maps = ring_maps(rows, cols, count)
    longest = int(max(maps[1].sum(), maps[2].sum())) + (TILE - 1) * kinds + GROUP * TILE
    longest = -(-longest // 128) * 128
    edge_meta = pl.BlockSpec((8, 128), lambda i: (sizings * 2 * cols // 8, 0))
    side_meta = pl.BlockSpec((8, 128), lambda i: (side_rows // 8, 0))
    plan, keys = call(
        functools.partial(order_kernel, dims, kinds),
        [SMEM] + [VMEM] * 3 + [edge_meta, edge_meta, side_meta, side_meta, VMEM],
        [shape((8, longest), jnp.int32), shape((1, maps.shape[1]), jnp.int32)],
        [],
        1_000_000,
        8,
        grid=(1,),
    )(
        info, jnp.asarray(maps), block_types, aggregate_map,
        row_first, row_second, col_first, col_second, solved,
    )
    z, q, u, au, pay = call(
        functools.partial(middle_kernel, dims),
        [SMEM] * 3 + [VMEM] * 11,
        [own] * 4 + [shape((n_dev, 2 * height + 1, 1, 128), F32)],
        [big] * 7,
        1_000_000_000,
        20 if count <= 64 else 48,
    )(
        plan, info, aggregate_map,
        solved, keys, blocks, row_first, row_second, col_first, col_second,
        stacked, low, row_sums, strap_conductance,
    )
    gathered = lax.all_to_all(pay, ("row", "col"), 0, 0)
    out = shape((sizings * rows * cols, nodes), F32)
    voltage, residual = call(
        functools.partial(last_kernel, dims, mesh_dims),
        [SMEM] * 2 + [VMEM] * 11,
        [out, out],
        [big, pltpu.VMEM(coarse_shape, F32)],
        1_000_000_000,
        8 if count <= 64 else 32,
    )(
        block_types, info,
        gathered, keys, inverses, cross, z, q, u, au, blocks, row_sums, strap_conductance,
    )
    return voltage.reshape(load_currents.shape), residual.reshape(load_currents.shape)


def solution(mesh):
    placed = (P(None, "row", "col", None), P(), P(), P("row", "col"), P("row", "col"))
    return jax.shard_map(
        on_device,
        mesh=mesh,
        in_specs=placed,
        out_specs=(P(None, "row", "col", None), P(None, "row", "col", None)),
        check_vma=False,
    )
```

```python
import functools

import jax
import jax.numpy as jnp
from jax import lax
from jax.experimental import pallas as pl
from jax.experimental.pallas import tpu as pltpu
from jax.sharding import PartitionSpec as P
import numpy as np

AGR = 4
AGC = 4
TILE = 8
GROUP = 4
PANEL = 8
F32 = jnp.float32
BF16 = jnp.bfloat16
HIGHEST = lax.Precision.HIGHEST
VMEM = pl.BlockSpec(memory_space=pltpu.VMEM)
SMEM = pl.BlockSpec(memory_space=pltpu.SMEM)


def iota(shape, dim):
    return lax.broadcasted_iota(jnp.int32, shape, dim)


def pack(values, count):
    if count < 128:
        fold = 128 // count
        height = values.shape[0] // fold
        return jnp.concatenate(
            [values[p * height : (p + 1) * height, :count] for p in range(fold)], axis=1
        )
    return jnp.concatenate([values[:, j : j + 128] for j in range(0, count, 128)], axis=0)


def unpack(rows, count, sizings):
    if count < 128:
        return jnp.concatenate(
            [rows[:, j : j + count] for j in range(0, 128, count)], axis=0
        )
    return jnp.concatenate(
        [rows[j : j + sizings] for j in range(0, rows.shape[0], sizings)], axis=1
    )


def split3(values):
    first = values.astype(BF16)
    rest = values - first.astype(F32)
    second = rest.astype(BF16)
    third = (rest - second.astype(F32)).astype(BF16)
    return first, second, third


def flat_row(table, many):
    rows, cols = table.shape
    repeat = (iota((cols, many), 1) % cols == iota((cols, many), 0)).astype(F32).astype(BF16)
    wide = jnp.dot(table.astype(F32).astype(BF16), repeat, preferred_element_type=F32)
    own = iota((rows, many), 1) // cols == iota((rows, many), 0)
    return jnp.sum(jnp.where(own, wide, 0.0), axis=0, keepdims=True)


def meta_rows(types, ids, many, height):
    rows = [flat_row(types[...], many), flat_row(ids[...], many) + 1.0]
    spare = [jnp.zeros((height - 2, many), F32)] if height > 2 else []
    return jnp.concatenate(rows + spare, axis=0)


def either(odd, if_even, if_odd):
    return jnp.where(odd == 1, if_odd, if_even)


def sums_kernel(dims, ids_smem, types, ids, load, pay):
    sizings, rows, cols, nodes, count = dims
    many = rows * cols
    width = max(count, 128)
    lane, side = iota((cols, width), 1), iota((cols, width), 0)
    hots = []
    for r in range(rows):
        names = jnp.zeros((cols, width), jnp.int32)
        for c in range(cols):
            names = jnp.where(side == c, ids_smem[r, c], names)
        hots.append((names == lane).astype(F32))
    sums = []
    for s in range(sizings):
        total = jnp.zeros((cols, width), F32)
        for r in range(rows):
            at = s * many + r * cols
            total = total + hots[r] * jnp.sum(load[at : at + cols, :], axis=1, keepdims=True)
        sums.append(jnp.sum(total, axis=0, keepdims=True))
    height = sizings * count // 128
    meta = meta_rows(types, ids, many, pay.shape[1] - height)
    whole = jnp.concatenate([pack(jnp.concatenate(sums, axis=0), count), meta], axis=0)
    send_all(pay, whole)


def send_all(pay, whole):
    def copy(d, carry):
        pay[d] = whole.reshape(pay.shape[1:])
        return carry

    lax.fori_loop(0, pay.shape[0], copy, 0)


def blocks_kernel(dims, load, blocks):
    sizings, rows, cols, nodes, count = dims
    many = rows * cols

    def step(r, carry):
        for c in range(cols):
            b = r * cols + c
            at = pl.ds(pl.multiple_of(b * sizings, sizings), sizings)
            blocks[at, :] = load[pl.ds(b, sizings, stride=many), :]
        return carry

    lax.fori_loop(0, rows, step, 0)


def weights_kernel(library, strap, stacked, low, row_sums):
    kinds, nodes, _ = library.shape
    eye = iota((nodes, nodes), 0) == iota((nodes, nodes), 1)
    couple_row = 2.0 * strap[0:1, :] + 2.0 * strap[1:2, :]
    couple_col = jnp.sum(jnp.where(eye, couple_row, 0.0), axis=1, keepdims=True)

    def step(t, carry):
        block = library[t]
        on = jnp.where(eye, block, 0.0)
        inv_row = 1.0 / (jnp.sum(on, axis=0, keepdims=True) + couple_row)
        inv_col = 1.0 / (jnp.sum(on, axis=1, keepdims=True) + couple_col)
        off = jnp.where(eye, 0.0, -block)
        once = inv_col * off * inv_row
        twice = jnp.dot(once, off, precision=HIGHEST, preferred_element_type=F32) * inv_row
        smoother = jnp.where(eye, inv_row, 0.0) + once + twice
        product = jnp.dot(smoother, block, precision=HIGHEST, preferred_element_type=F32)
        both = jnp.concatenate([smoother, product], axis=1)
        high = both.astype(BF16)
        stacked[t] = jnp.concatenate([high, high], axis=0)
        low[t] = (both - high.astype(F32)).astype(BF16)
        row_sums[pl.ds(t, 1), :] = jnp.sum(block, axis=0, keepdims=True)
        return carry

    lax.fori_loop(0, kinds, step, 0, unroll=True)


def sides_kernel(dims, info, blocks, row_first, row_second, row_sums, first, second):
    sizings, rows, cols, nodes, count = dims
    row_odd, odd = info[5], info[6]
    for out, begin in ((first, either(odd, cols - 2, 0)), (second, either(odd, 0, cols - 2))):
        for side in range(2):
            c = begin + side
            above = pl.ds(cols + c, sizings, stride=2 * cols)
            below = pl.ds(c, sizings, stride=2 * cols)
            to = side * sizings
            out[to : to + sizings, :] = either(row_odd, row_second[above, :], row_first[above, :])
            to = ((rows + 1) * 2 + side) * sizings
            out[to : to + sizings, :] = either(row_odd, row_first[below, :], row_second[below, :])
            for r in range(rows):
                at = pl.multiple_of((r * cols + c) * sizings, sizings)
                to = ((r + 1) * 2 + side) * sizings
                out[to : to + sizings, :] = blocks[pl.ds(at, sizings), :]


def order_blocks(dims, mesh_dims, kinds, info, maps, gathered, plan, keys):
    sizings, rows, cols, nodes, count = dims
    n_row, n_col = mesh_dims
    height = sizings * count // 128
    metas = []
    for down in (-1, 0, 1):
        for right in (-1, 0, 1):
            r, c = info[7] + down, info[0] + right
            inside = (r >= 0) & (r < n_row) & (c >= 0) & (c < n_col)
            device = jnp.clip(r, 0, n_row - 1) * n_col + jnp.clip(c, 0, n_col - 1)
            meta = gathered[device, height : height + 2].reshape(2, 128)
            metas.append(meta * inside.astype(F32))
    metas = jnp.concatenate(metas, axis=1)
    shape = (metas.shape[1], maps.shape[1])
    pick = (iota(shape, 0) == maps[0:1, :]).astype(F32).astype(BF16)
    near = jnp.dot(metas.astype(BF16), pick, preferred_element_type=F32)
    near_types, near_ids = near[0:1, :], near[1:2, :]
    keys[...] = jnp.where(
        near_ids > 0.0, near_ids - 1.0 + maps[3:4, :].astype(F32), -1.0
    ).astype(jnp.int32)

    length = maps.shape[1]
    total = (rows + 4) * (cols + 4)
    before = (iota((length, length), 0) < iota((length, length), 1)).astype(F32).astype(BF16)
    upto = (iota((kinds, kinds), 0) >= iota((kinds, kinds), 1)).astype(F32).astype(BF16)
    slot = iota((plan.shape[1], length), 0).astype(F32)
    slot_row = iota((kinds, plan.shape[1]), 1).astype(F32)
    side = iota((8, length), 0)
    index = jnp.where(side == 0, iota((8, length), 1), jnp.where(side == 1, 1, 0))
    index = index.astype(F32).astype(BF16)
    orders, tile_kinds, groups = [], [], []
    for which in (1, 2):
        needed = maps[which : which + 1, :] > 0
        hot = (iota((kinds, length), 0).astype(F32) == near_types) & needed
        hot = hot.astype(F32)
        rank = jnp.dot(hot.astype(BF16), before, preferred_element_type=F32)
        tiles = jnp.floor((jnp.sum(hot, axis=1, keepdims=True) + (TILE - 1)) * (1.0 / TILE))
        tiles = jnp.broadcast_to(tiles, (kinds, 128))
        ends = jnp.dot(upto, tiles.astype(BF16), preferred_element_type=F32)
        starts = (ends - tiles)[:, :1]
        place = jnp.sum(hot * (starts * TILE + rank + 1.0), axis=0, keepdims=True) - 1.0
        hit = (slot == place).astype(F32).astype(BF16)
        found = lax.dot_general(
            index, hit, (((1,), (1,)), ((), ())), preferred_element_type=F32
        )
        orders.append(found[0:1, :] + float(total) * (1.0 - found[1:2, :]))
        kind = jnp.sum(jnp.where(slot_row >= ends[:, :1], 1.0, 0.0), axis=0, keepdims=True)
        tile_kinds.append(jnp.minimum(kind, kinds - 1.0))
        last = jnp.floor((ends[kinds - 1 : kinds, :1] + (GROUP - 1)) * (1.0 / GROUP))
        groups.append(jnp.broadcast_to(last, (1, plan.shape[1])))
    rest = jnp.zeros((2, plan.shape[1]), F32)
    whole = jnp.concatenate(orders + tile_kinds + groups + [rest], axis=0)
    plan[...] = whole.astype(jnp.int32)


def sorted_products(plan, which, source, stacked, low, sizings, store):
    def step(it, carry):
        for one in range(GROUP):
            tile = it * GROUP + one
            kind = plan[2 + which, tile]
            places = [
                pl.ds(pl.multiple_of(plan[which, tile * TILE + j] * sizings, sizings), sizings)
                for j in range(TILE)
            ]
            field = jnp.concatenate([source[place, :] for place in places], axis=0)
            high = field.astype(BF16)
            rest = (field - high.astype(F32)).astype(BF16)
            out = jnp.dot(
                jnp.concatenate([high, rest], axis=1), stacked[kind], preferred_element_type=F32
            ) + jnp.dot(high, low[kind], preferred_element_type=F32)
            store(kind, places, out)
        return carry

    lax.fori_loop(0, plan[4 + which, 0], step, 0)


def neighbour_ids(ids, cols):
    height, many = ids.shape
    lane, row = iota(ids.shape, 1), iota(ids.shape, 0)
    down = pltpu.roll(ids, many - cols, 1)
    south = jnp.where(lane < many - cols, down, pltpu.roll(down, height - 1, 0))
    south = jnp.where((lane >= many - cols) & (row == height - 1), -1.0, south)
    up = pltpu.roll(ids, cols, 1)
    north = jnp.where(lane >= cols, up, pltpu.roll(up, 1, 0))
    north = jnp.where((lane < cols) & (row == 0), -1.0, north)
    east = jnp.where(lane % cols == cols - 1, -1.0, pltpu.roll(ids, many - 1, 1))
    west = jnp.where(lane % cols == 0, -1.0, pltpu.roll(ids, 1, 1))
    return south, north, east, west


def invert_unrolled(ref, count):
    width = ref.shape[1]
    fold = 128 // count
    lane = iota((8, width), 1) % count
    row = iota((8, width), 0)
    tile_lane = iota((8, 128), 1)
    many = count // 8
    tiles = [ref[i * 8 : (i + 1) * 8, :] for i in range(many)]

    def column(tile, k):
        parts = []
        for base in range(0, width, 128):
            part = jnp.broadcast_to(tile[:, base + k : base + k + 1], (8, 128))
            for j in range(1, fold):
                at = base + j * count + k
                part = jnp.where(tile_lane >= j * count, tile[:, at : at + 1], part)
            parts.append(part)
        return jnp.concatenate(parts, axis=1)

    for first in range(0, count, PANEL):
        columns = [[column(t, first + j) for t in tiles] for j in range(PANEL)]
        for j in range(PANEL):
            k = first + j
            at, within = k // 8, k % 8
            here = columns[j]
            inverse = 1.0 / here[at][within : within + 1, :]
            scaled = jnp.where(
                lane[:1] == k, inverse, tiles[at][within : within + 1, :] * inverse
            )
            pivot = row == within
            for i in range(many):
                new = jnp.where(lane == k, 0.0, tiles[i]) - here[i] * scaled
                tiles[i] = jnp.where(pivot, scaled, new) if i == at else new
            for later in range(j + 1, PANEL):
                other = columns[later]
                factor = other[at][within : within + 1, :] * inverse
                for i in range(many):
                    new = other[i] - here[i] * factor
                    other[i] = jnp.where(pivot, factor, new) if i == at else new
    for i in range(many):
        ref[i * 8 : (i + 1) * 8, :] = tiles[i]


def invert_looped(ref, count):
    def step(k, carry):
        for base in range(0, ref.shape[1], count):
            here = slice(base, base + count)
            lane = iota((1, count), 1)
            row = iota((count, 1), 0)
            pivot_row = ref[pl.ds(k, 1), here]
            part = ref[:, here]
            column = jnp.sum(jnp.where(lane == k, part, 0.0), axis=1, keepdims=True)
            inverse = 1.0 / jnp.sum(jnp.where(lane == k, pivot_row, 0.0), axis=1, keepdims=True)
            scaled = jnp.where(lane == k, 1.0, pivot_row) * inverse
            column = jnp.where(row == k, -1.0, column)
            ref[:, here] = jnp.where((lane == k) | (row == k), 0.0, part) - column * scaled
        return carry

    lax.fori_loop(0, count, step, 0)


def coarse_matrices(dims, mesh_dims, gathered, row_sums, strap, inverses, cross):
    sizings, rows, cols, nodes, count = dims
    n_row, n_col = mesh_dims
    many = rows * cols
    height = sizings * count // 128
    kinds = row_sums.shape[0]
    north_weight = jnp.sum(strap[0:1, :], axis=1, keepdims=True)
    east_weight = jnp.sum(strap[1:2, :], axis=1, keepdims=True)
    names = iota((count, many), 0).astype(F32).astype(BF16)
    kind_names = iota((16, many), 0).astype(F32).astype(BF16)
    lane = iota((n_row, many), 1)
    eye = iota((count, count), 0) == iota((count, count), 1)
    contract = (((1,), (1,)), ((), ()))
    spot = iota((kinds, 16), 0) == iota((kinds, 16), 1)
    centre = jnp.sum(row_sums[...], axis=1, keepdims=True) + 2.0 * north_weight
    centre = centre + 2.0 * east_weight
    centre = jnp.sum(jnp.where(spot, centre, 0.0), axis=0, keepdims=True)

    def rows_of(g, at):
        return jnp.concatenate(
            [gathered[i * n_col + g, at : at + 1, 0, :] for i in range(n_row)], axis=0
        )

    def hot(values, labels):
        rows_bf = values.astype(BF16)
        one, zero = jnp.ones(labels.shape, BF16), jnp.zeros(labels.shape, BF16)
        return [
            jnp.where(labels == rows_bf[i : i + 1, :], one, zero) for i in range(n_row)
        ]

    all_ids = [rows_of(g, height + 1) - 1.0 for g in range(n_col)]
    for g in range(n_col):
        ids = all_ids[g]
        beyond = all_ids[min(g + 1, n_col - 1)]
        beyond = jnp.where(lane % cols == cols - 1, pltpu.roll(beyond, cols - 1, 1), -1.0)
        south, north, east, west = [hot(v, names) for v in neighbour_ids(ids, cols)]
        own, over = hot(ids, names), hot(beyond, names)
        types = hot(rows_of(g, height), kind_names)
        right = jnp.concatenate(
            [
                jnp.concatenate([south[i] + north[i], east[i] + west[i], over[i], types[i]], axis=0)
                for i in range(n_row)
            ],
            axis=1,
        )
        pairs = lax.dot_general(
            jnp.concatenate(own, axis=1), right, contract, preferred_element_type=F32
        )
        diagonal = jnp.sum(pairs[:, 3 * count :] * centre, axis=1, keepdims=True)
        inverses[:, g * count : (g + 1) * count] = jnp.where(eye, diagonal, 0.0) - (
            north_weight * pairs[:, :count] + east_weight * pairs[:, count : 2 * count]
        )
        cross[g] = pairs[:, 2 * count : 3 * count]


def total_of(gathered, first, height, mesh_dims, g):
    n_row, n_col = mesh_dims
    total = gathered[g, first : first + height]
    for i in range(1, n_row):
        total = total + gathered[i * n_col + g, first : first + height]
    return total.reshape(height, 128)


def coarse_solve(gathered, first, height, mesh_dims, count, sizings, inverses, g):
    sums = unpack(total_of(gathered, first, height, mesh_dims, g), count, sizings)
    solved = jnp.dot(
        sums, inverses[:, g * count : (g + 1) * count], precision=HIGHEST,
        preferred_element_type=F32,
    )
    return sums, solved


def spread(solved, col, keys, out, count, sizings, nodes, many):
    three = jnp.concatenate([solved[col], solved[col + 1], solved[col + 2]], axis=1)
    hot = (iota((3 * count, keys.shape[1]), 0) == keys[...]).astype(F32).astype(BF16)
    parts = jnp.concatenate(split3(three), axis=0)
    values = jnp.dot(parts, hot, preferred_element_type=F32)
    values = (
        values[2 * sizings : 3 * sizings] + values[sizings : 2 * sizings] + values[:sizings]
    )
    for e in range(many):
        out[e * sizings : (e + 1) * sizings, :] = jnp.broadcast_to(
            values[:, e : e + 1], (sizings, nodes)
        )


def coarse_kernel(
    dims, mesh_dims, kinds, info, maps, gathered, row_sums, strap,
    inverses, cross, solved, plan, keys,
):
    sizings, rows, cols, nodes, count = dims
    n_col = mesh_dims[1]
    height = sizings * count // 128
    order_blocks(dims, mesh_dims, kinds, info, maps, gathered, plan, keys)
    coarse_matrices(dims, mesh_dims, gathered, row_sums, strap, inverses, cross)
    if count <= 64:
        invert_unrolled(inverses, count)
    else:
        invert_looped(inverses, count)
    solved[0] = jnp.zeros((sizings, count), F32)
    solved[n_col + 1] = jnp.zeros((sizings, count), F32)
    for g in range(n_col):
        _, solved[g + 1] = coarse_solve(
            gathered, 0, height, mesh_dims, count, sizings, inverses, g
        )


def middle_kernel(
    dims,
    plan, info, ids,
    solved, keys, blocks, row_first, row_second, col_first, col_second,
    stacked, low, row_sums, strap,
    z_out, q_out, u_out, au_out, pay,
    field, level, z, bz, q, u, bu,
):
    sizings, rows, cols, nodes, count = dims
    wide = cols + 4
    many = (rows + 4) * wide

    def at(er, ec):
        return pl.ds(pl.multiple_of((er * wide + ec) * sizings, sizings), sizings)

    row_odd, col_odd = info[5], info[6]
    span = cols * sizings
    for r in range(rows):
        to = ((r + 2) * wide + 2) * sizings
        field[to : to + span, :] = blocks[r * span : (r + 1) * span, :]
    for r in range(2):
        for c in range(cols):
            edge = pl.ds(r * cols + c, sizings, stride=2 * cols)
            one, two = row_first[edge, :], row_second[edge, :]
            to = (r * wide + 2 + c) * sizings
            field[to : to + sizings, :] = either(row_odd, two, one)
            to = ((rows + 2 + r) * wide + 2 + c) * sizings
            field[to : to + sizings, :] = either(row_odd, one, two)
    for k in range(rows + 2):
        pair = 2 * sizings
        one, two = [ref[k * pair : (k + 1) * pair, :] for ref in (col_first, col_second)]
        to = (k + 1) * wide * sizings
        field[to : to + pair, :] = either(col_odd, two, one)
        to = to + (cols + 2) * sizings
        field[to : to + pair, :] = either(col_odd, one, two)
    field[many * sizings :, :] = jnp.zeros((sizings, nodes), F32)
    level[many * sizings :, :] = jnp.zeros((sizings, nodes), F32)
    q[many * sizings :, :] = jnp.zeros((sizings, nodes), F32)
    spread(solved, info[0], keys, level, count, sizings, nodes, many)

    def store_z(kind, places, out):
        sums = row_sums[pl.ds(kind, 1), :]
        for j, place in enumerate(places):
            here = level[place, :]
            z[place, :] = out[j * sizings : (j + 1) * sizings, :nodes] + here
            bz[place, :] = out[j * sizings : (j + 1) * sizings, nodes:] + sums * here

    sorted_products(plan, 0, field, stacked, low, sizings, store_z)

    north, east_strap = strap[0:1, :], strap[1:2, :]
    couple = 2.0 * north + 2.0 * east_strap

    def operator(v, bv, er, ec, row=None):
        row = row or [v[at(er, ec + j), :] for j in (-1, 0, 1)]
        image = (
            bv[at(er, ec), :]
            + couple * row[1]
            - north * (v[at(er - 1, ec), :] + v[at(er + 1, ec), :])
            - east_strap * (row[0] + row[2])
        )
        return row[1], image

    for er, flag in ((1, info[1]), (rows + 2, info[2])):
        inside = flag.astype(F32)

        def across(ec, carry):
            q[at(er, ec), :] = operator(z, bz, er, ec)[1] * inside
            return carry

        lax.fori_loop(2, cols + 2, across, 0)
    for ec, flag in ((1, info[3]), (cols + 2, info[4])):
        inside = flag.astype(F32)

        def along(er, carry):
            q[at(er, ec), :] = operator(z, bz, er, ec)[1] * inside
            return carry

        lax.fori_loop(2, rows + 2, along, 0)

    lanes = iota((sizings, max(count, 128)), 1)
    blank = jnp.zeros((sizings, nodes), F32)
    zero_sums = jnp.zeros(lanes.shape, F32)

    def first_row(r, carry):
        rz, zq, sums = carry
        line = [z[at(r + 2, 1), :], z[at(r + 2, 2), :]]
        for c in range(cols):
            line.append(z[at(r + 2, c + 3), :])
            here, image = operator(z, bz, r + 2, c + 2, line[c : c + 3])
            q[at(r + 2, c + 2), :] = image
            b = r * cols + c
            own = pl.ds(pl.multiple_of(b * sizings, sizings), sizings)
            z_out[own, :] = here
            q_out[own, :] = image
            rz = rz + blocks[own, :] * here
            zq = zq + here * image
            total = jnp.sum(image, axis=1, keepdims=True)
            sums = sums + jnp.where(lanes == ids[r, c], total, 0.0)
        return rz, zq, sums

    rz, zq, sums_q = lax.fori_loop(0, rows, first_row, (blank, blank, zero_sums))

    def store_u(kind, places, out):
        for j, place in enumerate(places):
            u[place, :] = out[j * sizings : (j + 1) * sizings, :nodes]
            bu[place, :] = out[j * sizings : (j + 1) * sizings, nodes:]

    sorted_products(plan, 1, q, stacked, low, sizings, store_u)

    def second_row(r, carry):
        qu, uau, sums = carry
        line = [u[at(r + 2, 1), :], u[at(r + 2, 2), :]]
        for c in range(cols):
            line.append(u[at(r + 2, c + 3), :])
            here, image = operator(u, bu, r + 2, c + 2, line[c : c + 3])
            b = r * cols + c
            own = pl.ds(pl.multiple_of(b * sizings, sizings), sizings)
            u_out[own, :] = here
            au_out[own, :] = image
            qu = qu + q[at(r + 2, c + 2), :] * here
            uau = uau + here * image
            total = jnp.sum(image, axis=1, keepdims=True)
            sums = sums + jnp.where(lanes == ids[r, c], total, 0.0)
        return qu, uau, sums

    qu, uau, sums_u = lax.fori_loop(0, rows, second_row, (blank, blank, zero_sums))

    lane = iota((sizings, 128), 1)
    dots = jnp.zeros((sizings, 128), F32)
    for j, one in enumerate((rz, zq, qu, uau)):
        dots = jnp.where(lane % 4 == j, jnp.sum(one, axis=1, keepdims=True), dots)
    dots = jnp.where(lane // 4 == iota((sizings, 128), 0), dots, 0.0)
    dots = jnp.sum(dots, axis=0, keepdims=True)
    whole = jnp.concatenate([pack(sums_q, count), pack(sums_u, count), dots], axis=0)

    send_all(pay, whole)


def last_kernel(
    dims, mesh_dims,
    types, info,
    gathered, keys, inverses, cross, z, q, u, au, blocks, row_sums, strap,
    voltage, residual,
    level, solved,
):
    sizings, rows, cols, nodes, count = dims
    n_row, n_col = mesh_dims
    wide = cols + 4
    many = (rows + 4) * wide
    height = sizings * count // 128
    mesh_args = (mesh_dims, count, sizings)

    solved[0] = jnp.zeros((sizings, count), F32)
    solved[n_col + 1] = jnp.zeros((sizings, count), F32)
    with_q = jnp.zeros((sizings, count), F32)
    with_u = jnp.zeros((sizings, count), F32)
    crossed = jnp.zeros((sizings, count), F32)
    before = None
    for g in range(n_col):
        sums, one = coarse_solve(gathered, 0, height, *mesh_args, inverses, g)
        solved[g + 1] = one
        image = total_of(gathered, height, height, mesh_dims, g)
        with_q = with_q + sums * one
        with_u = with_u + unpack(image, count, sizings) * one
        if before is not None:
            crossed = crossed + one * jnp.dot(
                before, cross[g - 1], precision=HIGHEST, preferred_element_type=F32
            )
        before = one
    spread(solved, info[0], keys, level, count, sizings, nodes, many)

    dots = gathered[0, 2 * height]
    for d in range(1, n_row * n_col):
        dots = dots + gathered[d, 2 * height]
    lane = iota((sizings, 128), 1)
    dots = jnp.where(lane // 4 == iota((sizings, 128), 0), dots, 0.0)
    rz, zq, qu, uau = [
        jnp.sum(jnp.where(lane % 4 == j, dots, 0.0), axis=1, keepdims=True) for j in range(4)
    ]
    east_weight = jnp.sum(strap[1:2, :], axis=1, keepdims=True)
    total = functools.partial(jnp.sum, axis=1, keepdims=True)
    qw = qu + total(with_q)
    wp = uau + 2.0 * total(with_u) + total(with_q) - 2.0 * east_weight * total(crossed)
    step_1 = rz / zq
    fresh = step_1 * step_1 * qw - rz
    grown = 1.0 + fresh / rz
    step_2 = fresh / (grown * grown * zq - 2.0 * grown * step_1 * qw + step_1 * step_1 * wp)
    alpha = jnp.broadcast_to(step_1 + step_2 * grown, (sizings, nodes))
    gamma = jnp.broadcast_to(-step_2 * step_1, (sizings, nodes))

    north, east_strap = strap[0:1, :], strap[1:2, :]
    couple = 2.0 * north + 2.0 * east_strap

    def step(r, carry):
        for c in range(cols):
            b = r * cols + c
            own = pl.ds(pl.multiple_of(b * sizings, sizings), sizings)

            def value(dr, dc):
                e = (r + 2 + dr) * wide + c + 2 + dc
                return level[pl.ds(pl.multiple_of(e * sizings, sizings), sizings), :]

            here = value(0, 0)
            lift = (
                (row_sums[pl.ds(types[r, c], 1), :] + couple) * here
                - north * (value(-1, 0) + value(1, 0))
                - east_strap * (value(0, -1) + value(0, 1))
            )
            voltage[pl.ds(b, sizings, stride=rows * cols), :] = alpha * z[own, :] + gamma * (
                u[own, :] + here
            )
            residual[pl.ds(b, sizings, stride=rows * cols), :] = (
                blocks[own, :] - alpha * q[own, :] - gamma * (au[own, :] + lift)
            )
        return carry

    lax.fori_loop(0, rows, step, 0)


def ring_maps(rows, cols, count):
    tall, wide = rows + 4, cols + 4
    length = -(-tall * wide // 128) * 128
    maps = np.zeros((8, length), np.int32)
    maps[0] = -1
    for er in range(tall):
        for ec in range(wide):
            e = er * wide + ec
            down = max(2 - er, er - (rows + 1), 0)
            over = max(2 - ec, ec - (cols + 1), 0)
            maps[1, e] = down + over <= 2
            maps[2, e] = down + over <= 1
            maps[3, e] = count * ((ec >= 2) + (ec >= cols + 2))
            device = 3 * ((er >= 2) + (er >= rows + 2)) + (ec >= 2) + (ec >= cols + 2)
            maps[0, e] = (device * rows + (er - 2) % rows) * cols + (ec - 2) % cols
    return maps


def call(kernel, in_specs, out_shape, scratch, cost, megabytes, **more):
    return pl.pallas_call(
        kernel,
        in_specs=in_specs,
        out_specs=jax.tree.map(lambda _: VMEM, out_shape),
        out_shape=out_shape,
        scratch_shapes=scratch,
        compiler_params=pltpu.CompilerParams(vmem_limit_bytes=megabytes * 1024 * 1024),
        cost_estimate=pl.CostEstimate(flops=cost, bytes_accessed=4_000_000, transcendentals=0),
        **more,
    )


def swap(payload, axis, begin):
    pairs = [(i, i + 1) for i in range(begin, lax.axis_size(axis) - 1, 2)]
    return lax.ppermute(payload, axis, pairs + [(j, i) for i, j in pairs])


def on_device(load_currents, block_library, strap_conductance, block_types, aggregate_map):
    sizings, rows, cols, nodes = load_currents.shape
    kinds = block_library.shape[0]
    n_row, n_col = lax.axis_size("row"), lax.axis_size("col")
    n_dev = n_row * n_col
    row, col = lax.axis_index("row"), lax.axis_index("col")
    count = rows * n_row // AGR * (cols // AGC)
    dims, mesh_dims = (sizings, rows, cols, nodes, count), (n_row, n_col)
    block_rows = rows * cols * sizings
    many = (rows + 4) * (cols + 4)
    height = sizings * count // 128
    shape = jax.ShapeDtypeStruct
    own = shape((block_rows, nodes), F32)

    info = jnp.stack(
        [
            col,
            (row > 0).astype(jnp.int32),
            (row < n_row - 1).astype(jnp.int32),
            (col > 0).astype(jnp.int32),
            (col < n_col - 1).astype(jnp.int32),
            row % 2,
            col % 2,
            row,
        ]
    )
    begin = (rows - 2) * (1 - row % 2)
    first = lax.dynamic_slice_in_dim(load_currents, begin, 2, axis=1)
    second = lax.dynamic_slice_in_dim(load_currents, rows - 2 - begin, 2, axis=1)
    row_first = swap(first.reshape(-1, nodes), "row", 0)
    row_second = swap(second.reshape(-1, nodes), "row", 1)

    pay_rows = height + 2
    flat_load = load_currents.reshape(-1, nodes)
    (pay,) = call(
        functools.partial(sums_kernel, dims),
        [SMEM] + [VMEM] * 3,
        [shape((n_dev, pay_rows, 1, 128), F32)],
        [],
        20_000_000_000,
        4 if count <= 64 else 16,
    )(aggregate_map, block_types, aggregate_map, flat_load)
    gathered = lax.all_to_all(pay, ("row", "col"), 0, 0)
    stacked, low, row_sums = call(
        weights_kernel,
        [VMEM, VMEM],
        [
            shape((kinds, 2 * nodes, 2 * nodes), BF16),
            shape((kinds, nodes, 2 * nodes), BF16),
            shape((kinds, nodes), F32),
        ],
        [],
        1_000_000,
        8,
    )(block_library, strap_conductance)
    (blocks,) = call(
        functools.partial(blocks_kernel, dims), [VMEM], [own], [], 1_000_000, 4
    )(flat_load)
    side_rows = (rows + 2) * 2 * sizings
    side = shape((side_rows, nodes), F32)
    first, second = call(
        functools.partial(sides_kernel, dims),
        [SMEM] + [VMEM] * 4,
        [side, side],
        [],
        40_000_000_000,
        4,
    )(info, blocks, row_first, row_second, row_sums)
    col_first, col_second = swap(first, "col", 0), swap(second, "col", 1)

    big = pltpu.VMEM(((many + 1) * sizings, nodes), F32)
    coarse_shape = (n_col + 2, sizings, count)
    maps = ring_maps(rows, cols, count)
    longest = int(max(maps[1].sum(), maps[2].sum())) + (TILE - 1) * kinds + GROUP * TILE
    longest = -(-longest // 128) * 128
    inverses, cross, solved, plan, keys = call(
        functools.partial(coarse_kernel, dims, mesh_dims, kinds),
        [SMEM] + [VMEM] * 4,
        [
            shape((count, n_col * count), F32),
            shape((n_col, count, count), F32),
            shape(coarse_shape, F32),
            shape((8, longest), jnp.int32),
            shape((1, maps.shape[1]), jnp.int32),
        ],
        [],
        10_000_000_000,
        8 if count <= 64 else 48,
    )(info, jnp.asarray(maps), gathered, row_sums, strap_conductance)
    z, q, u, au, pay = call(
        functools.partial(middle_kernel, dims),
        [SMEM] * 3 + [VMEM] * 11,
        [own] * 4 + [shape((n_dev, 2 * height + 1, 1, 128), F32)],
        [big] * 7,
        1_000_000_000,
        20 if count <= 64 else 48,
    )(
        plan, info, aggregate_map,
        solved, keys, blocks, row_first, row_second, col_first, col_second,
        stacked, low, row_sums, strap_conductance,
    )
    gathered = lax.all_to_all(pay, ("row", "col"), 0, 0)
    out = shape((sizings * rows * cols, nodes), F32)
    voltage, residual = call(
        functools.partial(last_kernel, dims, mesh_dims),
        [SMEM] * 2 + [VMEM] * 11,
        [out, out],
        [big, pltpu.VMEM(coarse_shape, F32)],
        1_000_000_000,
        8 if count <= 64 else 32,
    )(
        block_types, info,
        gathered, keys, inverses, cross, z, q, u, au, blocks, row_sums, strap_conductance,
    )
    return voltage.reshape(load_currents.shape), residual.reshape(load_currents.shape)


def solution(mesh):
    placed = (P(None, "row", "col", None), P(), P(), P("row", "col"), P("row", "col"))
    return jax.shard_map(
        on_device,
        mesh=mesh,
        in_specs=placed,
        out_specs=(P(None, "row", "col", None), P(None, "row", "col", None)),
        check_vma=False,
    )
```

```python
import functools

import jax
import jax.numpy as jnp
from jax import lax
from jax.experimental import pallas as pl
from jax.experimental.pallas import tpu as pltpu
from jax.sharding import PartitionSpec as P
import numpy as np

AGR = 4
AGC = 4
TILE = 8
GROUP = 8
PANEL = 8
F32 = jnp.float32
BF16 = jnp.bfloat16
HIGHEST = lax.Precision.HIGHEST
VMEM = pl.BlockSpec(memory_space=pltpu.VMEM)
SMEM = pl.BlockSpec(memory_space=pltpu.SMEM)


def iota(shape, dim):
    return lax.broadcasted_iota(jnp.int32, shape, dim)


def pack(values, count):
    if count < 128:
        fold = 128 // count
        height = values.shape[0] // fold
        return jnp.concatenate(
            [values[p * height : (p + 1) * height, :count] for p in range(fold)], axis=1
        )
    return jnp.concatenate([values[:, j : j + 128] for j in range(0, count, 128)], axis=0)


def unpack(rows, count, sizings):
    if count < 128:
        return jnp.concatenate(
            [rows[:, j : j + count] for j in range(0, 128, count)], axis=0
        )
    return jnp.concatenate(
        [rows[j : j + sizings] for j in range(0, rows.shape[0], sizings)], axis=1
    )


def split3(values):
    first = values.astype(BF16)
    rest = values - first.astype(F32)
    second = rest.astype(BF16)
    third = (rest - second.astype(F32)).astype(BF16)
    return first, second, third


def flat_row(table, many):
    rows, cols = table.shape
    repeat = (iota((cols, many), 1) % cols == iota((cols, many), 0)).astype(F32).astype(BF16)
    wide = jnp.dot(table.astype(F32).astype(BF16), repeat, preferred_element_type=F32)
    own = iota((rows, many), 1) // cols == iota((rows, many), 0)
    return jnp.sum(jnp.where(own, wide, 0.0), axis=0, keepdims=True)


def meta_rows(types, ids, many, height):
    rows = [flat_row(types[...], many), flat_row(ids[...], many) + 1.0]
    spare = [jnp.zeros((height - 2, many), F32)] if height > 2 else []
    return jnp.concatenate(rows + spare, axis=0)


def either(odd, if_even, if_odd):
    return jnp.where(odd == 1, if_odd, if_even)


def sums_kernel(dims, ids_smem, types, ids, load, pay):
    sizings, rows, cols, nodes, count = dims
    many = rows * cols
    width = max(count, 128)
    lane, side = iota((cols, width), 1), iota((cols, width), 0)
    hots = []
    for r in range(rows):
        names = jnp.zeros((cols, width), jnp.int32)
        for c in range(cols):
            names = jnp.where(side == c, ids_smem[r, c], names)
        hots.append((names == lane).astype(F32))
    sums = []
    for s in range(sizings):
        total = jnp.zeros((cols, width), F32)
        for r in range(rows):
            at = s * many + r * cols
            total = total + hots[r] * jnp.sum(load[at : at + cols, :], axis=1, keepdims=True)
        sums.append(jnp.sum(total, axis=0, keepdims=True))
    height = sizings * count // 128
    meta = meta_rows(types, ids, many, pay.shape[1] - height)
    whole = jnp.concatenate([pack(jnp.concatenate(sums, axis=0), count), meta], axis=0)
    send_all(pay, whole)


def send_all(pay, whole):
    rows = whole.reshape(pay.shape[1:])

    def copy(d, carry):
        pay[d] = rows
        return carry

    lax.fori_loop(0, pay.shape[0], copy, 0, unroll=4)


def blocks_kernel(dims, load, blocks):
    sizings, rows, cols, nodes, count = dims
    many = rows * cols

    def step(r, carry):
        for c in range(cols):
            b = r * cols + c
            at = pl.ds(pl.multiple_of(b * sizings, sizings), sizings)
            blocks[at, :] = load[pl.ds(b, sizings, stride=many), :]
        return carry

    lax.fori_loop(0, rows, step, 0)


def weights_kernel(library, strap, stacked, low, row_sums):
    kinds, nodes, _ = library.shape
    eye = iota((nodes, nodes), 0) == iota((nodes, nodes), 1)
    couple_row = 2.0 * strap[0:1, :] + 2.0 * strap[1:2, :]
    couple_col = jnp.sum(jnp.where(eye, couple_row, 0.0), axis=1, keepdims=True)

    def step(t, carry):
        block = library[t]
        on = jnp.where(eye, block, 0.0)
        inv_row = 1.0 / (jnp.sum(on, axis=0, keepdims=True) + couple_row)
        inv_col = 1.0 / (jnp.sum(on, axis=1, keepdims=True) + couple_col)
        off = jnp.where(eye, 0.0, -block)
        once = inv_col * off * inv_row
        twice = jnp.dot(once, off, precision=HIGHEST, preferred_element_type=F32) * inv_row
        smoother = jnp.where(eye, inv_row, 0.0) + once + twice
        product = jnp.dot(smoother, block, precision=HIGHEST, preferred_element_type=F32)
        both = jnp.concatenate([smoother, product], axis=1)
        high = both.astype(BF16)
        stacked[t] = jnp.concatenate([high, high], axis=0)
        low[t] = (both - high.astype(F32)).astype(BF16)
        row_sums[pl.ds(t, 1), :] = jnp.sum(block, axis=0, keepdims=True)
        return carry

    lax.fori_loop(0, kinds, step, 0, unroll=True)


def sides_kernel(dims, info, blocks, row_first, row_second, row_sums, first, second):
    sizings, rows, cols, nodes, count = dims
    row_odd, odd = info[5], info[6]
    for out, begin in ((first, either(odd, cols - 2, 0)), (second, either(odd, 0, cols - 2))):
        for side in range(2):
            c = begin + side
            above = pl.ds(cols + c, sizings, stride=2 * cols)
            below = pl.ds(c, sizings, stride=2 * cols)
            to = side * sizings
            out[to : to + sizings, :] = either(row_odd, row_second[above, :], row_first[above, :])
            to = ((rows + 1) * 2 + side) * sizings
            out[to : to + sizings, :] = either(row_odd, row_first[below, :], row_second[below, :])
            for r in range(rows):
                at = pl.multiple_of((r * cols + c) * sizings, sizings)
                to = ((r + 1) * 2 + side) * sizings
                out[to : to + sizings, :] = blocks[pl.ds(at, sizings), :]


def order_blocks(dims, mesh_dims, kinds, info, maps, gathered, plan, keys):
    sizings, rows, cols, nodes, count = dims
    n_row, n_col = mesh_dims
    height = sizings * count // 128
    metas = []
    for down in (-1, 0, 1):
        for right in (-1, 0, 1):
            r, c = info[7] + down, info[0] + right
            inside = (r >= 0) & (r < n_row) & (c >= 0) & (c < n_col)
            device = jnp.clip(r, 0, n_row - 1) * n_col + jnp.clip(c, 0, n_col - 1)
            meta = gathered[device, height : height + 2].reshape(2, 128)
            metas.append(meta * inside.astype(F32))
    metas = jnp.concatenate(metas, axis=1)
    shape = (metas.shape[1], maps.shape[1])
    pick = (iota(shape, 0) == maps[0:1, :]).astype(F32).astype(BF16)
    near = jnp.dot(metas.astype(BF16), pick, preferred_element_type=F32)
    near_types, near_ids = near[0:1, :], near[1:2, :]
    keys[...] = jnp.where(
        near_ids > 0.0, near_ids - 1.0 + maps[3:4, :].astype(F32), -1.0
    ).astype(jnp.int32)

    length = maps.shape[1]
    total = (rows + 4) * (cols + 4)
    before = (iota((length, length), 0) < iota((length, length), 1)).astype(F32).astype(BF16)
    upto = (iota((kinds, kinds), 0) >= iota((kinds, kinds), 1)).astype(F32).astype(BF16)
    slot = iota((plan.shape[1], length), 0).astype(F32)
    slot_row = iota((kinds, plan.shape[1]), 1).astype(F32)
    side = iota((8, length), 0)
    index = jnp.where(side == 0, iota((8, length), 1), jnp.where(side == 1, 1, 0))
    index = index.astype(F32).astype(BF16)
    orders, tile_kinds, groups = [], [], []
    for which in (1, 2):
        needed = maps[which : which + 1, :] > 0
        hot = (iota((kinds, length), 0).astype(F32) == near_types) & needed
        hot = hot.astype(F32)
        rank = jnp.dot(hot.astype(BF16), before, preferred_element_type=F32)
        tiles = jnp.floor((jnp.sum(hot, axis=1, keepdims=True) + (TILE - 1)) * (1.0 / TILE))
        tiles = jnp.broadcast_to(tiles, (kinds, 128))
        ends = jnp.dot(upto, tiles.astype(BF16), preferred_element_type=F32)
        starts = (ends - tiles)[:, :1]
        place = jnp.sum(hot * (starts * TILE + rank + 1.0), axis=0, keepdims=True) - 1.0
        hit = (slot == place).astype(F32).astype(BF16)
        found = lax.dot_general(
            index, hit, (((1,), (1,)), ((), ())), preferred_element_type=F32
        )
        orders.append(found[0:1, :] + float(total) * (1.0 - found[1:2, :]))
        kind = jnp.sum(jnp.where(slot_row >= ends[:, :1], 1.0, 0.0), axis=0, keepdims=True)
        tile_kinds.append(jnp.minimum(kind, kinds - 1.0))
        last = jnp.floor((ends[kinds - 1 : kinds, :1] + (GROUP - 1)) * (1.0 / GROUP))
        groups.append(jnp.broadcast_to(last, (1, plan.shape[1])))
    rest = jnp.zeros((2, plan.shape[1]), F32)
    whole = jnp.concatenate(orders + tile_kinds + groups + [rest], axis=0)
    plan[...] = whole.astype(jnp.int32)


def sorted_products(plan, which, source, stacked, low, sizings, store):
    def step(it, carry):
        for one in range(GROUP):
            tile = it * GROUP + one
            kind = plan[2 + which, tile]
            places = [
                pl.ds(pl.multiple_of(plan[which, tile * TILE + j] * sizings, sizings), sizings)
                for j in range(TILE)
            ]
            field = jnp.concatenate([source[place, :] for place in places], axis=0)
            high = field.astype(BF16)
            rest = (field - high.astype(F32)).astype(BF16)
            out = jnp.dot(
                jnp.concatenate([high, rest], axis=1), stacked[kind], preferred_element_type=F32
            ) + jnp.dot(high, low[kind], preferred_element_type=F32)
            store(kind, places, out)
        return carry

    lax.fori_loop(0, plan[4 + which, 0], step, 0)


def neighbour_ids(ids, cols):
    height, many = ids.shape
    lane, row = iota(ids.shape, 1), iota(ids.shape, 0)
    down = pltpu.roll(ids, many - cols, 1)
    south = jnp.where(lane < many - cols, down, pltpu.roll(down, height - 1, 0))
    south = jnp.where((lane >= many - cols) & (row == height - 1), -1.0, south)
    up = pltpu.roll(ids, cols, 1)
    north = jnp.where(lane >= cols, up, pltpu.roll(up, 1, 0))
    north = jnp.where((lane < cols) & (row == 0), -1.0, north)
    east = jnp.where(lane % cols == cols - 1, -1.0, pltpu.roll(ids, many - 1, 1))
    west = jnp.where(lane % cols == 0, -1.0, pltpu.roll(ids, 1, 1))
    return south, north, east, west


def invert_unrolled(ref, count):
    width = ref.shape[1]
    fold = 128 // count
    lane = iota((8, width), 1) % count
    row = iota((8, width), 0)
    tile_lane = iota((8, 128), 1)
    many = count // 8
    tiles = [ref[i * 8 : (i + 1) * 8, :] for i in range(many)]

    def column(tile, k):
        parts = []
        for base in range(0, width, 128):
            part = jnp.broadcast_to(tile[:, base + k : base + k + 1], (8, 128))
            for j in range(1, fold):
                at = base + j * count + k
                part = jnp.where(tile_lane >= j * count, tile[:, at : at + 1], part)
            parts.append(part)
        return jnp.concatenate(parts, axis=1)

    for first in range(0, count, PANEL):
        columns = [[column(t, first + j) for t in tiles] for j in range(PANEL)]
        for j in range(PANEL):
            k = first + j
            at, within = k // 8, k % 8
            here = columns[j]
            pivots = here[at][within : within + 1, :]
            inverse = pl.reciprocal(pivots, approx=True)
            inverse = inverse * (2.0 - pivots * inverse)
            inverse = inverse * (2.0 - pivots * inverse)
            scaled = jnp.where(
                lane[:1] == k, inverse, tiles[at][within : within + 1, :] * inverse
            )
            pivot = row == within
            for i in range(many):
                new = jnp.where(lane == k, 0.0, tiles[i]) - here[i] * scaled
                tiles[i] = jnp.where(pivot, scaled, new) if i == at else new
            for later in range(j + 1, PANEL):
                other = columns[later]
                factor = other[at][within : within + 1, :] * inverse
                for i in range(many):
                    new = other[i] - here[i] * factor
                    other[i] = jnp.where(pivot, factor, new) if i == at else new
    for i in range(many):
        ref[i * 8 : (i + 1) * 8, :] = tiles[i]


def invert_looped(ref, count):
    def step(k, carry):
        for base in range(0, ref.shape[1], count):
            here = slice(base, base + count)
            lane = iota((1, count), 1)
            row = iota((count, 1), 0)
            pivot_row = ref[pl.ds(k, 1), here]
            part = ref[:, here]
            column = jnp.sum(jnp.where(lane == k, part, 0.0), axis=1, keepdims=True)
            inverse = 1.0 / jnp.sum(jnp.where(lane == k, pivot_row, 0.0), axis=1, keepdims=True)
            scaled = jnp.where(lane == k, 1.0, pivot_row) * inverse
            column = jnp.where(row == k, -1.0, column)
            ref[:, here] = jnp.where((lane == k) | (row == k), 0.0, part) - column * scaled
        return carry

    lax.fori_loop(0, count, step, 0)


def coarse_matrices(dims, mesh_dims, gathered, row_sums, strap, inverses, cross):
    sizings, rows, cols, nodes, count = dims
    n_row, n_col = mesh_dims
    many = rows * cols
    height = sizings * count // 128
    kinds = row_sums.shape[0]
    north_weight = jnp.sum(strap[0:1, :], axis=1, keepdims=True)
    east_weight = jnp.sum(strap[1:2, :], axis=1, keepdims=True)
    names = iota((count, many), 0).astype(F32).astype(BF16)
    kind_names = iota((16, many), 0).astype(F32).astype(BF16)
    lane = iota((n_row, many), 1)
    eye = iota((count, count), 0) == iota((count, count), 1)
    contract = (((1,), (1,)), ((), ()))
    spot = iota((kinds, 16), 0) == iota((kinds, 16), 1)
    centre = jnp.sum(row_sums[...], axis=1, keepdims=True) + 2.0 * north_weight
    centre = centre + 2.0 * east_weight
    centre = jnp.sum(jnp.where(spot, centre, 0.0), axis=0, keepdims=True)

    def rows_of(g, at):
        return jnp.concatenate(
            [gathered[i * n_col + g, at : at + 1, 0, :] for i in range(n_row)], axis=0
        )

    def hot(values, labels):
        rows_bf = values.astype(BF16)
        one, zero = jnp.ones(labels.shape, BF16), jnp.zeros(labels.shape, BF16)
        return [
            jnp.where(labels == rows_bf[i : i + 1, :], one, zero) for i in range(n_row)
        ]

    all_ids = [rows_of(g, height + 1) - 1.0 for g in range(n_col)]
    for g in range(n_col):
        ids = all_ids[g]
        beyond = all_ids[min(g + 1, n_col - 1)]
        beyond = jnp.where(lane % cols == cols - 1, pltpu.roll(beyond, cols - 1, 1), -1.0)
        south, north, east, west = [hot(v, names) for v in neighbour_ids(ids, cols)]
        own, over = hot(ids, names), hot(beyond, names)
        types = hot(rows_of(g, height), kind_names)
        right = jnp.concatenate(
            [
                jnp.concatenate([south[i] + north[i], east[i] + west[i], over[i], types[i]], axis=0)
                for i in range(n_row)
            ],
            axis=1,
        )
        pairs = lax.dot_general(
            jnp.concatenate(own, axis=1), right, contract, preferred_element_type=F32
        )
        diagonal = jnp.sum(pairs[:, 3 * count :] * centre, axis=1, keepdims=True)
        inverses[:, g * count : (g + 1) * count] = jnp.where(eye, diagonal, 0.0) - (
            north_weight * pairs[:, :count] + east_weight * pairs[:, count : 2 * count]
        )
        cross[g] = pairs[:, 2 * count : 3 * count]


def total_of(gathered, first, height, mesh_dims, g):
    n_row, n_col = mesh_dims
    total = gathered[g, first : first + height]
    for i in range(1, n_row):
        total = total + gathered[i * n_col + g, first : first + height]
    return total.reshape(height, 128)


def coarse_solve(gathered, first, height, mesh_dims, count, sizings, inverses, g):
    sums = unpack(total_of(gathered, first, height, mesh_dims, g), count, sizings)
    solved = jnp.dot(
        sums, inverses[:, g * count : (g + 1) * count], precision=HIGHEST,
        preferred_element_type=F32,
    )
    return sums, solved


def spread(solved, col, keys, out, count, sizings, nodes, many):
    three = jnp.concatenate([solved[col], solved[col + 1], solved[col + 2]], axis=1)
    hot = (iota((3 * count, keys.shape[1]), 0) == keys[...]).astype(F32).astype(BF16)
    parts = jnp.concatenate(split3(three), axis=0)
    values = jnp.dot(parts, hot, preferred_element_type=F32)
    values = (
        values[2 * sizings : 3 * sizings] + values[sizings : 2 * sizings] + values[:sizings]
    )
    for e in range(many):
        out[e * sizings : (e + 1) * sizings, :] = jnp.broadcast_to(
            values[:, e : e + 1], (sizings, nodes)
        )


def coarse_kernel(
    dims, mesh_dims, kinds, info, maps, gathered, row_sums, strap,
    inverses, cross, solved, plan, keys,
):
    sizings, rows, cols, nodes, count = dims
    n_col = mesh_dims[1]
    height = sizings * count // 128
    order_blocks(dims, mesh_dims, kinds, info, maps, gathered, plan, keys)
    coarse_matrices(dims, mesh_dims, gathered, row_sums, strap, inverses, cross)
    if count <= 64:
        invert_unrolled(inverses, count)
    else:
        invert_looped(inverses, count)
    solved[0] = jnp.zeros((sizings, count), F32)
    solved[n_col + 1] = jnp.zeros((sizings, count), F32)
    for g in range(n_col):
        _, solved[g + 1] = coarse_solve(
            gathered, 0, height, mesh_dims, count, sizings, inverses, g
        )


def middle_kernel(
    dims,
    plan, info, ids,
    solved, keys, blocks, row_first, row_second, col_first, col_second,
    stacked, low, row_sums, strap,
    z_out, q_out, u_out, au_out, pay,
    field, level, z, bz, q, u, bu,
):
    sizings, rows, cols, nodes, count = dims
    wide = cols + 4
    many = (rows + 4) * wide

    def at(er, ec):
        return pl.ds(pl.multiple_of((er * wide + ec) * sizings, sizings), sizings)

    row_odd, col_odd = info[5], info[6]
    span = cols * sizings
    for r in range(rows):
        to = ((r + 2) * wide + 2) * sizings
        field[to : to + span, :] = blocks[r * span : (r + 1) * span, :]
    for r in range(2):
        for c in range(cols):
            edge = pl.ds(r * cols + c, sizings, stride=2 * cols)
            one, two = row_first[edge, :], row_second[edge, :]
            to = (r * wide + 2 + c) * sizings
            field[to : to + sizings, :] = either(row_odd, two, one)
            to = ((rows + 2 + r) * wide + 2 + c) * sizings
            field[to : to + sizings, :] = either(row_odd, one, two)
    for k in range(rows + 2):
        pair = 2 * sizings
        one, two = [ref[k * pair : (k + 1) * pair, :] for ref in (col_first, col_second)]
        to = (k + 1) * wide * sizings
        field[to : to + pair, :] = either(col_odd, two, one)
        to = to + (cols + 2) * sizings
        field[to : to + pair, :] = either(col_odd, one, two)
    field[many * sizings :, :] = jnp.zeros((sizings, nodes), F32)
    level[many * sizings :, :] = jnp.zeros((sizings, nodes), F32)
    q[many * sizings :, :] = jnp.zeros((sizings, nodes), F32)
    spread(solved, info[0], keys, level, count, sizings, nodes, many)

    def store_z(kind, places, out):
        sums = row_sums[pl.ds(kind, 1), :]
        for j, place in enumerate(places):
            here = level[place, :]
            z[place, :] = out[j * sizings : (j + 1) * sizings, :nodes] + here
            bz[place, :] = out[j * sizings : (j + 1) * sizings, nodes:] + sums * here

    sorted_products(plan, 0, field, stacked, low, sizings, store_z)

    north, east_strap = strap[0:1, :], strap[1:2, :]
    couple = 2.0 * north + 2.0 * east_strap

    def operator(v, bv, er, ec, row=None):
        row = row or [v[at(er, ec + j), :] for j in (-1, 0, 1)]
        image = (
            bv[at(er, ec), :]
            + couple * row[1]
            - north * (v[at(er - 1, ec), :] + v[at(er + 1, ec), :])
            - east_strap * (row[0] + row[2])
        )
        return row[1], image

    for er, flag in ((1, info[1]), (rows + 2, info[2])):
        inside = flag.astype(F32)

        def across(ec, carry):
            q[at(er, ec), :] = operator(z, bz, er, ec)[1] * inside
            return carry

        lax.fori_loop(2, cols + 2, across, 0)
    for ec, flag in ((1, info[3]), (cols + 2, info[4])):
        inside = flag.astype(F32)

        def along(er, carry):
            q[at(er, ec), :] = operator(z, bz, er, ec)[1] * inside
            return carry

        lax.fori_loop(2, rows + 2, along, 0)

    lanes = iota((sizings, max(count, 128)), 1)
    blank = jnp.zeros((sizings, nodes), F32)
    zero_sums = jnp.zeros(lanes.shape, F32)

    def first_row(r, carry):
        rz, zq, sums = carry
        line = [z[at(r + 2, 1), :], z[at(r + 2, 2), :]]
        for c in range(cols):
            line.append(z[at(r + 2, c + 3), :])
            here, image = operator(z, bz, r + 2, c + 2, line[c : c + 3])
            q[at(r + 2, c + 2), :] = image
            b = r * cols + c
            own = pl.ds(pl.multiple_of(b * sizings, sizings), sizings)
            z_out[own, :] = here
            q_out[own, :] = image
            rz = rz + blocks[own, :] * here
            zq = zq + here * image
            total = jnp.sum(image, axis=1, keepdims=True)
            sums = sums + jnp.where(lanes == ids[r, c], total, 0.0)
        return rz, zq, sums

    rz, zq, sums_q = lax.fori_loop(0, rows, first_row, (blank, blank, zero_sums))

    def store_u(kind, places, out):
        for j, place in enumerate(places):
            u[place, :] = out[j * sizings : (j + 1) * sizings, :nodes]
            bu[place, :] = out[j * sizings : (j + 1) * sizings, nodes:]

    sorted_products(plan, 1, q, stacked, low, sizings, store_u)

    def second_row(r, carry):
        qu, uau, sums = carry
        line = [u[at(r + 2, 1), :], u[at(r + 2, 2), :]]
        for c in range(cols):
            line.append(u[at(r + 2, c + 3), :])
            here, image = operator(u, bu, r + 2, c + 2, line[c : c + 3])
            b = r * cols + c
            own = pl.ds(pl.multiple_of(b * sizings, sizings), sizings)
            u_out[own, :] = here
            au_out[own, :] = image
            qu = qu + q[at(r + 2, c + 2), :] * here
            uau = uau + here * image
            total = jnp.sum(image, axis=1, keepdims=True)
            sums = sums + jnp.where(lanes == ids[r, c], total, 0.0)
        return qu, uau, sums

    qu, uau, sums_u = lax.fori_loop(0, rows, second_row, (blank, blank, zero_sums))

    lane = iota((sizings, 128), 1)
    dots = jnp.zeros((sizings, 128), F32)
    for j, one in enumerate((rz, zq, qu, uau)):
        dots = jnp.where(lane % 4 == j, jnp.sum(one, axis=1, keepdims=True), dots)
    dots = jnp.where(lane // 4 == iota((sizings, 128), 0), dots, 0.0)
    dots = jnp.sum(dots, axis=0, keepdims=True)
    whole = jnp.concatenate([pack(sums_q, count), pack(sums_u, count), dots], axis=0)

    send_all(pay, whole)


def last_kernel(
    dims, mesh_dims,
    types, info,
    gathered, keys, inverses, cross, z, q, u, au, blocks, row_sums, strap,
    voltage, residual,
    level, solved, voltage_rows, residual_rows, sems,
):
    sizings, rows, cols, nodes, count = dims
    n_row, n_col = mesh_dims
    wide = cols + 4
    many = (rows + 4) * wide
    height = sizings * count // 128
    mesh_args = (mesh_dims, count, sizings)

    solved[0] = jnp.zeros((sizings, count), F32)
    solved[n_col + 1] = jnp.zeros((sizings, count), F32)
    with_q = jnp.zeros((sizings, count), F32)
    with_u = jnp.zeros((sizings, count), F32)
    crossed = jnp.zeros((sizings, count), F32)
    before = None
    for g in range(n_col):
        sums, one = coarse_solve(gathered, 0, height, *mesh_args, inverses, g)
        solved[g + 1] = one
        image = total_of(gathered, height, height, mesh_dims, g)
        with_q = with_q + sums * one
        with_u = with_u + unpack(image, count, sizings) * one
        if before is not None:
            crossed = crossed + one * jnp.dot(
                before, cross[g - 1], precision=HIGHEST, preferred_element_type=F32
            )
        before = one
    spread(solved, info[0], keys, level, count, sizings, nodes, many)

    dots = gathered[0, 2 * height]
    for d in range(1, n_row * n_col):
        dots = dots + gathered[d, 2 * height]
    lane = iota((sizings, 128), 1)
    dots = jnp.where(lane // 4 == iota((sizings, 128), 0), dots, 0.0)
    rz, zq, qu, uau = [
        jnp.sum(jnp.where(lane % 4 == j, dots, 0.0), axis=1, keepdims=True) for j in range(4)
    ]
    east_weight = jnp.sum(strap[1:2, :], axis=1, keepdims=True)
    total = functools.partial(jnp.sum, axis=1, keepdims=True)
    qw = qu + total(with_q)
    wp = uau + 2.0 * total(with_u) + total(with_q) - 2.0 * east_weight * total(crossed)
    step_1 = rz / zq
    fresh = step_1 * step_1 * qw - rz
    grown = 1.0 + fresh / rz
    step_2 = fresh / (grown * grown * zq - 2.0 * grown * step_1 * qw + step_1 * step_1 * wp)
    alpha = jnp.broadcast_to(step_1 + step_2 * grown, (sizings, nodes))
    gamma = jnp.broadcast_to(-step_2 * step_1, (sizings, nodes))

    north, east_strap = strap[0:1, :], strap[1:2, :]
    couple = 2.0 * north + 2.0 * east_strap

    span = sizings * cols
    flat_voltage = voltage_rows.reshape(rows * span, nodes)
    flat_residual = residual_rows.reshape(rows * span, nodes)

    def value(er, ec):
        at = (er * wide + ec) * sizings
        return level[pl.ds(pl.multiple_of(at, sizings), sizings), :]

    def copies(r):
        return [
            pltpu.make_async_copy(buffer.at[r], out.at[:, r], sems.at[i, r])
            for i, (buffer, out) in enumerate(((voltage_rows, voltage), (residual_rows, residual)))
        ]

    def step(r, carry):
        line = [value(r + 2, 1), value(r + 2, 2)]
        for c in range(cols):
            line.append(value(r + 2, c + 3))
            here = line[c + 1]
            own = pl.ds(pl.multiple_of((r * cols + c) * sizings, sizings), sizings)
            lift = (
                (row_sums[pl.ds(types[r, c], 1), :] + couple) * here
                - north * (value(r + 1, c + 2) + value(r + 3, c + 2))
                - east_strap * (line[c] + line[c + 2])
            )
            to = pl.ds(r * span + c, sizings, stride=cols)
            flat_voltage[to, :] = alpha * z[own, :] + gamma * (u[own, :] + here)
            flat_residual[to, :] = (
                blocks[own, :] - alpha * q[own, :] - gamma * (au[own, :] + lift)
            )
        for copy in copies(r):
            copy.start()
        return carry

    lax.fori_loop(0, rows, step, 0)
    for r in range(rows):
        for copy in copies(r):
            copy.wait()


def ring_maps(rows, cols, count):
    tall, wide = rows + 4, cols + 4
    length = -(-tall * wide // 128) * 128
    maps = np.zeros((8, length), np.int32)
    maps[0] = -1
    for er in range(tall):
        for ec in range(wide):
            e = er * wide + ec
            down = max(2 - er, er - (rows + 1), 0)
            over = max(2 - ec, ec - (cols + 1), 0)
            maps[1, e] = down + over <= 2
            maps[2, e] = down + over <= 1
            maps[3, e] = count * ((ec >= 2) + (ec >= cols + 2))
            device = 3 * ((er >= 2) + (er >= rows + 2)) + (ec >= 2) + (ec >= cols + 2)
            maps[0, e] = (device * rows + (er - 2) % rows) * cols + (ec - 2) % cols
    return maps


def call(kernel, in_specs, out_shape, scratch, cost, megabytes, **more):
    return pl.pallas_call(
        kernel,
        in_specs=in_specs,
        out_specs=more.pop("out_specs", [VMEM] * len(out_shape)),
        out_shape=out_shape,
        scratch_shapes=scratch,
        compiler_params=pltpu.CompilerParams(vmem_limit_bytes=megabytes * 1024 * 1024),
        cost_estimate=pl.CostEstimate(flops=cost, bytes_accessed=4_000_000, transcendentals=0),
        **more,
    )


def swap(payload, axis, begin):
    pairs = [(i, i + 1) for i in range(begin, lax.axis_size(axis) - 1, 2)]
    return lax.ppermute(payload, axis, pairs + [(j, i) for i, j in pairs])


def on_device(load_currents, block_library, strap_conductance, block_types, aggregate_map):
    sizings, rows, cols, nodes = load_currents.shape
    kinds = block_library.shape[0]
    n_row, n_col = lax.axis_size("row"), lax.axis_size("col")
    n_dev = n_row * n_col
    row, col = lax.axis_index("row"), lax.axis_index("col")
    count = rows * n_row // AGR * (cols // AGC)
    dims, mesh_dims = (sizings, rows, cols, nodes, count), (n_row, n_col)
    block_rows = rows * cols * sizings
    many = (rows + 4) * (cols + 4)
    height = sizings * count // 128
    shape = jax.ShapeDtypeStruct
    own = shape((block_rows, nodes), F32)

    info = jnp.stack(
        [
            col,
            (row > 0).astype(jnp.int32),
            (row < n_row - 1).astype(jnp.int32),
            (col > 0).astype(jnp.int32),
            (col < n_col - 1).astype(jnp.int32),
            row % 2,
            col % 2,
            row,
        ]
    )
    begin = (rows - 2) * (1 - row % 2)
    first = lax.dynamic_slice_in_dim(load_currents, begin, 2, axis=1)
    second = lax.dynamic_slice_in_dim(load_currents, rows - 2 - begin, 2, axis=1)
    row_first = swap(first.reshape(-1, nodes), "row", 0)
    row_second = swap(second.reshape(-1, nodes), "row", 1)

    pay_rows = height + 2
    flat_load = load_currents.reshape(-1, nodes)
    (pay,) = call(
        functools.partial(sums_kernel, dims),
        [SMEM] + [VMEM] * 3,
        [shape((n_dev, pay_rows, 1, 128), F32)],
        [],
        20_000_000_000,
        4 if count <= 64 else 16,
    )(aggregate_map, block_types, aggregate_map, flat_load)
    gathered = lax.all_to_all(pay, ("row", "col"), 0, 0)
    stacked, low, row_sums = call(
        weights_kernel,
        [VMEM, VMEM],
        [
            shape((kinds, 2 * nodes, 2 * nodes), BF16),
            shape((kinds, nodes, 2 * nodes), BF16),
            shape((kinds, nodes), F32),
        ],
        [],
        1_000_000,
        8,
    )(block_library, strap_conductance)
    (blocks,) = call(
        functools.partial(blocks_kernel, dims), [VMEM], [own], [], 1_000_000, 4
    )(flat_load)
    side_rows = (rows + 2) * 2 * sizings
    side = shape((side_rows, nodes), F32)
    first, second = call(
        functools.partial(sides_kernel, dims),
        [SMEM] + [VMEM] * 4,
        [side, side],
        [],
        40_000_000_000,
        4,
    )(info, blocks, row_first, row_second, row_sums)
    col_first, col_second = swap(first, "col", 0), swap(second, "col", 1)

    big = pltpu.VMEM(((many + 1) * sizings, nodes), F32)
    coarse_shape = (n_col + 2, sizings, count)
    maps = ring_maps(rows, cols, count)
    longest = int(max(maps[1].sum(), maps[2].sum())) + (TILE - 1) * kinds + GROUP * TILE
    longest = -(-longest // 128) * 128
    inverses, cross, solved, plan, keys = call(
        functools.partial(coarse_kernel, dims, mesh_dims, kinds),
        [SMEM] + [VMEM] * 4,
        [
            shape((count, n_col * count), F32),
            shape((n_col, count, count), F32),
            shape(coarse_shape, F32),
            shape((8, longest), jnp.int32),
            shape((1, maps.shape[1]), jnp.int32),
        ],
        [],
        10_000_000_000,
        8 if count <= 64 else 48,
    )(info, jnp.asarray(maps), gathered, row_sums, strap_conductance)
    z, q, u, au, pay = call(
        functools.partial(middle_kernel, dims),
        [SMEM] * 3 + [VMEM] * 11,
        [own] * 4 + [shape((n_dev, 2 * height + 1, 1, 128), F32)],
        [big] * 7,
        1_000_000_000,
        20 if count <= 64 else 48,
    )(
        plan, info, aggregate_map,
        solved, keys, blocks, row_first, row_second, col_first, col_second,
        stacked, low, row_sums, strap_conductance,
    )
    gathered = lax.all_to_all(pay, ("row", "col"), 0, 0)
    out = shape(load_currents.shape, F32)
    row_buffer = pltpu.VMEM((rows, sizings, cols, nodes), F32)
    return call(
        functools.partial(last_kernel, dims, mesh_dims),
        [SMEM] * 2 + [VMEM] * 11,
        [out, out],
        [big, pltpu.VMEM(coarse_shape, F32), row_buffer, row_buffer]
        + [pltpu.SemaphoreType.DMA((2, rows))],
        1_000_000_000,
        8 if count <= 64 else 32,
        out_specs=[pl.BlockSpec(memory_space=pl.ANY)] * 2,
    )(
        block_types, info,
        gathered, keys, inverses, cross, z, q, u, au, blocks, row_sums, strap_conductance,
    )


def solution(mesh):
    placed = (P(None, "row", "col", None), P(), P(), P("row", "col"), P("row", "col"))
    return jax.shard_map(
        on_device,
        mesh=mesh,
        in_specs=placed,
        out_specs=(P(None, "row", "col", None), P(None, "row", "col", None)),
        check_vma=False,
    )
```

```python
import functools

import jax
import jax.numpy as jnp
from jax import lax
from jax.experimental import pallas as pl
from jax.experimental.pallas import tpu as pltpu
from jax.sharding import PartitionSpec as P
import numpy as np

AGR = 4
AGC = 4
TILE = 8
GROUP = 8
PANEL = 8
F32 = jnp.float32
BF16 = jnp.bfloat16
HIGHEST = lax.Precision.HIGHEST
VMEM = pl.BlockSpec(memory_space=pltpu.VMEM)
SMEM = pl.BlockSpec(memory_space=pltpu.SMEM)


def iota(shape, dim):
    return lax.broadcasted_iota(jnp.int32, shape, dim)


def pack(values, count):
    if count < 128:
        fold = 128 // count
        height = values.shape[0] // fold
        return jnp.concatenate(
            [values[p * height : (p + 1) * height, :count] for p in range(fold)], axis=1
        )
    return jnp.concatenate([values[:, j : j + 128] for j in range(0, count, 128)], axis=0)


def unpack(rows, count, sizings):
    if count < 128:
        return jnp.concatenate(
            [rows[:, j : j + count] for j in range(0, 128, count)], axis=0
        )
    return jnp.concatenate(
        [rows[j : j + sizings] for j in range(0, rows.shape[0], sizings)], axis=1
    )


def split3(values):
    first = values.astype(BF16)
    rest = values - first.astype(F32)
    second = rest.astype(BF16)
    third = (rest - second.astype(F32)).astype(BF16)
    return first, second, third


def flat_row(table, many):
    rows, cols = table.shape
    repeat = (iota((cols, many), 1) % cols == iota((cols, many), 0)).astype(F32).astype(BF16)
    wide = jnp.dot(table.astype(F32).astype(BF16), repeat, preferred_element_type=F32)
    own = iota((rows, many), 1) // cols == iota((rows, many), 0)
    return jnp.sum(jnp.where(own, wide, 0.0), axis=0, keepdims=True)


def meta_rows(types, ids, many, height):
    rows = [flat_row(types[...], many), flat_row(ids[...], many) + 1.0]
    spare = [jnp.zeros((height - 2, many), F32)] if height > 2 else []
    return jnp.concatenate(rows + spare, axis=0)


def either(odd, if_even, if_odd):
    return jnp.where(odd == 1, if_odd, if_even)


def sums_kernel(dims, ids_smem, types, ids, load, pay):
    sizings, rows, cols, nodes, count = dims
    many = rows * cols
    width = max(count, 128)
    lane, side = iota((cols, width), 1), iota((cols, width), 0)
    hots = []
    for r in range(rows):
        names = jnp.zeros((cols, width), jnp.int32)
        for c in range(cols):
            names = jnp.where(side == c, ids_smem[r, c], names)
        hots.append((names == lane).astype(F32))
    sums = []
    for s in range(sizings):
        total = jnp.zeros((cols, width), F32)
        for r in range(rows):
            at = s * many + r * cols
            total = total + hots[r] * jnp.sum(load[at : at + cols, :], axis=1, keepdims=True)
        sums.append(jnp.sum(total, axis=0, keepdims=True))
    height = sizings * count // 128
    meta = meta_rows(types, ids, many, pay.shape[1] - height)
    whole = jnp.concatenate([pack(jnp.concatenate(sums, axis=0), count), meta], axis=0)
    send_all(pay, whole)


def send_all(pay, whole):
    rows = whole.reshape(pay.shape[1:])

    def copy(d, carry):
        pay[d] = rows
        return carry

    lax.fori_loop(0, pay.shape[0], copy, 0, unroll=4)


def blocks_kernel(dims, load, blocks):
    sizings, rows, cols, nodes, count = dims
    many = rows * cols

    def step(r, carry):
        for c in range(cols):
            b = r * cols + c
            at = pl.ds(pl.multiple_of(b * sizings, sizings), sizings)
            blocks[at, :] = load[pl.ds(b, sizings, stride=many), :]
        return carry

    lax.fori_loop(0, rows, step, 0)


def weights_kernel(library, strap, stacked, low, row_sums):
    kinds, nodes, _ = library.shape
    eye = iota((nodes, nodes), 0) == iota((nodes, nodes), 1)
    couple_row = 2.0 * strap[0:1, :] + 2.0 * strap[1:2, :]
    couple_col = jnp.sum(jnp.where(eye, couple_row, 0.0), axis=1, keepdims=True)

    def step(t, carry):
        block = library[t]
        on = jnp.where(eye, block, 0.0)
        inv_row = 1.0 / (jnp.sum(on, axis=0, keepdims=True) + couple_row)
        inv_col = 1.0 / (jnp.sum(on, axis=1, keepdims=True) + couple_col)
        off = jnp.where(eye, 0.0, -block)
        once = inv_col * off * inv_row
        twice = jnp.dot(once, off, precision=HIGHEST, preferred_element_type=F32) * inv_row
        smoother = jnp.where(eye, inv_row, 0.0) + once + twice
        product = jnp.dot(smoother, block, precision=HIGHEST, preferred_element_type=F32)
        both = jnp.concatenate([smoother, product], axis=1)
        high = both.astype(BF16)
        stacked[t] = jnp.concatenate([high, high], axis=0)
        low[t] = (both - high.astype(F32)).astype(BF16)
        row_sums[pl.ds(t, 1), :] = jnp.sum(block, axis=0, keepdims=True)
        return carry

    lax.fori_loop(0, kinds, step, 0, unroll=True)


def sides_kernel(dims, info, blocks, row_first, row_second, row_sums, first, second):
    sizings, rows, cols, nodes, count = dims
    row_odd, odd = info[5], info[6]
    for out, begin in ((first, either(odd, cols - 2, 0)), (second, either(odd, 0, cols - 2))):
        for side in range(2):
            c = begin + side
            above = pl.ds(cols + c, sizings, stride=2 * cols)
            below = pl.ds(c, sizings, stride=2 * cols)
            to = side * sizings
            out[to : to + sizings, :] = either(row_odd, row_second[above, :], row_first[above, :])
            to = ((rows + 1) * 2 + side) * sizings
            out[to : to + sizings, :] = either(row_odd, row_first[below, :], row_second[below, :])
            for r in range(rows):
                at = pl.multiple_of((r * cols + c) * sizings, sizings)
                to = ((r + 1) * 2 + side) * sizings
                out[to : to + sizings, :] = blocks[pl.ds(at, sizings), :]


def order_blocks(dims, mesh_dims, kinds, info, maps, gathered, plan, keys):
    sizings, rows, cols, nodes, count = dims
    n_row, n_col = mesh_dims
    height = sizings * count // 128
    metas = []
    for down in (-1, 0, 1):
        for right in (-1, 0, 1):
            r, c = info[7] + down, info[0] + right
            inside = (r >= 0) & (r < n_row) & (c >= 0) & (c < n_col)
            device = jnp.clip(r, 0, n_row - 1) * n_col + jnp.clip(c, 0, n_col - 1)
            meta = gathered[device, height : height + 2].reshape(2, 128)
            metas.append(meta * inside.astype(F32))
    metas = jnp.concatenate(metas, axis=1)
    shape = (metas.shape[1], maps.shape[1])
    pick = (iota(shape, 0) == maps[0:1, :]).astype(F32).astype(BF16)
    near = jnp.dot(metas.astype(BF16), pick, preferred_element_type=F32)
    near_types, near_ids = near[0:1, :], near[1:2, :]
    keys[...] = jnp.where(
        near_ids > 0.0, near_ids - 1.0 + maps[3:4, :].astype(F32), -1.0
    ).astype(jnp.int32)

    length = maps.shape[1]
    total = (rows + 4) * (cols + 4)
    before = (iota((length, length), 0) < iota((length, length), 1)).astype(F32).astype(BF16)
    upto = (iota((kinds, kinds), 0) >= iota((kinds, kinds), 1)).astype(F32).astype(BF16)
    slot = iota((plan.shape[1], length), 0).astype(F32)
    slot_row = iota((kinds, plan.shape[1]), 1).astype(F32)
    side = iota((8, length), 0)
    index = jnp.where(side == 0, iota((8, length), 1), jnp.where(side == 1, 1, 0))
    index = index.astype(F32).astype(BF16)
    orders, tile_kinds, groups = [], [], []
    for which in (1, 2):
        needed = maps[which : which + 1, :] > 0
        hot = (iota((kinds, length), 0).astype(F32) == near_types) & needed
        hot = hot.astype(F32)
        rank = jnp.dot(hot.astype(BF16), before, preferred_element_type=F32)
        tiles = jnp.floor((jnp.sum(hot, axis=1, keepdims=True) + (TILE - 1)) * (1.0 / TILE))
        tiles = jnp.broadcast_to(tiles, (kinds, 128))
        ends = jnp.dot(upto, tiles.astype(BF16), preferred_element_type=F32)
        starts = (ends - tiles)[:, :1]
        place = jnp.sum(hot * (starts * TILE + rank + 1.0), axis=0, keepdims=True) - 1.0
        hit = (slot == place).astype(F32).astype(BF16)
        found = lax.dot_general(
            index, hit, (((1,), (1,)), ((), ())), preferred_element_type=F32
        )
        orders.append(found[0:1, :] + float(total) * (1.0 - found[1:2, :]))
        kind = jnp.sum(jnp.where(slot_row >= ends[:, :1], 1.0, 0.0), axis=0, keepdims=True)
        tile_kinds.append(jnp.minimum(kind, kinds - 1.0))
        last = jnp.floor((ends[kinds - 1 : kinds, :1] + (GROUP - 1)) * (1.0 / GROUP))
        groups.append(jnp.broadcast_to(last, (1, plan.shape[1])))
    rest = jnp.zeros((2, plan.shape[1]), F32)
    whole = jnp.concatenate(orders + tile_kinds + groups + [rest], axis=0)
    plan[...] = whole.astype(jnp.int32)


def sorted_products(plan, which, source, stacked, low, sizings, store):
    def step(it, carry):
        for one in range(GROUP):
            tile = it * GROUP + one
            kind = plan[2 + which, tile]
            places = [
                pl.ds(pl.multiple_of(plan[which, tile * TILE + j] * sizings, sizings), sizings)
                for j in range(TILE)
            ]
            field = jnp.concatenate([source[place, :] for place in places], axis=0)
            high = field.astype(BF16)
            rest = (field - high.astype(F32)).astype(BF16)
            out = jnp.dot(
                jnp.concatenate([high, rest], axis=1), stacked[kind], preferred_element_type=F32
            ) + jnp.dot(high, low[kind], preferred_element_type=F32)
            store(kind, places, out)
        return carry

    lax.fori_loop(0, plan[4 + which, 0], step, 0)


def neighbour_ids(ids, cols):
    height, many = ids.shape
    lane, row = iota(ids.shape, 1), iota(ids.shape, 0)
    down = pltpu.roll(ids, many - cols, 1)
    south = jnp.where(lane < many - cols, down, pltpu.roll(down, height - 1, 0))
    south = jnp.where((lane >= many - cols) & (row == height - 1), -1.0, south)
    up = pltpu.roll(ids, cols, 1)
    north = jnp.where(lane >= cols, up, pltpu.roll(up, 1, 0))
    north = jnp.where((lane < cols) & (row == 0), -1.0, north)
    east = jnp.where(lane % cols == cols - 1, -1.0, pltpu.roll(ids, many - 1, 1))
    west = jnp.where(lane % cols == 0, -1.0, pltpu.roll(ids, 1, 1))
    return south, north, east, west


def invert_unrolled(ref, count):
    width = ref.shape[1]
    fold = 128 // count
    lane = iota((8, width), 1) % count
    row = iota((8, width), 0)
    tile_lane = iota((8, 128), 1)
    many = count // 8
    tiles = [ref[i * 8 : (i + 1) * 8, :] for i in range(many)]

    def column(tile, k):
        place = tile_lane // count * count + k
        return jnp.concatenate(
            [
                jnp.take_along_axis(tile[:, base : base + 128], place, axis=1)
                for base in range(0, width, 128)
            ],
            axis=1,
        )

    for first in range(0, count, PANEL):
        columns = [[column(t, first + j) for t in tiles] for j in range(PANEL)]
        for j in range(0, PANEL, 2):
            k = first + j
            at, one, two = k // 8, slice(k % 8, k % 8 + 1), slice(k % 8 + 1, k % 8 + 2)
            left, right = columns[j], columns[j + 1]
            a, b, c, d = left[at][one], right[at][one], left[at][two], right[at][two]
            det = a * d - b * c
            scale = pl.reciprocal(det, approx=True)
            scale = scale * (2.0 - det * scale)
            scale = scale * (2.0 - det * scale)
            a, b, c, d = a * scale, b * scale, c * scale, d * scale

            def pivoted(upper, lower):
                return d * upper - b * lower, a * lower - c * upper

            def update(old, i, upper, lower):
                new = old - left[i] * upper - right[i] * lower
                if i == at:
                    new = jnp.where(row == k % 8, upper, new)
                    new = jnp.where(row == k % 8 + 1, lower, new)
                return new

            upper, lower = tiles[at][one], tiles[at][two]
            on, after = lane[:1] == k, lane[:1] == k + 1
            upper, lower = pivoted(
                jnp.where(on, 1.0, jnp.where(after, 0.0, upper)),
                jnp.where(on, 0.0, jnp.where(after, 1.0, lower)),
            )
            cleared = (lane == k) | (lane == k + 1)
            for i in range(many):
                tiles[i] = update(jnp.where(cleared, 0.0, tiles[i]), i, upper, lower)
            for other in columns[j + 2 :]:
                upper, lower = pivoted(other[at][one], other[at][two])
                for i in range(many):
                    other[i] = update(other[i], i, upper, lower)
    for i in range(many):
        ref[i * 8 : (i + 1) * 8, :] = tiles[i]


def invert_looped(ref, count):
    def step(k, carry):
        for base in range(0, ref.shape[1], count):
            here = slice(base, base + count)
            lane = iota((1, count), 1)
            row = iota((count, 1), 0)
            pivot_row = ref[pl.ds(k, 1), here]
            part = ref[:, here]
            column = jnp.sum(jnp.where(lane == k, part, 0.0), axis=1, keepdims=True)
            inverse = 1.0 / jnp.sum(jnp.where(lane == k, pivot_row, 0.0), axis=1, keepdims=True)
            scaled = jnp.where(lane == k, 1.0, pivot_row) * inverse
            column = jnp.where(row == k, -1.0, column)
            ref[:, here] = jnp.where((lane == k) | (row == k), 0.0, part) - column * scaled
        return carry

    lax.fori_loop(0, count, step, 0)


def coarse_matrices(dims, mesh_dims, gathered, row_sums, strap, inverses, cross):
    sizings, rows, cols, nodes, count = dims
    n_row, n_col = mesh_dims
    many = rows * cols
    height = sizings * count // 128
    kinds = row_sums.shape[0]
    north_weight = jnp.sum(strap[0:1, :], axis=1, keepdims=True)
    east_weight = jnp.sum(strap[1:2, :], axis=1, keepdims=True)
    names = iota((count, many), 0).astype(F32).astype(BF16)
    kind_names = iota((16, many), 0).astype(F32).astype(BF16)
    lane = iota((n_row, many), 1)
    eye = iota((count, count), 0) == iota((count, count), 1)
    contract = (((1,), (1,)), ((), ()))
    spot = iota((kinds, 16), 0) == iota((kinds, 16), 1)
    centre = jnp.sum(row_sums[...], axis=1, keepdims=True) + 2.0 * north_weight
    centre = centre + 2.0 * east_weight
    centre = jnp.sum(jnp.where(spot, centre, 0.0), axis=0, keepdims=True)

    def rows_of(g, at):
        return jnp.concatenate(
            [gathered[i * n_col + g, at : at + 1, 0, :] for i in range(n_row)], axis=0
        )

    def hot(values, labels):
        rows_bf = values.astype(BF16)
        one, zero = jnp.ones(labels.shape, BF16), jnp.zeros(labels.shape, BF16)
        return [
            jnp.where(labels == rows_bf[i : i + 1, :], one, zero) for i in range(n_row)
        ]

    all_ids = [rows_of(g, height + 1) - 1.0 for g in range(n_col)]
    for g in range(n_col):
        ids = all_ids[g]
        beyond = all_ids[min(g + 1, n_col - 1)]
        beyond = jnp.where(lane % cols == cols - 1, pltpu.roll(beyond, cols - 1, 1), -1.0)
        south, north, east, west = [hot(v, names) for v in neighbour_ids(ids, cols)]
        own, over = hot(ids, names), hot(beyond, names)
        types = hot(rows_of(g, height), kind_names)
        right = jnp.concatenate(
            [
                jnp.concatenate([south[i] + north[i], east[i] + west[i], over[i], types[i]], axis=0)
                for i in range(n_row)
            ],
            axis=1,
        )
        pairs = lax.dot_general(
            jnp.concatenate(own, axis=1), right, contract, preferred_element_type=F32
        )
        diagonal = jnp.sum(pairs[:, 3 * count :] * centre, axis=1, keepdims=True)
        inverses[:, g * count : (g + 1) * count] = jnp.where(eye, diagonal, 0.0) - (
            north_weight * pairs[:, :count] + east_weight * pairs[:, count : 2 * count]
        )
        cross[g] = pairs[:, 2 * count : 3 * count]


def total_of(gathered, first, height, mesh_dims, g):
    n_row, n_col = mesh_dims
    total = gathered[g, first : first + height]
    for i in range(1, n_row):
        total = total + gathered[i * n_col + g, first : first + height]
    return total.reshape(height, 128)


def coarse_solve(gathered, first, height, mesh_dims, count, sizings, inverses, g):
    sums = unpack(total_of(gathered, first, height, mesh_dims, g), count, sizings)
    solved = jnp.dot(
        sums, inverses[:, g * count : (g + 1) * count], precision=HIGHEST,
        preferred_element_type=F32,
    )
    return sums, solved


def spread(solved, info, keys, ids, out, table, dims, reach):
    sizings, rows, cols, nodes, count = dims
    wide = cols + 4
    col = info[0]
    own = solved[col + 1]
    for a in range(count):
        table[a * sizings : (a + 1) * sizings, :] = jnp.broadcast_to(
            own[:, a : a + 1], (sizings, nodes)
        )
    table[count * sizings :, :] = jnp.zeros((sizings, nodes), F32)

    def row(er, carry):
        for ec in range(2, cols + 2):
            e = er * wide + ec
            key = ids[0, e]
            place = jnp.where(key < 0, count, key - count) * sizings
            to = pl.ds(pl.multiple_of(e * sizings, sizings), sizings)
            out[to, :] = table[pl.ds(pl.multiple_of(place, sizings), sizings), :]
        return carry

    lax.fori_loop(2 - reach, rows + 2 + reach, row, 0)

    three = jnp.concatenate([solved[col], own, solved[col + 2]], axis=1)
    hot = (iota((3 * count, keys.shape[1]), 0) == keys[...]).astype(F32).astype(BF16)
    parts = jnp.concatenate(split3(three), axis=0)
    values = jnp.dot(parts, hot, preferred_element_type=F32)
    values = (
        values[2 * sizings : 3 * sizings] + values[sizings : 2 * sizings] + values[:sizings]
    )
    for over in range(1, reach + 1):
        for ec in (2 - over, cols + 1 + over):
            for er in range(2 - reach + over, rows + 2 + reach - over):
                e = er * wide + ec
                out[e * sizings : (e + 1) * sizings, :] = jnp.broadcast_to(
                    values[:, e : e + 1], (sizings, nodes)
                )


def coarse_kernel(
    dims, mesh_dims, kinds, info, maps, gathered, row_sums, strap,
    inverses, cross, solved, plan, keys,
):
    sizings, rows, cols, nodes, count = dims
    n_col = mesh_dims[1]
    height = sizings * count // 128
    order_blocks(dims, mesh_dims, kinds, info, maps, gathered, plan, keys)
    coarse_matrices(dims, mesh_dims, gathered, row_sums, strap, inverses, cross)
    if count <= 64:
        invert_unrolled(inverses, count)
    else:
        invert_looped(inverses, count)
    solved[0] = jnp.zeros((sizings, count), F32)
    solved[n_col + 1] = jnp.zeros((sizings, count), F32)
    for g in range(n_col):
        _, solved[g + 1] = coarse_solve(
            gathered, 0, height, mesh_dims, count, sizings, inverses, g
        )


def middle_kernel(
    dims,
    plan, info, ids, near_ids,
    solved, keys, blocks, row_first, row_second, col_first, col_second,
    stacked, low, row_sums, strap,
    z_out, q_out, u_out, au_out, pay,
    field, level, z, bz, q, u, bu, table,
):
    sizings, rows, cols, nodes, count = dims
    wide = cols + 4
    many = (rows + 4) * wide

    def at(er, ec):
        return pl.ds(pl.multiple_of((er * wide + ec) * sizings, sizings), sizings)

    row_odd, col_odd = info[5], info[6]
    span = cols * sizings
    for r in range(rows):
        to = ((r + 2) * wide + 2) * sizings
        field[to : to + span, :] = blocks[r * span : (r + 1) * span, :]
    for r in range(2):
        for c in range(cols):
            edge = pl.ds(r * cols + c, sizings, stride=2 * cols)
            one, two = row_first[edge, :], row_second[edge, :]
            to = (r * wide + 2 + c) * sizings
            field[to : to + sizings, :] = either(row_odd, two, one)
            to = ((rows + 2 + r) * wide + 2 + c) * sizings
            field[to : to + sizings, :] = either(row_odd, one, two)
    for k in range(rows + 2):
        pair = 2 * sizings
        one, two = [ref[k * pair : (k + 1) * pair, :] for ref in (col_first, col_second)]
        to = (k + 1) * wide * sizings
        field[to : to + pair, :] = either(col_odd, two, one)
        to = to + (cols + 2) * sizings
        field[to : to + pair, :] = either(col_odd, one, two)
    field[many * sizings :, :] = jnp.zeros((sizings, nodes), F32)
    level[many * sizings :, :] = jnp.zeros((sizings, nodes), F32)
    q[many * sizings :, :] = jnp.zeros((sizings, nodes), F32)
    spread(solved, info, keys, near_ids, level, table, dims, 2)

    def store_z(kind, places, out):
        sums = row_sums[pl.ds(kind, 1), :]
        for j, place in enumerate(places):
            here = level[place, :]
            z[place, :] = out[j * sizings : (j + 1) * sizings, :nodes] + here
            bz[place, :] = out[j * sizings : (j + 1) * sizings, nodes:] + sums * here

    sorted_products(plan, 0, field, stacked, low, sizings, store_z)

    north, east_strap = strap[0:1, :], strap[1:2, :]
    couple = 2.0 * north + 2.0 * east_strap

    def operator(v, bv, er, ec, row=None):
        row = row or [v[at(er, ec + j), :] for j in (-1, 0, 1)]
        image = (
            bv[at(er, ec), :]
            + couple * row[1]
            - north * (v[at(er - 1, ec), :] + v[at(er + 1, ec), :])
            - east_strap * (row[0] + row[2])
        )
        return row[1], image

    for er, flag in ((1, info[1]), (rows + 2, info[2])):
        inside = flag.astype(F32)

        def across(ec, carry):
            q[at(er, ec), :] = operator(z, bz, er, ec)[1] * inside
            return carry

        lax.fori_loop(2, cols + 2, across, 0)
    for ec, flag in ((1, info[3]), (cols + 2, info[4])):
        inside = flag.astype(F32)

        def along(er, carry):
            q[at(er, ec), :] = operator(z, bz, er, ec)[1] * inside
            return carry

        lax.fori_loop(2, rows + 2, along, 0)

    lanes = iota((sizings, max(count, 128)), 1)
    blank = jnp.zeros((sizings, nodes), F32)
    zero_sums = jnp.zeros(lanes.shape, F32)

    def first_row(r, carry):
        rz, zq, sums = carry
        line = [z[at(r + 2, 1), :], z[at(r + 2, 2), :]]
        for c in range(cols):
            line.append(z[at(r + 2, c + 3), :])
            here, image = operator(z, bz, r + 2, c + 2, line[c : c + 3])
            q[at(r + 2, c + 2), :] = image
            b = r * cols + c
            own = pl.ds(pl.multiple_of(b * sizings, sizings), sizings)
            z_out[own, :] = here
            q_out[own, :] = image
            rz = rz + blocks[own, :] * here
            zq = zq + here * image
            total = jnp.sum(image, axis=1, keepdims=True)
            sums = sums + jnp.where(lanes == ids[r, c], total, 0.0)
        return rz, zq, sums

    rz, zq, sums_q = lax.fori_loop(0, rows, first_row, (blank, blank, zero_sums))

    def store_u(kind, places, out):
        for j, place in enumerate(places):
            u[place, :] = out[j * sizings : (j + 1) * sizings, :nodes]
            bu[place, :] = out[j * sizings : (j + 1) * sizings, nodes:]

    sorted_products(plan, 1, q, stacked, low, sizings, store_u)

    def second_row(r, carry):
        qu, uau, sums = carry
        line = [u[at(r + 2, 1), :], u[at(r + 2, 2), :]]
        for c in range(cols):
            line.append(u[at(r + 2, c + 3), :])
            here, image = operator(u, bu, r + 2, c + 2, line[c : c + 3])
            b = r * cols + c
            own = pl.ds(pl.multiple_of(b * sizings, sizings), sizings)
            u_out[own, :] = here
            au_out[own, :] = image
            qu = qu + q[at(r + 2, c + 2), :] * here
            uau = uau + here * image
            total = jnp.sum(image, axis=1, keepdims=True)
            sums = sums + jnp.where(lanes == ids[r, c], total, 0.0)
        return qu, uau, sums

    qu, uau, sums_u = lax.fori_loop(0, rows, second_row, (blank, blank, zero_sums))

    lane = iota((sizings, 128), 1)
    dots = jnp.zeros((sizings, 128), F32)
    for j, one in enumerate((rz, zq, qu, uau)):
        dots = jnp.where(lane % 4 == j, jnp.sum(one, axis=1, keepdims=True), dots)
    dots = jnp.where(lane // 4 == iota((sizings, 128), 0), dots, 0.0)
    dots = jnp.sum(dots, axis=0, keepdims=True)
    whole = jnp.concatenate([pack(sums_q, count), pack(sums_u, count), dots], axis=0)

    send_all(pay, whole)


def last_kernel(
    dims, mesh_dims,
    types, info, near_ids,
    gathered, keys, inverses, cross, z, q, u, au, blocks, row_sums, strap,
    voltage, residual,
    level, solved, table, voltage_rows, residual_rows, sems,
):
    sizings, rows, cols, nodes, count = dims
    n_row, n_col = mesh_dims
    wide = cols + 4
    many = (rows + 4) * wide
    height = sizings * count // 128
    mesh_args = (mesh_dims, count, sizings)

    solved[0] = jnp.zeros((sizings, count), F32)
    solved[n_col + 1] = jnp.zeros((sizings, count), F32)
    with_q = jnp.zeros((sizings, count), F32)
    with_u = jnp.zeros((sizings, count), F32)
    crossed = jnp.zeros((sizings, count), F32)
    before = None
    for g in range(n_col):
        sums, one = coarse_solve(gathered, 0, height, *mesh_args, inverses, g)
        solved[g + 1] = one
        image = total_of(gathered, height, height, mesh_dims, g)
        with_q = with_q + sums * one
        with_u = with_u + unpack(image, count, sizings) * one
        if before is not None:
            crossed = crossed + one * jnp.dot(
                before, cross[g - 1], precision=HIGHEST, preferred_element_type=F32
            )
        before = one
    spread(solved, info, keys, near_ids, level, table, dims, 1)

    dots = gathered[0, 2 * height]
    for d in range(1, n_row * n_col):
        dots = dots + gathered[d, 2 * height]
    lane = iota((sizings, 128), 1)
    dots = jnp.where(lane // 4 == iota((sizings, 128), 0), dots, 0.0)
    rz, zq, qu, uau = [
        jnp.sum(jnp.where(lane % 4 == j, dots, 0.0), axis=1, keepdims=True) for j in range(4)
    ]
    east_weight = jnp.sum(strap[1:2, :], axis=1, keepdims=True)
    total = functools.partial(jnp.sum, axis=1, keepdims=True)
    qw = qu + total(with_q)
    wp = uau + 2.0 * total(with_u) + total(with_q) - 2.0 * east_weight * total(crossed)
    step_1 = rz / zq
    fresh = step_1 * step_1 * qw - rz
    grown = 1.0 + fresh / rz
    step_2 = fresh / (grown * grown * zq - 2.0 * grown * step_1 * qw + step_1 * step_1 * wp)
    alpha = jnp.broadcast_to(step_1 + step_2 * grown, (sizings, nodes))
    gamma = jnp.broadcast_to(-step_2 * step_1, (sizings, nodes))

    north, east_strap = strap[0:1, :], strap[1:2, :]
    couple = 2.0 * north + 2.0 * east_strap

    span = sizings * cols
    flat_voltage = voltage_rows.reshape(rows * span, nodes)
    flat_residual = residual_rows.reshape(rows * span, nodes)

    def value(er, ec):
        at = (er * wide + ec) * sizings
        return level[pl.ds(pl.multiple_of(at, sizings), sizings), :]

    def copies(r):
        return [
            pltpu.make_async_copy(buffer.at[r], out.at[:, r], sems.at[i, r])
            for i, (buffer, out) in enumerate(((voltage_rows, voltage), (residual_rows, residual)))
        ]

    def step(r, carry):
        line = [value(r + 2, 1), value(r + 2, 2)]
        for c in range(cols):
            line.append(value(r + 2, c + 3))
            here = line[c + 1]
            own = pl.ds(pl.multiple_of((r * cols + c) * sizings, sizings), sizings)
            lift = (
                (row_sums[pl.ds(types[r, c], 1), :] + couple) * here
                - north * (value(r + 1, c + 2) + value(r + 3, c + 2))
                - east_strap * (line[c] + line[c + 2])
            )
            to = pl.ds(r * span + c, sizings, stride=cols)
            flat_voltage[to, :] = alpha * z[own, :] + gamma * (u[own, :] + here)
            flat_residual[to, :] = (
                blocks[own, :] - alpha * q[own, :] - gamma * (au[own, :] + lift)
            )
        for copy in copies(r):
            copy.start()
        return carry

    lax.fori_loop(0, rows, step, 0)
    for r in range(rows):
        for copy in copies(r):
            copy.wait()


def ring_maps(rows, cols, count):
    tall, wide = rows + 4, cols + 4
    length = -(-tall * wide // 128) * 128
    maps = np.zeros((8, length), np.int32)
    maps[0] = -1
    for er in range(tall):
        for ec in range(wide):
            e = er * wide + ec
            down = max(2 - er, er - (rows + 1), 0)
            over = max(2 - ec, ec - (cols + 1), 0)
            maps[1, e] = down + over <= 2
            maps[2, e] = down + over <= 1
            maps[3, e] = count * ((ec >= 2) + (ec >= cols + 2))
            device = 3 * ((er >= 2) + (er >= rows + 2)) + (ec >= 2) + (ec >= cols + 2)
            maps[0, e] = (device * rows + (er - 2) % rows) * cols + (ec - 2) % cols
    return maps


def call(kernel, in_specs, out_shape, scratch, cost, megabytes, **more):
    return pl.pallas_call(
        kernel,
        in_specs=in_specs,
        out_specs=more.pop("out_specs", [VMEM] * len(out_shape)),
        out_shape=out_shape,
        scratch_shapes=scratch,
        compiler_params=pltpu.CompilerParams(vmem_limit_bytes=megabytes * 1024 * 1024),
        cost_estimate=pl.CostEstimate(flops=cost, bytes_accessed=4_000_000, transcendentals=0),
        **more,
    )


def swap(payload, axis, begin):
    pairs = [(i, i + 1) for i in range(begin, lax.axis_size(axis) - 1, 2)]
    return lax.ppermute(payload, axis, pairs + [(j, i) for i, j in pairs])


def on_device(load_currents, block_library, strap_conductance, block_types, aggregate_map):
    sizings, rows, cols, nodes = load_currents.shape
    kinds = block_library.shape[0]
    n_row, n_col = lax.axis_size("row"), lax.axis_size("col")
    n_dev = n_row * n_col
    row, col = lax.axis_index("row"), lax.axis_index("col")
    count = rows * n_row // AGR * (cols // AGC)
    dims, mesh_dims = (sizings, rows, cols, nodes, count), (n_row, n_col)
    block_rows = rows * cols * sizings
    many = (rows + 4) * (cols + 4)
    height = sizings * count // 128
    shape = jax.ShapeDtypeStruct
    own = shape((block_rows, nodes), F32)

    info = jnp.stack(
        [
            col,
            (row > 0).astype(jnp.int32),
            (row < n_row - 1).astype(jnp.int32),
            (col > 0).astype(jnp.int32),
            (col < n_col - 1).astype(jnp.int32),
            row % 2,
            col % 2,
            row,
        ]
    )
    begin = (rows - 2) * (1 - row % 2)
    first = lax.dynamic_slice_in_dim(load_currents, begin, 2, axis=1)
    second = lax.dynamic_slice_in_dim(load_currents, rows - 2 - begin, 2, axis=1)
    row_first = swap(first.reshape(-1, nodes), "row", 0)
    row_second = swap(second.reshape(-1, nodes), "row", 1)

    pay_rows = height + 2
    flat_load = load_currents.reshape(-1, nodes)
    (pay,) = call(
        functools.partial(sums_kernel, dims),
        [SMEM] + [VMEM] * 3,
        [shape((n_dev, pay_rows, 1, 128), F32)],
        [],
        20_000_000_000,
        4 if count <= 64 else 16,
    )(aggregate_map, block_types, aggregate_map, flat_load)
    gathered = lax.all_to_all(pay, ("row", "col"), 0, 0)
    stacked, low, row_sums = call(
        weights_kernel,
        [VMEM, VMEM],
        [
            shape((kinds, 2 * nodes, 2 * nodes), BF16),
            shape((kinds, nodes, 2 * nodes), BF16),
            shape((kinds, nodes), F32),
        ],
        [],
        1_000_000,
        8,
    )(block_library, strap_conductance)
    (blocks,) = call(
        functools.partial(blocks_kernel, dims), [VMEM], [own], [], 1_000_000, 4
    )(flat_load)
    side_rows = (rows + 2) * 2 * sizings
    side = shape((side_rows, nodes), F32)
    first, second = call(
        functools.partial(sides_kernel, dims),
        [SMEM] + [VMEM] * 4,
        [side, side],
        [],
        40_000_000_000,
        4,
    )(info, blocks, row_first, row_second, row_sums)
    col_first, col_second = swap(first, "col", 0), swap(second, "col", 1)

    big = pltpu.VMEM(((many + 1) * sizings, nodes), F32)
    coarse_shape = (n_col + 2, sizings, count)
    table = pltpu.VMEM(((count + 1) * sizings, nodes), F32)
    maps = ring_maps(rows, cols, count)
    longest = int(max(maps[1].sum(), maps[2].sum())) + (TILE - 1) * kinds + GROUP * TILE
    longest = -(-longest // 128) * 128
    inverses, cross, solved, plan, keys = call(
        functools.partial(coarse_kernel, dims, mesh_dims, kinds),
        [SMEM] + [VMEM] * 4,
        [
            shape((count, n_col * count), F32),
            shape((n_col, count, count), F32),
            shape(coarse_shape, F32),
            shape((8, longest), jnp.int32),
            shape((1, maps.shape[1]), jnp.int32),
        ],
        [],
        10_000_000_000,
        8 if count <= 64 else 48,
    )(info, jnp.asarray(maps), gathered, row_sums, strap_conductance)
    z, q, u, au, pay = call(
        functools.partial(middle_kernel, dims),
        [SMEM] * 4 + [VMEM] * 11,
        [own] * 4 + [shape((n_dev, 2 * height + 1, 1, 128), F32)],
        [big] * 7 + [table],
        1_000_000_000,
        20 if count <= 64 else 48,
    )(
        plan, info, aggregate_map, keys,
        solved, keys, blocks, row_first, row_second, col_first, col_second,
        stacked, low, row_sums, strap_conductance,
    )
    gathered = lax.all_to_all(pay, ("row", "col"), 0, 0)
    out = shape(load_currents.shape, F32)
    row_buffer = pltpu.VMEM((rows, sizings, cols, nodes), F32)
    return call(
        functools.partial(last_kernel, dims, mesh_dims),
        [SMEM] * 3 + [VMEM] * 11,
        [out, out],
        [big, pltpu.VMEM(coarse_shape, F32), table, row_buffer, row_buffer]
        + [pltpu.SemaphoreType.DMA((2, rows))],
        1_000_000_000,
        8 if count <= 64 else 32,
        out_specs=[pl.BlockSpec(memory_space=pl.ANY)] * 2,
    )(
        block_types, info, keys,
        gathered, keys, inverses, cross, z, q, u, au, blocks, row_sums, strap_conductance,
    )


def solution(mesh):
    placed = (P(None, "row", "col", None), P(), P(), P("row", "col"), P("row", "col"))
    return jax.shard_map(
        on_device,
        mesh=mesh,
        in_specs=placed,
        out_specs=(P(None, "row", "col", None), P(None, "row", "col", None)),
        check_vma=False,
    )
```

```python
import functools

import jax
import jax.numpy as jnp
from jax import lax
from jax.experimental import pallas as pl
from jax.experimental.pallas import tpu as pltpu
from jax.sharding import PartitionSpec as P
import numpy as np

AGR = 4
AGC = 4
TILE = 8
GROUP = 8
PANEL = 8
F32 = jnp.float32
BF16 = jnp.bfloat16
HIGHEST = lax.Precision.HIGHEST
VMEM = pl.BlockSpec(memory_space=pltpu.VMEM)
SMEM = pl.BlockSpec(memory_space=pltpu.SMEM)


def iota(shape, dim):
    return lax.broadcasted_iota(jnp.int32, shape, dim)


def pack(values, count):
    if count < 128:
        fold = 128 // count
        height = values.shape[0] // fold
        return jnp.concatenate(
            [values[p * height : (p + 1) * height, :count] for p in range(fold)], axis=1
        )
    return jnp.concatenate([values[:, j : j + 128] for j in range(0, count, 128)], axis=0)


def unpack(rows, count, sizings):
    if count < 128:
        return jnp.concatenate(
            [rows[:, j : j + count] for j in range(0, 128, count)], axis=0
        )
    return jnp.concatenate(
        [rows[j : j + sizings] for j in range(0, rows.shape[0], sizings)], axis=1
    )


def split3(values):
    first = values.astype(BF16)
    rest = values - first.astype(F32)
    second = rest.astype(BF16)
    third = (rest - second.astype(F32)).astype(BF16)
    return first, second, third


def flat_row(table, many):
    rows, cols = table.shape
    repeat = (iota((cols, many), 1) % cols == iota((cols, many), 0)).astype(F32).astype(BF16)
    wide = jnp.dot(table.astype(F32).astype(BF16), repeat, preferred_element_type=F32)
    own = iota((rows, many), 1) // cols == iota((rows, many), 0)
    return jnp.sum(jnp.where(own, wide, 0.0), axis=0, keepdims=True)


def meta_rows(types, ids, many, height):
    rows = [flat_row(types[...], many), flat_row(ids[...], many) + 1.0]
    spare = [jnp.zeros((height - 2, many), F32)] if height > 2 else []
    return jnp.concatenate(rows + spare, axis=0)


def either(odd, if_even, if_odd):
    return jnp.where(odd == 1, if_odd, if_even)


def sums_kernel(dims, ids_smem, types, ids, load, pay):
    sizings, rows, cols, nodes, count = dims
    many = rows * cols
    width = max(count, 128)
    lane, side = iota((cols, width), 1), iota((cols, width), 0)
    hots = []
    for r in range(rows):
        names = jnp.zeros((cols, width), jnp.int32)
        for c in range(cols):
            names = jnp.where(side == c, ids_smem[r, c], names)
        hots.append((names == lane).astype(F32))
    sums = []
    for s in range(sizings):
        total = jnp.zeros((cols, width), F32)
        for r in range(rows):
            at = s * many + r * cols
            total = total + hots[r] * jnp.sum(load[at : at + cols, :], axis=1, keepdims=True)
        sums.append(jnp.sum(total, axis=0, keepdims=True))
    height = sizings * count // 128
    meta = meta_rows(types, ids, many, pay.shape[1] - height)
    whole = jnp.concatenate([pack(jnp.concatenate(sums, axis=0), count), meta], axis=0)
    send_all(pay, whole)


def send_all(pay, whole):
    rows = whole.reshape(pay.shape[1:])

    def copy(d, carry):
        pay[d] = rows
        return carry

    lax.fori_loop(0, pay.shape[0], copy, 0, unroll=4)


def blocks_kernel(dims, load, blocks):
    sizings, rows, cols, nodes, count = dims
    many = rows * cols

    def step(r, carry):
        for c in range(cols):
            b = r * cols + c
            at = pl.ds(pl.multiple_of(b * sizings, sizings), sizings)
            blocks[at, :] = load[pl.ds(b, sizings, stride=many), :]
        return carry

    lax.fori_loop(0, rows, step, 0)


def weights_kernel(library, strap, after, stacked, low, row_sums):
    kinds, nodes, _ = library.shape
    eye = iota((nodes, nodes), 0) == iota((nodes, nodes), 1)
    couple_row = 2.0 * strap[0:1, :] + 2.0 * strap[1:2, :]
    couple_col = jnp.sum(jnp.where(eye, couple_row, 0.0), axis=1, keepdims=True)

    def step(t, carry):
        block = library[t]
        on = jnp.where(eye, block, 0.0)
        inv_row = 1.0 / (jnp.sum(on, axis=0, keepdims=True) + couple_row)
        inv_col = 1.0 / (jnp.sum(on, axis=1, keepdims=True) + couple_col)
        off = jnp.where(eye, 0.0, -block)
        once = inv_col * off * inv_row
        twice = jnp.dot(once, off, precision=HIGHEST, preferred_element_type=F32) * inv_row
        smoother = jnp.where(eye, inv_row, 0.0) + once + twice
        product = jnp.dot(smoother, block, precision=HIGHEST, preferred_element_type=F32)
        both = jnp.concatenate([smoother, product], axis=1)
        high = both.astype(BF16)
        stacked[t] = jnp.concatenate([high, high], axis=0)
        low[t] = (both - high.astype(F32)).astype(BF16)
        row_sums[pl.ds(t, 1), :] = jnp.sum(block, axis=0, keepdims=True)
        return carry

    lax.fori_loop(0, kinds, step, 0, unroll=True)


def sides_kernel(dims, info, blocks, row_first, row_second, first, second):
    sizings, rows, cols, nodes, count = dims
    row_odd, odd = info[5], info[6]
    for out, begin in ((first, either(odd, cols - 2, 0)), (second, either(odd, 0, cols - 2))):
        for side in range(2):
            c = begin + side
            above = pl.ds(cols + c, sizings, stride=2 * cols)
            below = pl.ds(c, sizings, stride=2 * cols)
            to = side * sizings
            out[to : to + sizings, :] = either(row_odd, row_second[above, :], row_first[above, :])
            to = ((rows + 1) * 2 + side) * sizings
            out[to : to + sizings, :] = either(row_odd, row_first[below, :], row_second[below, :])
            for r in range(rows):
                at = pl.multiple_of((r * cols + c) * sizings, sizings)
                to = ((r + 1) * 2 + side) * sizings
                out[to : to + sizings, :] = blocks[pl.ds(at, sizings), :]


def order_blocks(dims, mesh_dims, kinds, info, maps, gathered, plan, keys):
    sizings, rows, cols, nodes, count = dims
    n_row, n_col = mesh_dims
    height = sizings * count // 128
    metas = []
    for down in (-1, 0, 1):
        for right in (-1, 0, 1):
            r, c = info[7] + down, info[0] + right
            inside = (r >= 0) & (r < n_row) & (c >= 0) & (c < n_col)
            device = jnp.clip(r, 0, n_row - 1) * n_col + jnp.clip(c, 0, n_col - 1)
            meta = gathered[device, height : height + 2].reshape(2, 128)
            metas.append(meta * inside.astype(F32))
    metas = jnp.concatenate(metas, axis=1)
    shape = (metas.shape[1], maps.shape[1])
    pick = (iota(shape, 0) == maps[0:1, :]).astype(F32).astype(BF16)
    near = jnp.dot(metas.astype(BF16), pick, preferred_element_type=F32)
    near_types, near_ids = near[0:1, :], near[1:2, :]
    keys[...] = jnp.where(
        near_ids > 0.0, near_ids - 1.0 + maps[3:4, :].astype(F32), -1.0
    ).astype(jnp.int32)

    length = maps.shape[1]
    total = (rows + 4) * (cols + 4)
    before = (iota((length, length), 0) < iota((length, length), 1)).astype(F32).astype(BF16)
    upto = (iota((kinds, kinds), 0) >= iota((kinds, kinds), 1)).astype(F32).astype(BF16)
    slot = iota((plan.shape[1], length), 0).astype(F32)
    slot_row = iota((kinds, plan.shape[1]), 1).astype(F32)
    side = iota((8, length), 0)
    index = jnp.where(side == 0, iota((8, length), 1), jnp.where(side == 1, 1, 0))
    index = index.astype(F32).astype(BF16)
    orders, tile_kinds, groups = [], [], []
    for which in (1, 2):
        needed = maps[which : which + 1, :] > 0
        hot = (iota((kinds, length), 0).astype(F32) == near_types) & needed
        hot = hot.astype(F32)
        rank = jnp.dot(hot.astype(BF16), before, preferred_element_type=F32)
        tiles = jnp.floor((jnp.sum(hot, axis=1, keepdims=True) + (TILE - 1)) * (1.0 / TILE))
        tiles = jnp.broadcast_to(tiles, (kinds, 128))
        ends = jnp.dot(upto, tiles.astype(BF16), preferred_element_type=F32)
        starts = (ends - tiles)[:, :1]
        place = jnp.sum(hot * (starts * TILE + rank + 1.0), axis=0, keepdims=True) - 1.0
        hit = (slot == place).astype(F32).astype(BF16)
        found = lax.dot_general(
            index, hit, (((1,), (1,)), ((), ())), preferred_element_type=F32
        )
        orders.append(found[0:1, :] + float(total) * (1.0 - found[1:2, :]))
        kind = jnp.sum(jnp.where(slot_row >= ends[:, :1], 1.0, 0.0), axis=0, keepdims=True)
        tile_kinds.append(jnp.minimum(kind, kinds - 1.0))
        last = jnp.floor((ends[kinds - 1 : kinds, :1] + (GROUP - 1)) * (1.0 / GROUP))
        groups.append(jnp.broadcast_to(last, (1, plan.shape[1])))
    rest = jnp.zeros((2, plan.shape[1]), F32)
    whole = jnp.concatenate(orders + tile_kinds + groups + [rest], axis=0)
    plan[...] = whole.astype(jnp.int32)


def sorted_products(plan, which, source, stacked, low, sizings, store):
    def step(it, carry):
        for one in range(GROUP):
            tile = it * GROUP + one
            kind = plan[2 + which, tile]
            places = [
                pl.ds(pl.multiple_of(plan[which, tile * TILE + j] * sizings, sizings), sizings)
                for j in range(TILE)
            ]
            field = jnp.concatenate([source[place, :] for place in places], axis=0)
            high = field.astype(BF16)
            rest = (field - high.astype(F32)).astype(BF16)
            out = jnp.dot(
                jnp.concatenate([high, rest], axis=1), stacked[kind], preferred_element_type=F32
            ) + jnp.dot(high, low[kind], preferred_element_type=F32)
            store(kind, places, out)
        return carry

    lax.fori_loop(0, plan[4 + which, 0], step, 0)


def neighbour_ids(ids, cols):
    height, many = ids.shape
    lane, row = iota(ids.shape, 1), iota(ids.shape, 0)
    down = pltpu.roll(ids, many - cols, 1)
    south = jnp.where(lane < many - cols, down, pltpu.roll(down, height - 1, 0))
    south = jnp.where((lane >= many - cols) & (row == height - 1), -1.0, south)
    up = pltpu.roll(ids, cols, 1)
    north = jnp.where(lane >= cols, up, pltpu.roll(up, 1, 0))
    north = jnp.where((lane < cols) & (row == 0), -1.0, north)
    east = jnp.where(lane % cols == cols - 1, -1.0, pltpu.roll(ids, many - 1, 1))
    west = jnp.where(lane % cols == 0, -1.0, pltpu.roll(ids, 1, 1))
    return south, north, east, west


def invert_unrolled(ref, count):
    width = ref.shape[1]
    fold = 128 // count
    lane = iota((8, width), 1) % count
    row = iota((8, width), 0)
    tile_lane = iota((8, 128), 1)
    many = count // 8
    tiles = [ref[i * 8 : (i + 1) * 8, :] for i in range(many)]

    def column(tile, k):
        place = tile_lane // count * count + k
        return jnp.concatenate(
            [
                jnp.take_along_axis(tile[:, base : base + 128], place, axis=1)
                for base in range(0, width, 128)
            ],
            axis=1,
        )

    for first in range(0, count, PANEL):
        columns = [[column(t, first + j) for t in tiles] for j in range(PANEL)]
        for j in range(0, PANEL, 2):
            k = first + j
            at, one, two = k // 8, slice(k % 8, k % 8 + 1), slice(k % 8 + 1, k % 8 + 2)
            left, right = columns[j], columns[j + 1]
            a, b, c, d = left[at][one], right[at][one], left[at][two], right[at][two]
            det = a * d - b * c
            scale = pl.reciprocal(det, approx=True)
            scale = scale * (2.0 - det * scale)
            scale = scale * (2.0 - det * scale)
            a, b, c, d = a * scale, b * scale, c * scale, d * scale

            def pivoted(upper, lower):
                return d * upper - b * lower, a * lower - c * upper

            def update(old, i, upper, lower):
                new = old - left[i] * upper - right[i] * lower
                if i == at:
                    new = jnp.where(row == k % 8, upper, new)
                    new = jnp.where(row == k % 8 + 1, lower, new)
                return new

            upper, lower = tiles[at][one], tiles[at][two]
            on, after = lane[:1] == k, lane[:1] == k + 1
            upper, lower = pivoted(
                jnp.where(on, 1.0, jnp.where(after, 0.0, upper)),
                jnp.where(on, 0.0, jnp.where(after, 1.0, lower)),
            )
            cleared = (lane == k) | (lane == k + 1)
            for i in range(many):
                tiles[i] = update(jnp.where(cleared, 0.0, tiles[i]), i, upper, lower)
            for other in columns[j + 2 :]:
                upper, lower = pivoted(other[at][one], other[at][two])
                for i in range(many):
                    other[i] = update(other[i], i, upper, lower)
    for i in range(many):
        ref[i * 8 : (i + 1) * 8, :] = tiles[i]


def invert_looped(ref, count):
    def step(k, carry):
        for base in range(0, ref.shape[1], count):
            here = slice(base, base + count)
            lane = iota((1, count), 1)
            row = iota((count, 1), 0)
            pivot_row = ref[pl.ds(k, 1), here]
            part = ref[:, here]
            column = jnp.sum(jnp.where(lane == k, part, 0.0), axis=1, keepdims=True)
            inverse = 1.0 / jnp.sum(jnp.where(lane == k, pivot_row, 0.0), axis=1, keepdims=True)
            scaled = jnp.where(lane == k, 1.0, pivot_row) * inverse
            column = jnp.where(row == k, -1.0, column)
            ref[:, here] = jnp.where((lane == k) | (row == k), 0.0, part) - column * scaled
        return carry

    lax.fori_loop(0, count, step, 0)


def coarse_matrices(dims, mesh_dims, gathered, row_sums, strap, inverses, cross):
    sizings, rows, cols, nodes, count = dims
    n_row, n_col = mesh_dims
    many = rows * cols
    height = sizings * count // 128
    kinds = row_sums.shape[0]
    north_weight = jnp.sum(strap[0:1, :], axis=1, keepdims=True)
    east_weight = jnp.sum(strap[1:2, :], axis=1, keepdims=True)
    names = iota((count, many), 0).astype(F32).astype(BF16)
    kind_names = iota((16, many), 0).astype(F32).astype(BF16)
    lane = iota((n_row, many), 1)
    eye = iota((count, count), 0) == iota((count, count), 1)
    contract = (((1,), (1,)), ((), ()))
    spot = iota((kinds, 16), 0) == iota((kinds, 16), 1)
    centre = jnp.sum(row_sums[...], axis=1, keepdims=True) + 2.0 * north_weight
    centre = centre + 2.0 * east_weight
    centre = jnp.sum(jnp.where(spot, centre, 0.0), axis=0, keepdims=True)

    def rows_of(g, at):
        return jnp.concatenate(
            [gathered[i * n_col + g, at : at + 1, 0, :] for i in range(n_row)], axis=0
        )

    def hot(values, labels):
        rows_bf = values.astype(BF16)
        one, zero = jnp.ones(labels.shape, BF16), jnp.zeros(labels.shape, BF16)
        return [
            jnp.where(labels == rows_bf[i : i + 1, :], one, zero) for i in range(n_row)
        ]

    all_ids = [rows_of(g, height + 1) - 1.0 for g in range(n_col)]
    for g in range(n_col):
        ids = all_ids[g]
        beyond = all_ids[min(g + 1, n_col - 1)]
        beyond = jnp.where(lane % cols == cols - 1, pltpu.roll(beyond, cols - 1, 1), -1.0)
        south, north, east, west = [hot(v, names) for v in neighbour_ids(ids, cols)]
        own, over = hot(ids, names), hot(beyond, names)
        types = hot(rows_of(g, height), kind_names)
        right = jnp.concatenate(
            [
                jnp.concatenate([south[i] + north[i], east[i] + west[i], over[i], types[i]], axis=0)
                for i in range(n_row)
            ],
            axis=1,
        )
        pairs = lax.dot_general(
            jnp.concatenate(own, axis=1), right, contract, preferred_element_type=F32
        )
        diagonal = jnp.sum(pairs[:, 3 * count :] * centre, axis=1, keepdims=True)
        inverses[:, g * count : (g + 1) * count] = jnp.where(eye, diagonal, 0.0) - (
            north_weight * pairs[:, :count] + east_weight * pairs[:, count : 2 * count]
        )
        cross[g] = pairs[:, 2 * count : 3 * count]


def total_of(gathered, first, height, mesh_dims, g):
    n_row, n_col = mesh_dims
    total = gathered[g, first : first + height]
    for i in range(1, n_row):
        total = total + gathered[i * n_col + g, first : first + height]
    return total.reshape(height, 128)


def coarse_solve(gathered, first, height, mesh_dims, count, sizings, inverses, g):
    sums = unpack(total_of(gathered, first, height, mesh_dims, g), count, sizings)
    solved = jnp.dot(
        sums, inverses[:, g * count : (g + 1) * count], precision=HIGHEST,
        preferred_element_type=F32,
    )
    return sums, solved


def spread(solved, info, keys, ids, out, table, dims, reach):
    sizings, rows, cols, nodes, count = dims
    wide = cols + 4
    col = info[0]
    own = solved[col + 1]
    for a in range(count):
        table[a * sizings : (a + 1) * sizings, :] = jnp.broadcast_to(
            own[:, a : a + 1], (sizings, nodes)
        )
    table[count * sizings :, :] = jnp.zeros((sizings, nodes), F32)

    def row(er, carry):
        for ec in range(2, cols + 2):
            e = er * wide + ec
            key = ids[0, e]
            place = jnp.where(key < 0, count, key - count) * sizings
            to = pl.ds(pl.multiple_of(e * sizings, sizings), sizings)
            out[to, :] = table[pl.ds(pl.multiple_of(place, sizings), sizings), :]
        return carry

    lax.fori_loop(2 - reach, rows + 2 + reach, row, 0)

    three = jnp.concatenate([solved[col], own, solved[col + 2]], axis=1)
    hot = (iota((3 * count, keys.shape[1]), 0) == keys[...]).astype(F32).astype(BF16)
    parts = jnp.concatenate(split3(three), axis=0)
    values = jnp.dot(parts, hot, preferred_element_type=F32)
    values = (
        values[2 * sizings : 3 * sizings] + values[sizings : 2 * sizings] + values[:sizings]
    )
    for over in range(1, reach + 1):
        for ec in (2 - over, cols + 1 + over):
            for er in range(2 - reach + over, rows + 2 + reach - over):
                e = er * wide + ec
                out[e * sizings : (e + 1) * sizings, :] = jnp.broadcast_to(
                    values[:, e : e + 1], (sizings, nodes)
                )


def coarse_kernel(
    dims, mesh_dims, kinds, info, maps, gathered, row_sums, strap,
    inverses, cross, solved, plan, keys,
):
    sizings, rows, cols, nodes, count = dims
    n_col = mesh_dims[1]
    height = sizings * count // 128
    order_blocks(dims, mesh_dims, kinds, info, maps, gathered, plan, keys)
    coarse_matrices(dims, mesh_dims, gathered, row_sums, strap, inverses, cross)
    if count <= 64:
        invert_unrolled(inverses, count)
    else:
        invert_looped(inverses, count)
    solved[0] = jnp.zeros((sizings, count), F32)
    solved[n_col + 1] = jnp.zeros((sizings, count), F32)
    for g in range(n_col):
        _, solved[g + 1] = coarse_solve(
            gathered, 0, height, mesh_dims, count, sizings, inverses, g
        )


def middle_kernel(
    dims,
    plan, info, ids, near_ids,
    solved, keys, blocks, row_first, row_second, col_first, col_second,
    stacked, low, row_sums, strap,
    z_out, q_out, u_out, au_out, pay,
    field, level, z, bz, q, u, bu, table,
):
    sizings, rows, cols, nodes, count = dims
    wide = cols + 4
    many = (rows + 4) * wide

    def at(er, ec):
        return pl.ds(pl.multiple_of((er * wide + ec) * sizings, sizings), sizings)

    row_odd, col_odd = info[5], info[6]
    span = cols * sizings
    for r in range(rows):
        to = ((r + 2) * wide + 2) * sizings
        field[to : to + span, :] = blocks[r * span : (r + 1) * span, :]
    for r in range(2):
        for c in range(cols):
            edge = pl.ds(r * cols + c, sizings, stride=2 * cols)
            one, two = row_first[edge, :], row_second[edge, :]
            to = (r * wide + 2 + c) * sizings
            field[to : to + sizings, :] = either(row_odd, two, one)
            to = ((rows + 2 + r) * wide + 2 + c) * sizings
            field[to : to + sizings, :] = either(row_odd, one, two)
    for k in range(rows + 2):
        pair = 2 * sizings
        one, two = [ref[k * pair : (k + 1) * pair, :] for ref in (col_first, col_second)]
        to = (k + 1) * wide * sizings
        field[to : to + pair, :] = either(col_odd, two, one)
        to = to + (cols + 2) * sizings
        field[to : to + pair, :] = either(col_odd, one, two)
    field[many * sizings :, :] = jnp.zeros((sizings, nodes), F32)
    level[many * sizings :, :] = jnp.zeros((sizings, nodes), F32)
    q[many * sizings :, :] = jnp.zeros((sizings, nodes), F32)
    spread(solved, info, keys, near_ids, level, table, dims, 2)

    def store_z(kind, places, out):
        sums = row_sums[pl.ds(kind, 1), :]
        for j, place in enumerate(places):
            here = level[place, :]
            z[place, :] = out[j * sizings : (j + 1) * sizings, :nodes] + here
            bz[place, :] = out[j * sizings : (j + 1) * sizings, nodes:] + sums * here

    sorted_products(plan, 0, field, stacked, low, sizings, store_z)

    north, east_strap = strap[0:1, :], strap[1:2, :]
    couple = 2.0 * north + 2.0 * east_strap

    def operator(v, bv, er, ec, row=None):
        row = row or [v[at(er, ec + j), :] for j in (-1, 0, 1)]
        image = (
            bv[at(er, ec), :]
            + couple * row[1]
            - north * (v[at(er - 1, ec), :] + v[at(er + 1, ec), :])
            - east_strap * (row[0] + row[2])
        )
        return row[1], image

    for er, flag in ((1, info[1]), (rows + 2, info[2])):
        inside = flag.astype(F32)

        def across(ec, carry):
            q[at(er, ec), :] = operator(z, bz, er, ec)[1] * inside
            return carry

        lax.fori_loop(2, cols + 2, across, 0)
    for ec, flag in ((1, info[3]), (cols + 2, info[4])):
        inside = flag.astype(F32)

        def along(er, carry):
            q[at(er, ec), :] = operator(z, bz, er, ec)[1] * inside
            return carry

        lax.fori_loop(2, rows + 2, along, 0)

    lanes = iota((sizings, max(count, 128)), 1)
    blank = jnp.zeros((sizings, nodes), F32)
    zero_sums = jnp.zeros(lanes.shape, F32)

    def first_row(r, carry):
        rz, zq, sums = carry
        line = [z[at(r + 2, 1), :], z[at(r + 2, 2), :]]
        for c in range(cols):
            line.append(z[at(r + 2, c + 3), :])
            here, image = operator(z, bz, r + 2, c + 2, line[c : c + 3])
            q[at(r + 2, c + 2), :] = image
            b = r * cols + c
            own = pl.ds(pl.multiple_of(b * sizings, sizings), sizings)
            z_out[own, :] = here
            q_out[own, :] = image
            rz = rz + blocks[own, :] * here
            zq = zq + here * image
            total = jnp.sum(image, axis=1, keepdims=True)
            sums = sums + jnp.where(lanes == ids[r, c], total, 0.0)
        return rz, zq, sums

    rz, zq, sums_q = lax.fori_loop(0, rows, first_row, (blank, blank, zero_sums))

    def store_u(kind, places, out):
        for j, place in enumerate(places):
            u[place, :] = out[j * sizings : (j + 1) * sizings, :nodes]
            bu[place, :] = out[j * sizings : (j + 1) * sizings, nodes:]

    sorted_products(plan, 1, q, stacked, low, sizings, store_u)

    def second_row(r, carry):
        qu, uau, sums = carry
        line = [u[at(r + 2, 1), :], u[at(r + 2, 2), :]]
        for c in range(cols):
            line.append(u[at(r + 2, c + 3), :])
            here, image = operator(u, bu, r + 2, c + 2, line[c : c + 3])
            b = r * cols + c
            own = pl.ds(pl.multiple_of(b * sizings, sizings), sizings)
            u_out[own, :] = here
            au_out[own, :] = image
            qu = qu + q[at(r + 2, c + 2), :] * here
            uau = uau + here * image
            total = jnp.sum(image, axis=1, keepdims=True)
            sums = sums + jnp.where(lanes == ids[r, c], total, 0.0)
        return qu, uau, sums

    qu, uau, sums_u = lax.fori_loop(0, rows, second_row, (blank, blank, zero_sums))

    lane = iota((sizings, 128), 1)
    dots = jnp.zeros((sizings, 128), F32)
    for j, one in enumerate((rz, zq, qu, uau)):
        dots = jnp.where(lane % 4 == j, jnp.sum(one, axis=1, keepdims=True), dots)
    dots = jnp.where(lane // 4 == iota((sizings, 128), 0), dots, 0.0)
    dots = jnp.sum(dots, axis=0, keepdims=True)
    whole = jnp.concatenate([pack(sums_q, count), pack(sums_u, count), dots], axis=0)

    send_all(pay, whole)


def last_kernel(
    dims, mesh_dims,
    types, info, near_ids,
    gathered, keys, inverses, cross, z, q, u, au, blocks, row_sums, strap,
    voltage, residual,
    level, solved, table, voltage_rows, residual_rows, sems,
):
    sizings, rows, cols, nodes, count = dims
    n_row, n_col = mesh_dims
    wide = cols + 4
    many = (rows + 4) * wide
    height = sizings * count // 128
    mesh_args = (mesh_dims, count, sizings)

    solved[0] = jnp.zeros((sizings, count), F32)
    solved[n_col + 1] = jnp.zeros((sizings, count), F32)
    with_q = jnp.zeros((sizings, count), F32)
    with_u = jnp.zeros((sizings, count), F32)
    crossed = jnp.zeros((sizings, count), F32)
    before = None
    for g in range(n_col):
        sums, one = coarse_solve(gathered, 0, height, *mesh_args, inverses, g)
        solved[g + 1] = one
        image = total_of(gathered, height, height, mesh_dims, g)
        with_q = with_q + sums * one
        with_u = with_u + unpack(image, count, sizings) * one
        if before is not None:
            crossed = crossed + one * jnp.dot(
                before, cross[g - 1], precision=HIGHEST, preferred_element_type=F32
            )
        before = one
    spread(solved, info, keys, near_ids, level, table, dims, 1)

    dots = gathered[0, 2 * height]
    for d in range(1, n_row * n_col):
        dots = dots + gathered[d, 2 * height]
    lane = iota((sizings, 128), 1)
    dots = jnp.where(lane // 4 == iota((sizings, 128), 0), dots, 0.0)
    rz, zq, qu, uau = [
        jnp.sum(jnp.where(lane % 4 == j, dots, 0.0), axis=1, keepdims=True) for j in range(4)
    ]
    east_weight = jnp.sum(strap[1:2, :], axis=1, keepdims=True)
    total = functools.partial(jnp.sum, axis=1, keepdims=True)
    qw = qu + total(with_q)
    wp = uau + 2.0 * total(with_u) + total(with_q) - 2.0 * east_weight * total(crossed)
    step_1 = rz / zq
    fresh = step_1 * step_1 * qw - rz
    grown = 1.0 + fresh / rz
    step_2 = fresh / (grown * grown * zq - 2.0 * grown * step_1 * qw + step_1 * step_1 * wp)
    alpha = jnp.broadcast_to(step_1 + step_2 * grown, (sizings, nodes))
    gamma = jnp.broadcast_to(-step_2 * step_1, (sizings, nodes))

    north, east_strap = strap[0:1, :], strap[1:2, :]
    couple = 2.0 * north + 2.0 * east_strap

    span = sizings * cols
    flat_voltage = voltage_rows.reshape(rows * span, nodes)
    flat_residual = residual_rows.reshape(rows * span, nodes)

    def value(er, ec):
        at = (er * wide + ec) * sizings
        return level[pl.ds(pl.multiple_of(at, sizings), sizings), :]

    def copies(r):
        return [
            pltpu.make_async_copy(buffer.at[r], out.at[:, r], sems.at[i, r])
            for i, (buffer, out) in enumerate(((voltage_rows, voltage), (residual_rows, residual)))
        ]

    def step(r, carry):
        line = [value(r + 2, 1), value(r + 2, 2)]
        for c in range(cols):
            line.append(value(r + 2, c + 3))
            here = line[c + 1]
            own = pl.ds(pl.multiple_of((r * cols + c) * sizings, sizings), sizings)
            lift = (
                (row_sums[pl.ds(types[r, c], 1), :] + couple) * here
                - north * (value(r + 1, c + 2) + value(r + 3, c + 2))
                - east_strap * (line[c] + line[c + 2])
            )
            to = pl.ds(r * span + c, sizings, stride=cols)
            flat_voltage[to, :] = alpha * z[own, :] + gamma * (u[own, :] + here)
            flat_residual[to, :] = (
                blocks[own, :] - alpha * q[own, :] - gamma * (au[own, :] + lift)
            )
        for copy in copies(r):
            copy.start()
        return carry

    lax.fori_loop(0, rows, step, 0)
    for r in range(rows):
        for copy in copies(r):
            copy.wait()


def ring_maps(rows, cols, count):
    tall, wide = rows + 4, cols + 4
    length = -(-tall * wide // 128) * 128
    maps = np.zeros((8, length), np.int32)
    maps[0] = -1
    for er in range(tall):
        for ec in range(wide):
            e = er * wide + ec
            down = max(2 - er, er - (rows + 1), 0)
            over = max(2 - ec, ec - (cols + 1), 0)
            maps[1, e] = down + over <= 2
            maps[2, e] = down + over <= 1
            maps[3, e] = count * ((ec >= 2) + (ec >= cols + 2))
            device = 3 * ((er >= 2) + (er >= rows + 2)) + (ec >= 2) + (ec >= cols + 2)
            maps[0, e] = (device * rows + (er - 2) % rows) * cols + (ec - 2) % cols
    return maps


def call(kernel, in_specs, out_shape, scratch, cost, megabytes, **more):
    return pl.pallas_call(
        kernel,
        in_specs=in_specs,
        out_specs=more.pop("out_specs", [VMEM] * len(out_shape)),
        out_shape=out_shape,
        scratch_shapes=scratch,
        compiler_params=pltpu.CompilerParams(vmem_limit_bytes=megabytes * 1024 * 1024),
        cost_estimate=pl.CostEstimate(flops=cost, bytes_accessed=4_000_000, transcendentals=0),
        **more,
    )


def swap(payload, axis, begin):
    pairs = [(i, i + 1) for i in range(begin, lax.axis_size(axis) - 1, 2)]
    return lax.ppermute(payload, axis, pairs + [(j, i) for i, j in pairs])


def on_device(load_currents, block_library, strap_conductance, block_types, aggregate_map):
    sizings, rows, cols, nodes = load_currents.shape
    kinds = block_library.shape[0]
    n_row, n_col = lax.axis_size("row"), lax.axis_size("col")
    n_dev = n_row * n_col
    row, col = lax.axis_index("row"), lax.axis_index("col")
    count = rows * n_row // AGR * (cols // AGC)
    dims, mesh_dims = (sizings, rows, cols, nodes, count), (n_row, n_col)
    block_rows = rows * cols * sizings
    many = (rows + 4) * (cols + 4)
    height = sizings * count // 128
    shape = jax.ShapeDtypeStruct
    own = shape((block_rows, nodes), F32)

    info = jnp.stack(
        [
            col,
            (row > 0).astype(jnp.int32),
            (row < n_row - 1).astype(jnp.int32),
            (col > 0).astype(jnp.int32),
            (col < n_col - 1).astype(jnp.int32),
            row % 2,
            col % 2,
            row,
        ]
    )
    begin = (rows - 2) * (1 - row % 2)
    first = lax.dynamic_slice_in_dim(load_currents, begin, 2, axis=1)
    second = lax.dynamic_slice_in_dim(load_currents, rows - 2 - begin, 2, axis=1)
    row_first = swap(first.reshape(-1, nodes), "row", 0)
    row_second = swap(second.reshape(-1, nodes), "row", 1)

    pay_rows = height + 2
    flat_load = load_currents.reshape(-1, nodes)
    (pay,) = call(
        functools.partial(sums_kernel, dims),
        [SMEM] + [VMEM] * 3,
        [shape((n_dev, pay_rows, 1, 128), F32)],
        [],
        20_000_000_000,
        4 if count <= 64 else 16,
    )(aggregate_map, block_types, aggregate_map, flat_load)
    gathered = lax.all_to_all(pay, ("row", "col"), 0, 0)
    (blocks,) = call(
        functools.partial(blocks_kernel, dims), [VMEM], [own], [], 1_000_000, 4
    )(flat_load)
    side_rows = (rows + 2) * 2 * sizings
    side = shape((side_rows, nodes), F32)
    first, second = call(
        functools.partial(sides_kernel, dims),
        [SMEM] + [VMEM] * 3,
        [side, side],
        [],
        40_000_000_000,
        4,
    )(info, blocks, row_first, row_second)
    col_first, col_second = swap(first, "col", 0), swap(second, "col", 1)
    stacked, low, row_sums = call(
        weights_kernel,
        [VMEM, VMEM, pl.BlockSpec(memory_space=pl.ANY)],
        [
            shape((kinds, 2 * nodes, 2 * nodes), BF16),
            shape((kinds, nodes, 2 * nodes), BF16),
            shape((kinds, nodes), F32),
        ],
        [],
        1_000_000,
        8,
    )(block_library, strap_conductance, first)

    big = pltpu.VMEM(((many + 1) * sizings, nodes), F32)
    coarse_shape = (n_col + 2, sizings, count)
    table = pltpu.VMEM(((count + 1) * sizings, nodes), F32)
    maps = ring_maps(rows, cols, count)
    longest = int(max(maps[1].sum(), maps[2].sum())) + (TILE - 1) * kinds + GROUP * TILE
    longest = -(-longest // 128) * 128
    inverses, cross, solved, plan, keys = call(
        functools.partial(coarse_kernel, dims, mesh_dims, kinds),
        [SMEM] + [VMEM] * 4,
        [
            shape((count, n_col * count), F32),
            shape((n_col, count, count), F32),
            shape(coarse_shape, F32),
            shape((8, longest), jnp.int32),
            shape((1, maps.shape[1]), jnp.int32),
        ],
        [],
        10_000_000_000,
        8 if count <= 64 else 48,
    )(info, jnp.asarray(maps), gathered, row_sums, strap_conductance)
    z, q, u, au, pay = call(
        functools.partial(middle_kernel, dims),
        [SMEM] * 4 + [VMEM] * 11,
        [own] * 4 + [shape((n_dev, 2 * height + 1, 1, 128), F32)],
        [big] * 7 + [table],
        1_000_000_000,
        20 if count <= 64 else 48,
    )(
        plan, info, aggregate_map, keys,
        solved, keys, blocks, row_first, row_second, col_first, col_second,
        stacked, low, row_sums, strap_conductance,
    )
    gathered = lax.all_to_all(pay, ("row", "col"), 0, 0)
    out = shape(load_currents.shape, F32)
    row_buffer = pltpu.VMEM((rows, sizings, cols, nodes), F32)
    return call(
        functools.partial(last_kernel, dims, mesh_dims),
        [SMEM] * 3 + [VMEM] * 11,
        [out, out],
        [big, pltpu.VMEM(coarse_shape, F32), table, row_buffer, row_buffer]
        + [pltpu.SemaphoreType.DMA((2, rows))],
        1_000_000_000,
        8 if count <= 64 else 32,
        out_specs=[pl.BlockSpec(memory_space=pl.ANY)] * 2,
    )(
        block_types, info, keys,
        gathered, keys, inverses, cross, z, q, u, au, blocks, row_sums, strap_conductance,
    )


def solution(mesh):
    placed = (P(None, "row", "col", None), P(), P(), P("row", "col"), P("row", "col"))
    return jax.shard_map(
        on_device,
        mesh=mesh,
        in_specs=placed,
        out_specs=(P(None, "row", "col", None), P(None, "row", "col", None)),
        check_vma=False,
    )
```

```python
import functools

import jax
import jax.numpy as jnp
from jax import lax
from jax.experimental import pallas as pl
from jax.experimental.pallas import tpu as pltpu
from jax.sharding import PartitionSpec as P
import numpy as np

AGR = 4
AGC = 4
TILE = 8
GROUP = 4
PANEL = 8
F32 = jnp.float32
BF16 = jnp.bfloat16
HIGHEST = lax.Precision.HIGHEST
VMEM = pl.BlockSpec(memory_space=pltpu.VMEM)
SMEM = pl.BlockSpec(memory_space=pltpu.SMEM)


def iota(shape, dim):
    return lax.broadcasted_iota(jnp.int32, shape, dim)


def pack(values, count):
    if count < 128:
        fold = 128 // count
        height = values.shape[0] // fold
        return jnp.concatenate(
            [values[p * height : (p + 1) * height, :count] for p in range(fold)], axis=1
        )
    return jnp.concatenate([values[:, j : j + 128] for j in range(0, count, 128)], axis=0)


def unpack(rows, count, sizings):
    if count < 128:
        return jnp.concatenate(
            [rows[:, j : j + count] for j in range(0, 128, count)], axis=0
        )
    return jnp.concatenate(
        [rows[j : j + sizings] for j in range(0, rows.shape[0], sizings)], axis=1
    )


def split3(values):
    first = values.astype(BF16)
    rest = values - first.astype(F32)
    second = rest.astype(BF16)
    third = (rest - second.astype(F32)).astype(BF16)
    return first, second, third


def flat_row(table, many):
    rows, cols = table.shape
    repeat = (iota((cols, many), 1) % cols == iota((cols, many), 0)).astype(F32).astype(BF16)
    wide = jnp.dot(table.astype(F32).astype(BF16), repeat, preferred_element_type=F32)
    own = iota((rows, many), 1) // cols == iota((rows, many), 0)
    return jnp.sum(jnp.where(own, wide, 0.0), axis=0, keepdims=True)


def meta_rows(types, ids, many, height):
    rows = [flat_row(types[...], many), flat_row(ids[...], many) + 1.0]
    spare = [jnp.zeros((height - 2, many), F32)] if height > 2 else []
    return jnp.concatenate(rows + spare, axis=0)


def either(odd, if_even, if_odd):
    return jnp.where(odd == 1, if_odd, if_even)


def sums_kernel(dims, ids_smem, types, ids, load, pay):
    sizings, rows, cols, nodes, count = dims
    many = rows * cols
    width = max(count, 128)
    lane, side = iota((cols, width), 1), iota((cols, width), 0)
    hots = []
    for r in range(rows):
        names = jnp.zeros((cols, width), jnp.int32)
        for c in range(cols):
            names = jnp.where(side == c, ids_smem[r, c], names)
        hots.append((names == lane).astype(F32))
    sums = []
    for s in range(sizings):
        total = jnp.zeros((cols, width), F32)
        for r in range(rows):
            at = s * many + r * cols
            total = total + hots[r] * jnp.sum(load[at : at + cols, :], axis=1, keepdims=True)
        sums.append(jnp.sum(total, axis=0, keepdims=True))
    height = sizings * count // 128
    meta = meta_rows(types, ids, many, pay.shape[1] - height)
    whole = jnp.concatenate([pack(jnp.concatenate(sums, axis=0), count), meta], axis=0)
    send_all(pay, whole)


def send_all(pay, whole):
    rows = whole.reshape(pay.shape[1:])

    def copy(d, carry):
        pay[d] = rows
        return carry

    lax.fori_loop(0, pay.shape[0], copy, 0, unroll=4)


def blocks_kernel(dims, load, blocks):
    sizings, rows, cols, nodes, count = dims
    many = rows * cols

    def step(r, carry):
        for c in range(cols):
            b = r * cols + c
            at = pl.ds(pl.multiple_of(b * sizings, sizings), sizings)
            blocks[at, :] = load[pl.ds(b, sizings, stride=many), :]
        return carry

    lax.fori_loop(0, rows, step, 0)


def weights_kernel(library, strap, after, stacked, low, row_sums):
    kinds, nodes, _ = library.shape
    eye = iota((nodes, nodes), 0) == iota((nodes, nodes), 1)
    couple_row = 2.0 * strap[0:1, :] + 2.0 * strap[1:2, :]
    couple_col = jnp.sum(jnp.where(eye, couple_row, 0.0), axis=1, keepdims=True)

    def step(t, carry):
        block = library[t]
        on = jnp.where(eye, block, 0.0)
        inv_row = 1.0 / (jnp.sum(on, axis=0, keepdims=True) + couple_row)
        inv_col = 1.0 / (jnp.sum(on, axis=1, keepdims=True) + couple_col)
        off = jnp.where(eye, 0.0, -block)
        once = inv_col * off * inv_row
        twice = jnp.dot(once, off, precision=HIGHEST, preferred_element_type=F32) * inv_row
        smoother = jnp.where(eye, inv_row, 0.0) + once + twice
        product = jnp.dot(smoother, block, precision=HIGHEST, preferred_element_type=F32)
        both = jnp.concatenate([smoother, product], axis=1)
        high = both.astype(BF16)
        stacked[t] = jnp.concatenate([high, high], axis=0)
        low[t] = (both - high.astype(F32)).astype(BF16)
        row_sums[pl.ds(t, 1), :] = jnp.sum(block, axis=0, keepdims=True)
        return carry

    lax.fori_loop(0, kinds, step, 0, unroll=True)


def sides_kernel(dims, info, blocks, row_first, row_second, first, second):
    sizings, rows, cols, nodes, count = dims
    row_odd, odd = info[5], info[6]
    for out, begin in ((first, either(odd, cols - 2, 0)), (second, either(odd, 0, cols - 2))):
        for side in range(2):
            c = begin + side
            above = pl.ds(cols + c, sizings, stride=2 * cols)
            below = pl.ds(c, sizings, stride=2 * cols)
            to = side * sizings
            out[to : to + sizings, :] = either(row_odd, row_second[above, :], row_first[above, :])
            to = ((rows + 1) * 2 + side) * sizings
            out[to : to + sizings, :] = either(row_odd, row_first[below, :], row_second[below, :])
            for r in range(rows):
                at = pl.multiple_of((r * cols + c) * sizings, sizings)
                to = ((r + 1) * 2 + side) * sizings
                out[to : to + sizings, :] = blocks[pl.ds(at, sizings), :]


def order_blocks(dims, mesh_dims, kinds, info, maps, gathered, plan, keys):
    sizings, rows, cols, nodes, count = dims
    n_row, n_col = mesh_dims
    height = sizings * count // 128
    metas = []
    for down in (-1, 0, 1):
        for right in (-1, 0, 1):
            r, c = info[7] + down, info[0] + right
            inside = (r >= 0) & (r < n_row) & (c >= 0) & (c < n_col)
            device = jnp.clip(r, 0, n_row - 1) * n_col + jnp.clip(c, 0, n_col - 1)
            meta = gathered[device, height : height + 2].reshape(2, 128)
            metas.append(meta * inside.astype(F32))
    metas = jnp.concatenate(metas, axis=1)
    shape = (metas.shape[1], maps.shape[1])
    pick = (iota(shape, 0) == maps[0:1, :]).astype(F32).astype(BF16)
    near = jnp.dot(metas.astype(BF16), pick, preferred_element_type=F32)
    near_types, near_ids = near[0:1, :], near[1:2, :]
    keys[...] = jnp.where(
        near_ids > 0.0, near_ids - 1.0 + maps[3:4, :].astype(F32), -1.0
    ).astype(jnp.int32)

    length = maps.shape[1]
    total = (rows + 4) * (cols + 4)
    before = (iota((length, length), 0) < iota((length, length), 1)).astype(F32).astype(BF16)
    upto = (iota((kinds, kinds), 0) >= iota((kinds, kinds), 1)).astype(F32).astype(BF16)
    slot = iota((plan.shape[1], length), 0).astype(F32)
    slot_row = iota((kinds, plan.shape[1]), 1).astype(F32)
    side = iota((8, length), 0)
    index = jnp.where(side == 0, iota((8, length), 1), jnp.where(side == 1, 1, 0))
    index = index.astype(F32).astype(BF16)
    orders, tile_kinds, groups = [], [], []
    for which in (1, 2):
        needed = maps[which : which + 1, :] > 0
        hot = (iota((kinds, length), 0).astype(F32) == near_types) & needed
        hot = hot.astype(F32)
        rank = jnp.dot(hot.astype(BF16), before, preferred_element_type=F32)
        tiles = jnp.floor((jnp.sum(hot, axis=1, keepdims=True) + (TILE - 1)) * (1.0 / TILE))
        tiles = jnp.broadcast_to(tiles, (kinds, 128))
        ends = jnp.dot(upto, tiles.astype(BF16), preferred_element_type=F32)
        starts = (ends - tiles)[:, :1]
        place = jnp.sum(hot * (starts * TILE + rank + 1.0), axis=0, keepdims=True) - 1.0
        hit = (slot == place).astype(F32).astype(BF16)
        found = lax.dot_general(
            index, hit, (((1,), (1,)), ((), ())), preferred_element_type=F32
        )
        orders.append(found[0:1, :] + float(total) * (1.0 - found[1:2, :]))
        kind = jnp.sum(jnp.where(slot_row >= ends[:, :1], 1.0, 0.0), axis=0, keepdims=True)
        tile_kinds.append(jnp.minimum(kind, kinds - 1.0))
        last = jnp.floor((ends[kinds - 1 : kinds, :1] + (GROUP - 1)) * (1.0 / GROUP))
        groups.append(jnp.broadcast_to(last, (1, plan.shape[1])))
    rest = jnp.zeros((2, plan.shape[1]), F32)
    whole = jnp.concatenate(orders + tile_kinds + groups + [rest], axis=0)
    plan[...] = whole.astype(jnp.int32)


def sorted_products(plan, which, source, stacked, low, sizings, store):
    def step(begin, size):
        for one in range(size):
            tile = begin + one
            kind = plan[2 + which, tile]
            places = [
                pl.ds(pl.multiple_of(plan[which, tile * TILE + j] * sizings, sizings), sizings)
                for j in range(TILE)
            ]
            field = jnp.concatenate([source[place, :] for place in places], axis=0)
            high = field.astype(BF16)
            rest = (field - high.astype(F32)).astype(BF16)
            out = jnp.dot(
                jnp.concatenate([high, rest], axis=1), stacked[kind], preferred_element_type=F32
            ) + jnp.dot(high, low[kind], preferred_element_type=F32)
            store(kind, places, out)

    groups = plan[4 + which, 0]

    def double(it, carry):
        step(it * (2 * GROUP), 2 * GROUP)
        return carry

    def single(it, carry):
        step((groups - 1) * GROUP, GROUP)
        return carry

    lax.fori_loop(0, groups // 2, double, 0)
    lax.fori_loop(0, groups % 2, single, 0)


def neighbour_ids(ids, cols):
    height, many = ids.shape
    lane, row = iota(ids.shape, 1), iota(ids.shape, 0)
    down = pltpu.roll(ids, many - cols, 1)
    south = jnp.where(lane < many - cols, down, pltpu.roll(down, height - 1, 0))
    south = jnp.where((lane >= many - cols) & (row == height - 1), -1.0, south)
    up = pltpu.roll(ids, cols, 1)
    north = jnp.where(lane >= cols, up, pltpu.roll(up, 1, 0))
    north = jnp.where((lane < cols) & (row == 0), -1.0, north)
    east = jnp.where(lane % cols == cols - 1, -1.0, pltpu.roll(ids, many - 1, 1))
    west = jnp.where(lane % cols == 0, -1.0, pltpu.roll(ids, 1, 1))
    return south, north, east, west


def invert_unrolled(ref, count):
    width = ref.shape[1]
    fold = 128 // count
    lane = iota((8, width), 1) % count
    row = iota((8, width), 0)
    tile_lane = iota((8, 128), 1)
    many = count // 8
    tiles = [ref[i * 8 : (i + 1) * 8, :] for i in range(many)]

    def column(tile, k):
        place = tile_lane // count * count + k
        return jnp.concatenate(
            [
                jnp.take_along_axis(tile[:, base : base + 128], place, axis=1)
                for base in range(0, width, 128)
            ],
            axis=1,
        )

    for first in range(0, count, PANEL):
        columns = [[column(t, first + j) for t in tiles] for j in range(PANEL)]
        for j in range(0, PANEL, 2):
            k = first + j
            at, one, two = k // 8, slice(k % 8, k % 8 + 1), slice(k % 8 + 1, k % 8 + 2)
            left, right = columns[j], columns[j + 1]
            a, b, c, d = left[at][one], right[at][one], left[at][two], right[at][two]
            det = a * d - b * c
            scale = pl.reciprocal(det, approx=True)
            scale = scale * (2.0 - det * scale)
            scale = scale * (2.0 - det * scale)
            a, b, c, d = a * scale, b * scale, c * scale, d * scale

            def pivoted(upper, lower):
                return d * upper - b * lower, a * lower - c * upper

            def update(old, i, upper, lower):
                new = old - left[i] * upper - right[i] * lower
                if i == at:
                    new = jnp.where(row == k % 8, upper, new)
                    new = jnp.where(row == k % 8 + 1, lower, new)
                return new

            upper, lower = tiles[at][one], tiles[at][two]
            on, after = lane[:1] == k, lane[:1] == k + 1
            upper, lower = pivoted(
                jnp.where(on, 1.0, jnp.where(after, 0.0, upper)),
                jnp.where(on, 0.0, jnp.where(after, 1.0, lower)),
            )
            cleared = (lane == k) | (lane == k + 1)
            for i in range(many):
                tiles[i] = update(jnp.where(cleared, 0.0, tiles[i]), i, upper, lower)
            for other in columns[j + 2 :]:
                upper, lower = pivoted(other[at][one], other[at][two])
                for i in range(many):
                    other[i] = update(other[i], i, upper, lower)
    for i in range(many):
        ref[i * 8 : (i + 1) * 8, :] = tiles[i]


def invert_looped(ref, count):
    def step(k, carry):
        for base in range(0, ref.shape[1], count):
            here = slice(base, base + count)
            lane = iota((1, count), 1)
            row = iota((count, 1), 0)
            pivot_row = ref[pl.ds(k, 1), here]
            part = ref[:, here]
            column = jnp.sum(jnp.where(lane == k, part, 0.0), axis=1, keepdims=True)
            inverse = 1.0 / jnp.sum(jnp.where(lane == k, pivot_row, 0.0), axis=1, keepdims=True)
            scaled = jnp.where(lane == k, 1.0, pivot_row) * inverse
            column = jnp.where(row == k, -1.0, column)
            ref[:, here] = jnp.where((lane == k) | (row == k), 0.0, part) - column * scaled
        return carry

    lax.fori_loop(0, count, step, 0)


def coarse_matrices(dims, mesh_dims, gathered, row_sums, strap, inverses, cross):
    sizings, rows, cols, nodes, count = dims
    n_row, n_col = mesh_dims
    many = rows * cols
    height = sizings * count // 128
    kinds = row_sums.shape[0]
    north_weight = jnp.sum(strap[0:1, :], axis=1, keepdims=True)
    east_weight = jnp.sum(strap[1:2, :], axis=1, keepdims=True)
    names = iota((count, many), 0).astype(F32).astype(BF16)
    kind_names = iota((16, many), 0).astype(F32).astype(BF16)
    lane = iota((n_row, many), 1)
    eye = iota((count, count), 0) == iota((count, count), 1)
    contract = (((1,), (1,)), ((), ()))
    spot = iota((kinds, 16), 0) == iota((kinds, 16), 1)
    centre = jnp.sum(row_sums[...], axis=1, keepdims=True) + 2.0 * north_weight
    centre = centre + 2.0 * east_weight
    centre = jnp.sum(jnp.where(spot, centre, 0.0), axis=0, keepdims=True)

    def rows_of(g, at):
        return jnp.concatenate(
            [gathered[i * n_col + g, at : at + 1, 0, :] for i in range(n_row)], axis=0
        )

    def hot(values, labels):
        rows_bf = values.astype(BF16)
        one, zero = jnp.ones(labels.shape, BF16), jnp.zeros(labels.shape, BF16)
        return [
            jnp.where(labels == rows_bf[i : i + 1, :], one, zero) for i in range(n_row)
        ]

    all_ids = [rows_of(g, height + 1) - 1.0 for g in range(n_col)]
    for g in range(n_col):
        ids = all_ids[g]
        beyond = all_ids[min(g + 1, n_col - 1)]
        beyond = jnp.where(lane % cols == cols - 1, pltpu.roll(beyond, cols - 1, 1), -1.0)
        south, north, east, west = [hot(v, names) for v in neighbour_ids(ids, cols)]
        own, over = hot(ids, names), hot(beyond, names)
        types = hot(rows_of(g, height), kind_names)
        right = jnp.concatenate(
            [
                jnp.concatenate([south[i] + north[i], east[i] + west[i], over[i], types[i]], axis=0)
                for i in range(n_row)
            ],
            axis=1,
        )
        pairs = lax.dot_general(
            jnp.concatenate(own, axis=1), right, contract, preferred_element_type=F32
        )
        diagonal = jnp.sum(pairs[:, 3 * count :] * centre, axis=1, keepdims=True)
        inverses[:, g * count : (g + 1) * count] = jnp.where(eye, diagonal, 0.0) - (
            north_weight * pairs[:, :count] + east_weight * pairs[:, count : 2 * count]
        )
        cross[g] = pairs[:, 2 * count : 3 * count]


def total_of(gathered, first, height, mesh_dims, g):
    n_row, n_col = mesh_dims
    total = gathered[g, first : first + height]
    for i in range(1, n_row):
        total = total + gathered[i * n_col + g, first : first + height]
    return total.reshape(height, 128)


def coarse_solve(gathered, first, height, mesh_dims, count, sizings, inverses, g):
    sums = unpack(total_of(gathered, first, height, mesh_dims, g), count, sizings)
    solved = jnp.dot(
        sums, inverses[:, g * count : (g + 1) * count], precision=HIGHEST,
        preferred_element_type=F32,
    )
    return sums, solved


def spread(solved, info, keys, ids, out, table, dims, reach):
    sizings, rows, cols, nodes, count = dims
    wide = cols + 4
    col = info[0]
    own = solved[col + 1]
    for a in range(count):
        table[a * sizings : (a + 1) * sizings, :] = jnp.broadcast_to(
            own[:, a : a + 1], (sizings, nodes)
        )
    table[count * sizings :, :] = jnp.zeros((sizings, nodes), F32)

    def row(er, carry):
        for ec in range(2, cols + 2):
            e = er * wide + ec
            key = ids[0, e]
            place = jnp.where(key < 0, count, key - count) * sizings
            to = pl.ds(pl.multiple_of(e * sizings, sizings), sizings)
            out[to, :] = table[pl.ds(pl.multiple_of(place, sizings), sizings), :]
        return carry

    lax.fori_loop(2 - reach, rows + 2 + reach, row, 0)

    three = jnp.concatenate([solved[col], own, solved[col + 2]], axis=1)
    hot = (iota((3 * count, keys.shape[1]), 0) == keys[...]).astype(F32).astype(BF16)
    parts = jnp.concatenate(split3(three), axis=0)
    values = jnp.dot(parts, hot, preferred_element_type=F32)
    values = (
        values[2 * sizings : 3 * sizings] + values[sizings : 2 * sizings] + values[:sizings]
    )
    for over in range(1, reach + 1):
        for ec in (2 - over, cols + 1 + over):
            for er in range(2 - reach + over, rows + 2 + reach - over):
                e = er * wide + ec
                out[e * sizings : (e + 1) * sizings, :] = jnp.broadcast_to(
                    values[:, e : e + 1], (sizings, nodes)
                )


def coarse_kernel(
    dims, mesh_dims, kinds, info, maps, gathered, row_sums, strap,
    inverses, cross, solved, plan, keys,
):
    sizings, rows, cols, nodes, count = dims
    n_col = mesh_dims[1]
    height = sizings * count // 128
    order_blocks(dims, mesh_dims, kinds, info, maps, gathered, plan, keys)
    coarse_matrices(dims, mesh_dims, gathered, row_sums, strap, inverses, cross)
    if count <= 64:
        invert_unrolled(inverses, count)
    else:
        invert_looped(inverses, count)
    solved[0] = jnp.zeros((sizings, count), F32)
    solved[n_col + 1] = jnp.zeros((sizings, count), F32)
    for g in range(n_col):
        _, solved[g + 1] = coarse_solve(
            gathered, 0, height, mesh_dims, count, sizings, inverses, g
        )


def middle_kernel(
    dims,
    plan, info, ids, near_ids,
    solved, keys, blocks, row_first, row_second, col_first, col_second,
    stacked, low, row_sums, strap,
    z_out, q_out, u_out, au_out, pay,
    field, level, z, bz, q, u, bu, table,
):
    sizings, rows, cols, nodes, count = dims
    wide = cols + 4
    many = (rows + 4) * wide

    def at(er, ec):
        return pl.ds(pl.multiple_of((er * wide + ec) * sizings, sizings), sizings)

    row_odd, col_odd = info[5], info[6]
    span = cols * sizings
    for r in range(rows):
        to = ((r + 2) * wide + 2) * sizings
        field[to : to + span, :] = blocks[r * span : (r + 1) * span, :]
    for r in range(2):
        for c in range(cols):
            edge = pl.ds(r * cols + c, sizings, stride=2 * cols)
            one, two = row_first[edge, :], row_second[edge, :]
            to = (r * wide + 2 + c) * sizings
            field[to : to + sizings, :] = either(row_odd, two, one)
            to = ((rows + 2 + r) * wide + 2 + c) * sizings
            field[to : to + sizings, :] = either(row_odd, one, two)
    for k in range(rows + 2):
        pair = 2 * sizings
        one, two = [ref[k * pair : (k + 1) * pair, :] for ref in (col_first, col_second)]
        to = (k + 1) * wide * sizings
        field[to : to + pair, :] = either(col_odd, two, one)
        to = to + (cols + 2) * sizings
        field[to : to + pair, :] = either(col_odd, one, two)
    field[many * sizings :, :] = jnp.zeros((sizings, nodes), F32)
    level[many * sizings :, :] = jnp.zeros((sizings, nodes), F32)
    q[many * sizings :, :] = jnp.zeros((sizings, nodes), F32)
    spread(solved, info, keys, near_ids, level, table, dims, 2)

    def store_z(kind, places, out):
        sums = row_sums[pl.ds(kind, 1), :]
        for j, place in enumerate(places):
            here = level[place, :]
            z[place, :] = out[j * sizings : (j + 1) * sizings, :nodes] + here
            bz[place, :] = out[j * sizings : (j + 1) * sizings, nodes:] + sums * here

    sorted_products(plan, 0, field, stacked, low, sizings, store_z)

    north, east_strap = strap[0:1, :], strap[1:2, :]
    couple = 2.0 * north + 2.0 * east_strap

    def operator(v, bv, er, ec, row=None):
        row = row or [v[at(er, ec + j), :] for j in (-1, 0, 1)]
        image = (
            bv[at(er, ec), :]
            + couple * row[1]
            - north * (v[at(er - 1, ec), :] + v[at(er + 1, ec), :])
            - east_strap * (row[0] + row[2])
        )
        return row[1], image

    for er, flag in ((1, info[1]), (rows + 2, info[2])):
        inside = flag.astype(F32)

        def across(ec, carry):
            q[at(er, ec), :] = operator(z, bz, er, ec)[1] * inside
            return carry

        lax.fori_loop(2, cols + 2, across, 0)
    for ec, flag in ((1, info[3]), (cols + 2, info[4])):
        inside = flag.astype(F32)

        def along(er, carry):
            q[at(er, ec), :] = operator(z, bz, er, ec)[1] * inside
            return carry

        lax.fori_loop(2, rows + 2, along, 0)

    lanes = iota((sizings, max(count, 128)), 1)
    blank = jnp.zeros((sizings, nodes), F32)
    zero_sums = jnp.zeros(lanes.shape, F32)

    def first_row(r, carry):
        rz, zq, sums = carry
        line = [z[at(r + 2, 1), :], z[at(r + 2, 2), :]]
        for c in range(cols):
            line.append(z[at(r + 2, c + 3), :])
            here, image = operator(z, bz, r + 2, c + 2, line[c : c + 3])
            q[at(r + 2, c + 2), :] = image
            b = r * cols + c
            own = pl.ds(pl.multiple_of(b * sizings, sizings), sizings)
            z_out[own, :] = here
            q_out[own, :] = image
            rz = rz + blocks[own, :] * here
            zq = zq + here * image
            total = jnp.sum(image, axis=1, keepdims=True)
            sums = sums + jnp.where(lanes == ids[r, c], total, 0.0)
        return rz, zq, sums

    rz, zq, sums_q = lax.fori_loop(0, rows, first_row, (blank, blank, zero_sums))

    def store_u(kind, places, out):
        for j, place in enumerate(places):
            u[place, :] = out[j * sizings : (j + 1) * sizings, :nodes]
            bu[place, :] = out[j * sizings : (j + 1) * sizings, nodes:]

    sorted_products(plan, 1, q, stacked, low, sizings, store_u)

    def second_row(r, carry):
        qu, uau, sums = carry
        line = [u[at(r + 2, 1), :], u[at(r + 2, 2), :]]
        for c in range(cols):
            line.append(u[at(r + 2, c + 3), :])
            here, image = operator(u, bu, r + 2, c + 2, line[c : c + 3])
            b = r * cols + c
            own = pl.ds(pl.multiple_of(b * sizings, sizings), sizings)
            u_out[own, :] = here
            au_out[own, :] = image
            qu = qu + q[at(r + 2, c + 2), :] * here
            uau = uau + here * image
            total = jnp.sum(image, axis=1, keepdims=True)
            sums = sums + jnp.where(lanes == ids[r, c], total, 0.0)
        return qu, uau, sums

    qu, uau, sums_u = lax.fori_loop(0, rows, second_row, (blank, blank, zero_sums))

    lane = iota((sizings, 128), 1)
    dots = jnp.zeros((sizings, 128), F32)
    for j, one in enumerate((rz, zq, qu, uau)):
        dots = jnp.where(lane % 4 == j, jnp.sum(one, axis=1, keepdims=True), dots)
    dots = jnp.where(lane // 4 == iota((sizings, 128), 0), dots, 0.0)
    dots = jnp.sum(dots, axis=0, keepdims=True)
    whole = jnp.concatenate([pack(sums_q, count), pack(sums_u, count), dots], axis=0)

    send_all(pay, whole)


def last_kernel(
    dims, mesh_dims,
    types, info, near_ids,
    gathered, keys, inverses, cross, z, q, u, au, blocks, row_sums, strap,
    voltage, residual,
    level, solved, table, voltage_rows, residual_rows, sems,
):
    sizings, rows, cols, nodes, count = dims
    n_row, n_col = mesh_dims
    wide = cols + 4
    many = (rows + 4) * wide
    height = sizings * count // 128
    mesh_args = (mesh_dims, count, sizings)

    solved[0] = jnp.zeros((sizings, count), F32)
    solved[n_col + 1] = jnp.zeros((sizings, count), F32)
    with_q = jnp.zeros((sizings, count), F32)
    with_u = jnp.zeros((sizings, count), F32)
    crossed = jnp.zeros((sizings, count), F32)
    before = None
    for g in range(n_col):
        sums, one = coarse_solve(gathered, 0, height, *mesh_args, inverses, g)
        solved[g + 1] = one
        image = total_of(gathered, height, height, mesh_dims, g)
        with_q = with_q + sums * one
        with_u = with_u + unpack(image, count, sizings) * one
        if before is not None:
            crossed = crossed + one * jnp.dot(
                before, cross[g - 1], precision=HIGHEST, preferred_element_type=F32
            )
        before = one
    spread(solved, info, keys, near_ids, level, table, dims, 1)

    dots = gathered[0, 2 * height]
    for d in range(1, n_row * n_col):
        dots = dots + gathered[d, 2 * height]
    lane = iota((sizings, 128), 1)
    dots = jnp.where(lane // 4 == iota((sizings, 128), 0), dots, 0.0)
    rz, zq, qu, uau = [
        jnp.sum(jnp.where(lane % 4 == j, dots, 0.0), axis=1, keepdims=True) for j in range(4)
    ]
    east_weight = jnp.sum(strap[1:2, :], axis=1, keepdims=True)
    total = functools.partial(jnp.sum, axis=1, keepdims=True)
    qw = qu + total(with_q)
    wp = uau + 2.0 * total(with_u) + total(with_q) - 2.0 * east_weight * total(crossed)
    step_1 = rz / zq
    fresh = step_1 * step_1 * qw - rz
    grown = 1.0 + fresh / rz
    step_2 = fresh / (grown * grown * zq - 2.0 * grown * step_1 * qw + step_1 * step_1 * wp)
    alpha = jnp.broadcast_to(step_1 + step_2 * grown, (sizings, nodes))
    gamma = jnp.broadcast_to(-step_2 * step_1, (sizings, nodes))

    north, east_strap = strap[0:1, :], strap[1:2, :]
    couple = 2.0 * north + 2.0 * east_strap

    span = sizings * cols
    flat_voltage = voltage_rows.reshape(rows * span, nodes)
    flat_residual = residual_rows.reshape(rows * span, nodes)

    def value(er, ec):
        at = (er * wide + ec) * sizings
        return level[pl.ds(pl.multiple_of(at, sizings), sizings), :]

    def copies(r):
        return [
            pltpu.make_async_copy(buffer.at[r], out.at[:, r], sems.at[i, r])
            for i, (buffer, out) in enumerate(((voltage_rows, voltage), (residual_rows, residual)))
        ]

    def step(r, carry):
        line = [value(r + 2, 1), value(r + 2, 2)]
        for c in range(cols):
            line.append(value(r + 2, c + 3))
            here = line[c + 1]
            own = pl.ds(pl.multiple_of((r * cols + c) * sizings, sizings), sizings)
            lift = (
                (row_sums[pl.ds(types[r, c], 1), :] + couple) * here
                - north * (value(r + 1, c + 2) + value(r + 3, c + 2))
                - east_strap * (line[c] + line[c + 2])
            )
            to = pl.ds(r * span + c, sizings, stride=cols)
            flat_voltage[to, :] = alpha * z[own, :] + gamma * (u[own, :] + here)
            flat_residual[to, :] = (
                blocks[own, :] - alpha * q[own, :] - gamma * (au[own, :] + lift)
            )
        for copy in copies(r):
            copy.start()
        return carry

    lax.fori_loop(0, rows, step, 0)
    for r in range(rows):
        for copy in copies(r):
            copy.wait()


def ring_maps(rows, cols, count):
    tall, wide = rows + 4, cols + 4
    length = -(-tall * wide // 128) * 128
    maps = np.zeros((8, length), np.int32)
    maps[0] = -1
    for er in range(tall):
        for ec in range(wide):
            e = er * wide + ec
            down = max(2 - er, er - (rows + 1), 0)
            over = max(2 - ec, ec - (cols + 1), 0)
            maps[1, e] = down + over <= 2
            maps[2, e] = down + over <= 1
            maps[3, e] = count * ((ec >= 2) + (ec >= cols + 2))
            device = 3 * ((er >= 2) + (er >= rows + 2)) + (ec >= 2) + (ec >= cols + 2)
            maps[0, e] = (device * rows + (er - 2) % rows) * cols + (ec - 2) % cols
    return maps


def call(kernel, in_specs, out_shape, scratch, cost, megabytes, **more):
    return pl.pallas_call(
        kernel,
        in_specs=in_specs,
        out_specs=more.pop("out_specs", [VMEM] * len(out_shape)),
        out_shape=out_shape,
        scratch_shapes=scratch,
        compiler_params=pltpu.CompilerParams(vmem_limit_bytes=megabytes * 1024 * 1024),
        cost_estimate=pl.CostEstimate(flops=cost, bytes_accessed=4_000_000, transcendentals=0),
        **more,
    )


def swap(payload, axis, begin):
    pairs = [(i, i + 1) for i in range(begin, lax.axis_size(axis) - 1, 2)]
    return lax.ppermute(payload, axis, pairs + [(j, i) for i, j in pairs])


def on_device(load_currents, block_library, strap_conductance, block_types, aggregate_map):
    sizings, rows, cols, nodes = load_currents.shape
    kinds = block_library.shape[0]
    n_row, n_col = lax.axis_size("row"), lax.axis_size("col")
    n_dev = n_row * n_col
    row, col = lax.axis_index("row"), lax.axis_index("col")
    count = rows * n_row // AGR * (cols // AGC)
    dims, mesh_dims = (sizings, rows, cols, nodes, count), (n_row, n_col)
    block_rows = rows * cols * sizings
    many = (rows + 4) * (cols + 4)
    height = sizings * count // 128
    shape = jax.ShapeDtypeStruct
    own = shape((block_rows, nodes), F32)

    info = jnp.stack(
        [
            col,
            (row > 0).astype(jnp.int32),
            (row < n_row - 1).astype(jnp.int32),
            (col > 0).astype(jnp.int32),
            (col < n_col - 1).astype(jnp.int32),
            row % 2,
            col % 2,
            row,
        ]
    )
    begin = (rows - 2) * (1 - row % 2)
    first = lax.dynamic_slice_in_dim(load_currents, begin, 2, axis=1)
    second = lax.dynamic_slice_in_dim(load_currents, rows - 2 - begin, 2, axis=1)
    row_first = swap(first.reshape(-1, nodes), "row", 0)
    row_second = swap(second.reshape(-1, nodes), "row", 1)

    pay_rows = height + 2
    flat_load = load_currents.reshape(-1, nodes)
    (pay,) = call(
        functools.partial(sums_kernel, dims),
        [SMEM] + [VMEM] * 3,
        [shape((n_dev, pay_rows, 1, 128), F32)],
        [],
        20_000_000_000,
        4 if count <= 64 else 16,
    )(aggregate_map, block_types, aggregate_map, flat_load)
    gathered = lax.all_to_all(pay, ("row", "col"), 0, 0)
    (blocks,) = call(
        functools.partial(blocks_kernel, dims), [VMEM], [own], [], 1_000_000, 4
    )(flat_load)
    side_rows = (rows + 2) * 2 * sizings
    side = shape((side_rows, nodes), F32)
    first, second = call(
        functools.partial(sides_kernel, dims),
        [SMEM] + [VMEM] * 3,
        [side, side],
        [],
        40_000_000_000,
        4,
    )(info, blocks, row_first, row_second)
    col_first, col_second = swap(first, "col", 0), swap(second, "col", 1)
    stacked, low, row_sums = call(
        weights_kernel,
        [VMEM, VMEM, pl.BlockSpec(memory_space=pl.ANY)],
        [
            shape((kinds, 2 * nodes, 2 * nodes), BF16),
            shape((kinds, nodes, 2 * nodes), BF16),
            shape((kinds, nodes), F32),
        ],
        [],
        1_000_000,
        8,
    )(block_library, strap_conductance, first)

    big = pltpu.VMEM(((many + 1) * sizings, nodes), F32)
    coarse_shape = (n_col + 2, sizings, count)
    table = pltpu.VMEM(((count + 1) * sizings, nodes), F32)
    maps = ring_maps(rows, cols, count)
    longest = int(max(maps[1].sum(), maps[2].sum())) + (TILE - 1) * kinds + GROUP * TILE
    longest = -(-longest // 128) * 128
    inverses, cross, solved, plan, keys = call(
        functools.partial(coarse_kernel, dims, mesh_dims, kinds),
        [SMEM] + [VMEM] * 4,
        [
            shape((count, n_col * count), F32),
            shape((n_col, count, count), F32),
            shape(coarse_shape, F32),
            shape((8, longest), jnp.int32),
            shape((1, maps.shape[1]), jnp.int32),
        ],
        [],
        10_000_000_000,
        8 if count <= 64 else 48,
    )(info, jnp.asarray(maps), gathered, row_sums, strap_conductance)
    z, q, u, au, pay = call(
        functools.partial(middle_kernel, dims),
        [SMEM] * 4 + [VMEM] * 11,
        [own] * 4 + [shape((n_dev, 2 * height + 1, 1, 128), F32)],
        [big] * 7 + [table],
        1_000_000_000,
        20 if count <= 64 else 48,
    )(
        plan, info, aggregate_map, keys,
        solved, keys, blocks, row_first, row_second, col_first, col_second,
        stacked, low, row_sums, strap_conductance,
    )
    gathered = lax.all_to_all(pay, ("row", "col"), 0, 0)
    out = shape(load_currents.shape, F32)
    row_buffer = pltpu.VMEM((rows, sizings, cols, nodes), F32)
    return call(
        functools.partial(last_kernel, dims, mesh_dims),
        [SMEM] * 3 + [VMEM] * 11,
        [out, out],
        [big, pltpu.VMEM(coarse_shape, F32), table, row_buffer, row_buffer]
        + [pltpu.SemaphoreType.DMA((2, rows))],
        1_000_000_000,
        8 if count <= 64 else 32,
        out_specs=[pl.BlockSpec(memory_space=pl.ANY)] * 2,
    )(
        block_types, info, keys,
        gathered, keys, inverses, cross, z, q, u, au, blocks, row_sums, strap_conductance,
    )


def solution(mesh):
    placed = (P(None, "row", "col", None), P(), P(), P("row", "col"), P("row", "col"))
    return jax.shard_map(
        on_device,
        mesh=mesh,
        in_specs=placed,
        out_specs=(P(None, "row", "col", None), P(None, "row", "col", None)),
        check_vma=False,
    )
```

```python
import functools

import jax
import jax.numpy as jnp
from jax import lax
from jax.experimental import pallas as pl
from jax.experimental.pallas import tpu as pltpu
from jax.sharding import PartitionSpec as P
import numpy as np

AGR = 4
AGC = 4
TILE = 8
GROUP = 4
PANEL = 8
F32 = jnp.float32
BF16 = jnp.bfloat16
HIGHEST = lax.Precision.HIGHEST
VMEM = pl.BlockSpec(memory_space=pltpu.VMEM)
SMEM = pl.BlockSpec(memory_space=pltpu.SMEM)


def iota(shape, dim):
    return lax.broadcasted_iota(jnp.int32, shape, dim)


def pack(values, count):
    if count < 128:
        fold = 128 // count
        height = values.shape[0] // fold
        return jnp.concatenate(
            [values[p * height : (p + 1) * height, :count] for p in range(fold)], axis=1
        )
    return jnp.concatenate([values[:, j : j + 128] for j in range(0, count, 128)], axis=0)


def unpack(rows, count, sizings):
    if count < 128:
        return jnp.concatenate(
            [rows[:, j : j + count] for j in range(0, 128, count)], axis=0
        )
    return jnp.concatenate(
        [rows[j : j + sizings] for j in range(0, rows.shape[0], sizings)], axis=1
    )


def split3(values):
    first = values.astype(BF16)
    rest = values - first.astype(F32)
    second = rest.astype(BF16)
    third = (rest - second.astype(F32)).astype(BF16)
    return first, second, third


def flat_row(table, many):
    rows, cols = table.shape
    repeat = (iota((cols, many), 1) % cols == iota((cols, many), 0)).astype(F32).astype(BF16)
    wide = jnp.dot(table.astype(F32).astype(BF16), repeat, preferred_element_type=F32)
    own = iota((rows, many), 1) // cols == iota((rows, many), 0)
    return jnp.sum(jnp.where(own, wide, 0.0), axis=0, keepdims=True)


def meta_rows(types, ids, many, height):
    rows = [flat_row(types[...], many), flat_row(ids[...], many) + 1.0]
    spare = [jnp.zeros((height - 2, many), F32)] if height > 2 else []
    return jnp.concatenate(rows + spare, axis=0)


def either(odd, if_even, if_odd):
    return jnp.where(odd == 1, if_odd, if_even)


def sums_kernel(dims, ids_smem, types, ids, load, pay):
    sizings, rows, cols, nodes, count = dims
    many = rows * cols
    width = max(count, 128)
    lane, side = iota((cols, width), 1), iota((cols, width), 0)
    hots = []
    for r in range(rows):
        names = jnp.zeros((cols, width), jnp.int32)
        for c in range(cols):
            names = jnp.where(side == c, ids_smem[r, c], names)
        hots.append((names == lane).astype(F32))
    sums = []
    for s in range(sizings):
        total = jnp.zeros((cols, width), F32)
        for r in range(rows):
            at = s * many + r * cols
            total = total + hots[r] * jnp.sum(load[at : at + cols, :], axis=1, keepdims=True)
        sums.append(jnp.sum(total, axis=0, keepdims=True))
    height = sizings * count // 128
    meta = meta_rows(types, ids, many, pay.shape[1] - height)
    whole = jnp.concatenate([pack(jnp.concatenate(sums, axis=0), count), meta], axis=0)
    send_all(pay, whole)


def send_all(pay, whole):
    rows = whole.reshape(pay.shape[1:])

    def copy(d, carry):
        pay[d] = rows
        return carry

    lax.fori_loop(0, pay.shape[0], copy, 0, unroll=8)


def blocks_kernel(dims, load, blocks):
    sizings, rows, cols, nodes, count = dims
    many = rows * cols

    def step(r, carry):
        for c in range(cols):
            b = r * cols + c
            at = pl.ds(pl.multiple_of(b * sizings, sizings), sizings)
            blocks[at, :] = load[pl.ds(b, sizings, stride=many), :]
        return carry

    lax.fori_loop(0, rows, step, 0)


def weights_kernel(library, strap, after, stacked, low, row_sums):
    kinds, nodes, _ = library.shape
    eye = iota((nodes, nodes), 0) == iota((nodes, nodes), 1)
    couple_row = 2.0 * strap[0:1, :] + 2.0 * strap[1:2, :]
    couple_col = jnp.sum(jnp.where(eye, couple_row, 0.0), axis=1, keepdims=True)

    def step(t, carry):
        block = library[t]
        on = jnp.where(eye, block, 0.0)
        inv_row = 1.0 / (jnp.sum(on, axis=0, keepdims=True) + couple_row)
        inv_col = 1.0 / (jnp.sum(on, axis=1, keepdims=True) + couple_col)
        off = jnp.where(eye, 0.0, -block)
        once = inv_col * off * inv_row
        twice = jnp.dot(once, off, precision=HIGHEST, preferred_element_type=F32) * inv_row
        smoother = jnp.where(eye, inv_row, 0.0) + once + twice
        product = jnp.dot(smoother, block, precision=HIGHEST, preferred_element_type=F32)
        both = jnp.concatenate([smoother, product], axis=1)
        high = both.astype(BF16)
        stacked[t] = jnp.concatenate([high, high], axis=0)
        low[t] = (both - high.astype(F32)).astype(BF16)
        row_sums[pl.ds(t, 1), :] = jnp.sum(block, axis=0, keepdims=True)
        return carry

    lax.fori_loop(0, kinds, step, 0, unroll=True)


def sides_kernel(dims, info, blocks, row_first, row_second, first, second):
    sizings, rows, cols, nodes, count = dims
    row_odd, odd = info[5], info[6]
    for out, begin in ((first, either(odd, cols - 2, 0)), (second, either(odd, 0, cols - 2))):
        for side in range(2):
            c = begin + side
            above = pl.ds(cols + c, sizings, stride=2 * cols)
            below = pl.ds(c, sizings, stride=2 * cols)
            to = side * sizings
            out[to : to + sizings, :] = either(row_odd, row_second[above, :], row_first[above, :])
            to = ((rows + 1) * 2 + side) * sizings
            out[to : to + sizings, :] = either(row_odd, row_first[below, :], row_second[below, :])
            for r in range(rows):
                at = pl.multiple_of((r * cols + c) * sizings, sizings)
                to = ((r + 1) * 2 + side) * sizings
                out[to : to + sizings, :] = blocks[pl.ds(at, sizings), :]


def order_blocks(dims, mesh_dims, kinds, info, maps, gathered, plan, keys):
    sizings, rows, cols, nodes, count = dims
    n_row, n_col = mesh_dims
    height = sizings * count // 128
    metas = []
    for down in (-1, 0, 1):
        for right in (-1, 0, 1):
            r, c = info[7] + down, info[0] + right
            inside = (r >= 0) & (r < n_row) & (c >= 0) & (c < n_col)
            device = jnp.clip(r, 0, n_row - 1) * n_col + jnp.clip(c, 0, n_col - 1)
            meta = gathered[device, height : height + 2].reshape(2, 128)
            metas.append(meta * inside.astype(F32))
    metas = jnp.concatenate(metas, axis=1)
    shape = (metas.shape[1], maps.shape[1])
    pick = (iota(shape, 0) == maps[0:1, :]).astype(F32).astype(BF16)
    near = jnp.dot(metas.astype(BF16), pick, preferred_element_type=F32)
    near_types, near_ids = near[0:1, :], near[1:2, :]
    keys[...] = jnp.where(
        near_ids > 0.0, near_ids - 1.0 + maps[3:4, :].astype(F32), -1.0
    ).astype(jnp.int32)

    length = maps.shape[1]
    total = (rows + 4) * (cols + 4)
    before = (iota((length, length), 0) < iota((length, length), 1)).astype(F32).astype(BF16)
    upto = (iota((kinds, kinds), 0) >= iota((kinds, kinds), 1)).astype(F32).astype(BF16)
    slot = iota((plan.shape[1], length), 0).astype(F32)
    slot_row = iota((kinds, plan.shape[1]), 1).astype(F32)
    side = iota((8, length), 0)
    index = jnp.where(side == 0, iota((8, length), 1), jnp.where(side == 1, 1, 0))
    index = index.astype(F32).astype(BF16)
    orders, tile_kinds, groups = [], [], []
    for which in (1, 2):
        needed = maps[which : which + 1, :] > 0
        hot = (iota((kinds, length), 0).astype(F32) == near_types) & needed
        hot = hot.astype(F32)
        rank = jnp.dot(hot.astype(BF16), before, preferred_element_type=F32)
        tiles = jnp.floor((jnp.sum(hot, axis=1, keepdims=True) + (TILE - 1)) * (1.0 / TILE))
        tiles = jnp.broadcast_to(tiles, (kinds, 128))
        ends = jnp.dot(upto, tiles.astype(BF16), preferred_element_type=F32)
        starts = (ends - tiles)[:, :1]
        place = jnp.sum(hot * (starts * TILE + rank + 1.0), axis=0, keepdims=True) - 1.0
        hit = (slot == place).astype(F32).astype(BF16)
        found = lax.dot_general(
            index, hit, (((1,), (1,)), ((), ())), preferred_element_type=F32
        )
        orders.append(found[0:1, :] + float(total) * (1.0 - found[1:2, :]))
        kind = jnp.sum(jnp.where(slot_row >= ends[:, :1], 1.0, 0.0), axis=0, keepdims=True)
        tile_kinds.append(jnp.minimum(kind, kinds - 1.0))
        last = jnp.floor((ends[kinds - 1 : kinds, :1] + (GROUP - 1)) * (1.0 / GROUP))
        groups.append(jnp.broadcast_to(last, (1, plan.shape[1])))
    rest = jnp.zeros((2, plan.shape[1]), F32)
    whole = jnp.concatenate(orders + tile_kinds + groups + [rest], axis=0)
    plan[...] = whole.astype(jnp.int32)


def sorted_products(plan, which, source, stacked, low, sizings, store):
    def step(begin, size):
        for one in range(size):
            tile = begin + one
            kind = plan[2 + which, tile]
            places = [
                pl.ds(pl.multiple_of(plan[which, tile * TILE + j] * sizings, sizings), sizings)
                for j in range(TILE)
            ]
            field = jnp.concatenate([source[place, :] for place in places], axis=0)
            high = field.astype(BF16)
            rest = (field - high.astype(F32)).astype(BF16)
            out = jnp.dot(
                jnp.concatenate([high, rest], axis=1), stacked[kind], preferred_element_type=F32
            ) + jnp.dot(high, low[kind], preferred_element_type=F32)
            store(kind, places, out)

    groups = plan[4 + which, 0]

    def double(it, carry):
        step(it * (2 * GROUP), 2 * GROUP)
        return carry

    def single(it, carry):
        step((groups - 1) * GROUP, GROUP)
        return carry

    lax.fori_loop(0, groups // 2, double, 0)
    lax.fori_loop(0, groups % 2, single, 0)


def neighbour_ids(ids, cols):
    height, many = ids.shape
    lane, row = iota(ids.shape, 1), iota(ids.shape, 0)
    down = pltpu.roll(ids, many - cols, 1)
    south = jnp.where(lane < many - cols, down, pltpu.roll(down, height - 1, 0))
    south = jnp.where((lane >= many - cols) & (row == height - 1), -1.0, south)
    up = pltpu.roll(ids, cols, 1)
    north = jnp.where(lane >= cols, up, pltpu.roll(up, 1, 0))
    north = jnp.where((lane < cols) & (row == 0), -1.0, north)
    east = jnp.where(lane % cols == cols - 1, -1.0, pltpu.roll(ids, many - 1, 1))
    west = jnp.where(lane % cols == 0, -1.0, pltpu.roll(ids, 1, 1))
    return south, north, east, west


def invert_unrolled(ref, count):
    width = ref.shape[1]
    fold = 128 // count
    lane = iota((8, width), 1) % count
    row = iota((8, width), 0)
    tile_lane = iota((8, 128), 1)
    many = count // 8
    tiles = [ref[i * 8 : (i + 1) * 8, :] for i in range(many)]

    def column(tile, k):
        place = tile_lane // count * count + k
        return jnp.concatenate(
            [
                jnp.take_along_axis(tile[:, base : base + 128], place, axis=1)
                for base in range(0, width, 128)
            ],
            axis=1,
        )

    for first in range(0, count, PANEL):
        columns = [[column(t, first + j) for t in tiles] for j in range(PANEL)]
        for j in range(0, PANEL, 2):
            k = first + j
            at, one, two = k // 8, slice(k % 8, k % 8 + 1), slice(k % 8 + 1, k % 8 + 2)
            left, right = columns[j], columns[j + 1]
            a, b, c, d = left[at][one], right[at][one], left[at][two], right[at][two]
            det = a * d - b * c
            scale = pl.reciprocal(det, approx=True)
            scale = scale * (2.0 - det * scale)
            scale = scale * (2.0 - det * scale)
            a, b, c, d = a * scale, b * scale, c * scale, d * scale

            def pivoted(upper, lower):
                return d * upper - b * lower, a * lower - c * upper

            def update(old, i, upper, lower):
                new = old - left[i] * upper - right[i] * lower
                if i == at:
                    new = jnp.where(row == k % 8, upper, new)
                    new = jnp.where(row == k % 8 + 1, lower, new)
                return new

            upper, lower = tiles[at][one], tiles[at][two]
            on, after = lane[:1] == k, lane[:1] == k + 1
            upper, lower = pivoted(
                jnp.where(on, 1.0, jnp.where(after, 0.0, upper)),
                jnp.where(on, 0.0, jnp.where(after, 1.0, lower)),
            )
            cleared = (lane == k) | (lane == k + 1)
            for i in range(many):
                tiles[i] = update(jnp.where(cleared, 0.0, tiles[i]), i, upper, lower)
            for other in columns[j + 2 :]:
                upper, lower = pivoted(other[at][one], other[at][two])
                for i in range(many):
                    other[i] = update(other[i], i, upper, lower)
    for i in range(many):
        ref[i * 8 : (i + 1) * 8, :] = tiles[i]


def invert_looped(ref, count):
    def step(k, carry):
        for base in range(0, ref.shape[1], count):
            here = slice(base, base + count)
            lane = iota((1, count), 1)
            row = iota((count, 1), 0)
            pivot_row = ref[pl.ds(k, 1), here]
            part = ref[:, here]
            column = jnp.sum(jnp.where(lane == k, part, 0.0), axis=1, keepdims=True)
            inverse = 1.0 / jnp.sum(jnp.where(lane == k, pivot_row, 0.0), axis=1, keepdims=True)
            scaled = jnp.where(lane == k, 1.0, pivot_row) * inverse
            column = jnp.where(row == k, -1.0, column)
            ref[:, here] = jnp.where((lane == k) | (row == k), 0.0, part) - column * scaled
        return carry

    lax.fori_loop(0, count, step, 0)


def coarse_matrices(dims, mesh_dims, gathered, row_sums, strap, inverses, cross):
    sizings, rows, cols, nodes, count = dims
    n_row, n_col = mesh_dims
    many = rows * cols
    height = sizings * count // 128
    kinds = row_sums.shape[0]
    north_weight = jnp.sum(strap[0:1, :], axis=1, keepdims=True)
    east_weight = jnp.sum(strap[1:2, :], axis=1, keepdims=True)
    names = iota((count, many), 0).astype(F32).astype(BF16)
    kind_names = iota((16, many), 0).astype(F32).astype(BF16)
    lane = iota((n_row, many), 1)
    eye = iota((count, count), 0) == iota((count, count), 1)
    contract = (((1,), (1,)), ((), ()))
    spot = iota((kinds, 16), 0) == iota((kinds, 16), 1)
    centre = jnp.sum(row_sums[...], axis=1, keepdims=True) + 2.0 * north_weight
    centre = centre + 2.0 * east_weight
    centre = jnp.sum(jnp.where(spot, centre, 0.0), axis=0, keepdims=True)

    def rows_of(g, at):
        return jnp.concatenate(
            [gathered[i * n_col + g, at : at + 1, 0, :] for i in range(n_row)], axis=0
        )

    def hot(values, labels):
        rows_bf = values.astype(BF16)
        one, zero = jnp.ones(labels.shape, BF16), jnp.zeros(labels.shape, BF16)
        return [
            jnp.where(labels == rows_bf[i : i + 1, :], one, zero) for i in range(n_row)
        ]

    all_ids = [rows_of(g, height + 1) - 1.0 for g in range(n_col)]
    for g in range(n_col):
        ids = all_ids[g]
        beyond = all_ids[min(g + 1, n_col - 1)]
        beyond = jnp.where(lane % cols == cols - 1, pltpu.roll(beyond, cols - 1, 1), -1.0)
        south, north, east, west = [hot(v, names) for v in neighbour_ids(ids, cols)]
        own, over = hot(ids, names), hot(beyond, names)
        types = hot(rows_of(g, height), kind_names)
        right = jnp.concatenate(
            [
                jnp.concatenate([south[i] + north[i], east[i] + west[i], over[i], types[i]], axis=0)
                for i in range(n_row)
            ],
            axis=1,
        )
        pairs = lax.dot_general(
            jnp.concatenate(own, axis=1), right, contract, preferred_element_type=F32
        )
        diagonal = jnp.sum(pairs[:, 3 * count :] * centre, axis=1, keepdims=True)
        inverses[:, g * count : (g + 1) * count] = jnp.where(eye, diagonal, 0.0) - (
            north_weight * pairs[:, :count] + east_weight * pairs[:, count : 2 * count]
        )
        cross[g] = pairs[:, 2 * count : 3 * count]


def total_of(gathered, first, height, mesh_dims, g):
    n_row, n_col = mesh_dims
    total = gathered[g, first : first + height]
    for i in range(1, n_row):
        total = total + gathered[i * n_col + g, first : first + height]
    return total.reshape(height, 128)


def coarse_solve(gathered, first, height, mesh_dims, count, sizings, inverses, g):
    sums = unpack(total_of(gathered, first, height, mesh_dims, g), count, sizings)
    solved = jnp.dot(
        sums, inverses[:, g * count : (g + 1) * count], precision=HIGHEST,
        preferred_element_type=F32,
    )
    return sums, solved


def spread(solved, info, keys, ids, out, table, dims, reach):
    sizings, rows, cols, nodes, count = dims
    wide = cols + 4
    col = info[0]
    own = solved[col + 1]
    for a in range(count):
        table[a * sizings : (a + 1) * sizings, :] = jnp.broadcast_to(
            own[:, a : a + 1], (sizings, nodes)
        )
    table[count * sizings :, :] = jnp.zeros((sizings, nodes), F32)

    def row(er, carry):
        for ec in range(2, cols + 2):
            e = er * wide + ec
            key = ids[0, e]
            place = jnp.where(key < 0, count, key - count) * sizings
            to = pl.ds(pl.multiple_of(e * sizings, sizings), sizings)
            out[to, :] = table[pl.ds(pl.multiple_of(place, sizings), sizings), :]
        return carry

    lax.fori_loop(2 - reach, rows + 2 + reach, row, 0)

    three = jnp.concatenate([solved[col], own, solved[col + 2]], axis=1)
    hot = (iota((3 * count, keys.shape[1]), 0) == keys[...]).astype(F32).astype(BF16)
    parts = jnp.concatenate(split3(three), axis=0)
    values = jnp.dot(parts, hot, preferred_element_type=F32)
    values = (
        values[2 * sizings : 3 * sizings] + values[sizings : 2 * sizings] + values[:sizings]
    )
    for over in range(1, reach + 1):
        for ec in (2 - over, cols + 1 + over):
            for er in range(2 - reach + over, rows + 2 + reach - over):
                e = er * wide + ec
                out[e * sizings : (e + 1) * sizings, :] = jnp.broadcast_to(
                    values[:, e : e + 1], (sizings, nodes)
                )


def coarse_kernel(
    dims, mesh_dims, kinds, info, maps, gathered, row_sums, strap,
    inverses, cross, solved, plan, keys,
):
    sizings, rows, cols, nodes, count = dims
    n_col = mesh_dims[1]
    height = sizings * count // 128
    order_blocks(dims, mesh_dims, kinds, info, maps, gathered, plan, keys)
    coarse_matrices(dims, mesh_dims, gathered, row_sums, strap, inverses, cross)
    if count <= 64:
        invert_unrolled(inverses, count)
    else:
        invert_looped(inverses, count)
    solved[0] = jnp.zeros((sizings, count), F32)
    solved[n_col + 1] = jnp.zeros((sizings, count), F32)
    for g in range(n_col):
        _, solved[g + 1] = coarse_solve(
            gathered, 0, height, mesh_dims, count, sizings, inverses, g
        )


def middle_kernel(
    dims,
    plan, info, ids, near_ids,
    solved, keys, blocks, row_first, row_second, col_first, col_second,
    stacked, low, row_sums, strap,
    z_out, q_out, u_out, au_out, pay,
    field, level, z, bz, q, u, bu, table,
):
    sizings, rows, cols, nodes, count = dims
    wide = cols + 4
    many = (rows + 4) * wide

    def at(er, ec):
        return pl.ds(pl.multiple_of((er * wide + ec) * sizings, sizings), sizings)

    row_odd, col_odd = info[5], info[6]
    span = cols * sizings
    for r in range(rows):
        to = ((r + 2) * wide + 2) * sizings
        field[to : to + span, :] = blocks[r * span : (r + 1) * span, :]
    for r in range(2):
        for c in range(cols):
            edge = pl.ds(r * cols + c, sizings, stride=2 * cols)
            one, two = row_first[edge, :], row_second[edge, :]
            to = (r * wide + 2 + c) * sizings
            field[to : to + sizings, :] = either(row_odd, two, one)
            to = ((rows + 2 + r) * wide + 2 + c) * sizings
            field[to : to + sizings, :] = either(row_odd, one, two)
    for k in range(rows + 2):
        pair = 2 * sizings
        one, two = [ref[k * pair : (k + 1) * pair, :] for ref in (col_first, col_second)]
        to = (k + 1) * wide * sizings
        field[to : to + pair, :] = either(col_odd, two, one)
        to = to + (cols + 2) * sizings
        field[to : to + pair, :] = either(col_odd, one, two)
    field[many * sizings :, :] = jnp.zeros((sizings, nodes), F32)
    level[many * sizings :, :] = jnp.zeros((sizings, nodes), F32)
    q[many * sizings :, :] = jnp.zeros((sizings, nodes), F32)
    spread(solved, info, keys, near_ids, level, table, dims, 2)

    def store_z(kind, places, out):
        sums = row_sums[pl.ds(kind, 1), :]
        for j, place in enumerate(places):
            here = level[place, :]
            z[place, :] = out[j * sizings : (j + 1) * sizings, :nodes] + here
            bz[place, :] = out[j * sizings : (j + 1) * sizings, nodes:] + sums * here

    sorted_products(plan, 0, field, stacked, low, sizings, store_z)

    north, east_strap = strap[0:1, :], strap[1:2, :]
    couple = 2.0 * north + 2.0 * east_strap

    def operator(v, bv, er, ec, row=None):
        row = row or [v[at(er, ec + j), :] for j in (-1, 0, 1)]
        image = (
            bv[at(er, ec), :]
            + couple * row[1]
            - north * (v[at(er - 1, ec), :] + v[at(er + 1, ec), :])
            - east_strap * (row[0] + row[2])
        )
        return row[1], image

    for er, flag in ((1, info[1]), (rows + 2, info[2])):
        inside = flag.astype(F32)

        def across(ec, carry):
            q[at(er, ec), :] = operator(z, bz, er, ec)[1] * inside
            return carry

        lax.fori_loop(2, cols + 2, across, 0)
    for ec, flag in ((1, info[3]), (cols + 2, info[4])):
        inside = flag.astype(F32)

        def along(er, carry):
            q[at(er, ec), :] = operator(z, bz, er, ec)[1] * inside
            return carry

        lax.fori_loop(2, rows + 2, along, 0)

    lanes = iota((sizings, max(count, 128)), 1)
    blank = jnp.zeros((sizings, nodes), F32)
    zero_sums = jnp.zeros(lanes.shape, F32)

    def first_row(r, carry):
        rz, zq, sums = carry
        line = [z[at(r + 2, 1), :], z[at(r + 2, 2), :]]
        for c in range(cols):
            line.append(z[at(r + 2, c + 3), :])
            here, image = operator(z, bz, r + 2, c + 2, line[c : c + 3])
            q[at(r + 2, c + 2), :] = image
            b = r * cols + c
            own = pl.ds(pl.multiple_of(b * sizings, sizings), sizings)
            z_out[own, :] = here
            q_out[own, :] = image
            rz = rz + blocks[own, :] * here
            zq = zq + here * image
            total = jnp.sum(image, axis=1, keepdims=True)
            sums = sums + jnp.where(lanes == ids[r, c], total, 0.0)
        return rz, zq, sums

    rz, zq, sums_q = lax.fori_loop(0, rows, first_row, (blank, blank, zero_sums))

    def store_u(kind, places, out):
        for j, place in enumerate(places):
            u[place, :] = out[j * sizings : (j + 1) * sizings, :nodes]
            bu[place, :] = out[j * sizings : (j + 1) * sizings, nodes:]

    sorted_products(plan, 1, q, stacked, low, sizings, store_u)

    def second_row(r, carry):
        qu, uau, sums = carry
        line = [u[at(r + 2, 1), :], u[at(r + 2, 2), :]]
        for c in range(cols):
            line.append(u[at(r + 2, c + 3), :])
            here, image = operator(u, bu, r + 2, c + 2, line[c : c + 3])
            b = r * cols + c
            own = pl.ds(pl.multiple_of(b * sizings, sizings), sizings)
            u_out[own, :] = here
            au_out[own, :] = image
            qu = qu + q[at(r + 2, c + 2), :] * here
            uau = uau + here * image
            total = jnp.sum(image, axis=1, keepdims=True)
            sums = sums + jnp.where(lanes == ids[r, c], total, 0.0)
        return qu, uau, sums

    qu, uau, sums_u = lax.fori_loop(0, rows, second_row, (blank, blank, zero_sums))

    lane = iota((sizings, 128), 1)
    dots = jnp.zeros((sizings, 128), F32)
    for j, one in enumerate((rz, zq, qu, uau)):
        dots = jnp.where(lane % 4 == j, jnp.sum(one, axis=1, keepdims=True), dots)
    dots = jnp.where(lane // 4 == iota((sizings, 128), 0), dots, 0.0)
    dots = jnp.sum(dots, axis=0, keepdims=True)
    whole = jnp.concatenate([pack(sums_q, count), pack(sums_u, count), dots], axis=0)

    send_all(pay, whole)


def last_kernel(
    dims, mesh_dims,
    types, info, near_ids,
    gathered, keys, inverses, cross, z, q, u, au, blocks, row_sums, strap,
    voltage, residual,
    level, solved, table, voltage_rows, residual_rows, sems,
):
    sizings, rows, cols, nodes, count = dims
    n_row, n_col = mesh_dims
    wide = cols + 4
    many = (rows + 4) * wide
    height = sizings * count // 128
    mesh_args = (mesh_dims, count, sizings)

    solved[0] = jnp.zeros((sizings, count), F32)
    solved[n_col + 1] = jnp.zeros((sizings, count), F32)
    with_q = jnp.zeros((sizings, count), F32)
    with_u = jnp.zeros((sizings, count), F32)
    crossed = jnp.zeros((sizings, count), F32)
    before = None
    for g in range(n_col):
        sums, one = coarse_solve(gathered, 0, height, *mesh_args, inverses, g)
        solved[g + 1] = one
        image = total_of(gathered, height, height, mesh_dims, g)
        with_q = with_q + sums * one
        with_u = with_u + unpack(image, count, sizings) * one
        if before is not None:
            crossed = crossed + one * jnp.dot(
                before, cross[g - 1], precision=HIGHEST, preferred_element_type=F32
            )
        before = one
    spread(solved, info, keys, near_ids, level, table, dims, 1)

    dots = gathered[0, 2 * height]
    for d in range(1, n_row * n_col):
        dots = dots + gathered[d, 2 * height]
    lane = iota((sizings, 128), 1)
    dots = jnp.where(lane // 4 == iota((sizings, 128), 0), dots, 0.0)
    rz, zq, qu, uau = [
        jnp.sum(jnp.where(lane % 4 == j, dots, 0.0), axis=1, keepdims=True) for j in range(4)
    ]
    east_weight = jnp.sum(strap[1:2, :], axis=1, keepdims=True)
    total = functools.partial(jnp.sum, axis=1, keepdims=True)
    qw = qu + total(with_q)
    wp = uau + 2.0 * total(with_u) + total(with_q) - 2.0 * east_weight * total(crossed)
    step_1 = rz / zq
    fresh = step_1 * step_1 * qw - rz
    grown = 1.0 + fresh / rz
    step_2 = fresh / (grown * grown * zq - 2.0 * grown * step_1 * qw + step_1 * step_1 * wp)
    alpha = jnp.broadcast_to(step_1 + step_2 * grown, (sizings, nodes))
    gamma = jnp.broadcast_to(-step_2 * step_1, (sizings, nodes))

    north, east_strap = strap[0:1, :], strap[1:2, :]
    couple = 2.0 * north + 2.0 * east_strap

    span = sizings * cols
    flat_voltage = voltage_rows.reshape(rows * span, nodes)
    flat_residual = residual_rows.reshape(rows * span, nodes)

    def value(er, ec):
        at = (er * wide + ec) * sizings
        return level[pl.ds(pl.multiple_of(at, sizings), sizings), :]

    def copies(r):
        return [
            pltpu.make_async_copy(buffer.at[r], out.at[:, r], sems.at[i, r])
            for i, (buffer, out) in enumerate(((voltage_rows, voltage), (residual_rows, residual)))
        ]

    def step(r, carry):
        line = [value(r + 2, 1), value(r + 2, 2)]
        for c in range(cols):
            line.append(value(r + 2, c + 3))
            here = line[c + 1]
            own = pl.ds(pl.multiple_of((r * cols + c) * sizings, sizings), sizings)
            lift = (
                (row_sums[pl.ds(types[r, c], 1), :] + couple) * here
                - north * (value(r + 1, c + 2) + value(r + 3, c + 2))
                - east_strap * (line[c] + line[c + 2])
            )
            to = pl.ds(r * span + c, sizings, stride=cols)
            flat_voltage[to, :] = alpha * z[own, :] + gamma * (u[own, :] + here)
            flat_residual[to, :] = (
                blocks[own, :] - alpha * q[own, :] - gamma * (au[own, :] + lift)
            )
        for copy in copies(r):
            copy.start()
        return carry

    lax.fori_loop(0, rows, step, 0)
    for r in range(rows):
        for copy in copies(r):
            copy.wait()


def ring_maps(rows, cols, count):
    tall, wide = rows + 4, cols + 4
    length = -(-tall * wide // 128) * 128
    maps = np.zeros((8, length), np.int32)
    maps[0] = -1
    for er in range(tall):
        for ec in range(wide):
            e = er * wide + ec
            down = max(2 - er, er - (rows + 1), 0)
            over = max(2 - ec, ec - (cols + 1), 0)
            maps[1, e] = down + over <= 2
            maps[2, e] = down + over <= 1
            maps[3, e] = count * ((ec >= 2) + (ec >= cols + 2))
            device = 3 * ((er >= 2) + (er >= rows + 2)) + (ec >= 2) + (ec >= cols + 2)
            maps[0, e] = (device * rows + (er - 2) % rows) * cols + (ec - 2) % cols
    return maps


def call(kernel, in_specs, out_shape, scratch, cost, megabytes, **more):
    return pl.pallas_call(
        kernel,
        in_specs=in_specs,
        out_specs=more.pop("out_specs", [VMEM] * len(out_shape)),
        out_shape=out_shape,
        scratch_shapes=scratch,
        compiler_params=pltpu.CompilerParams(vmem_limit_bytes=megabytes * 1024 * 1024),
        cost_estimate=pl.CostEstimate(flops=cost, bytes_accessed=4_000_000, transcendentals=0),
        **more,
    )


def swap(payload, axis, begin):
    pairs = [(i, i + 1) for i in range(begin, lax.axis_size(axis) - 1, 2)]
    return lax.ppermute(payload, axis, pairs + [(j, i) for i, j in pairs])


def on_device(load_currents, block_library, strap_conductance, block_types, aggregate_map):
    sizings, rows, cols, nodes = load_currents.shape
    kinds = block_library.shape[0]
    n_row, n_col = lax.axis_size("row"), lax.axis_size("col")
    n_dev = n_row * n_col
    row, col = lax.axis_index("row"), lax.axis_index("col")
    count = rows * n_row // AGR * (cols // AGC)
    dims, mesh_dims = (sizings, rows, cols, nodes, count), (n_row, n_col)
    block_rows = rows * cols * sizings
    many = (rows + 4) * (cols + 4)
    height = sizings * count // 128
    shape = jax.ShapeDtypeStruct
    own = shape((block_rows, nodes), F32)

    info = jnp.stack(
        [
            col,
            (row > 0).astype(jnp.int32),
            (row < n_row - 1).astype(jnp.int32),
            (col > 0).astype(jnp.int32),
            (col < n_col - 1).astype(jnp.int32),
            row % 2,
            col % 2,
            row,
        ]
    )
    begin = (rows - 2) * (1 - row % 2)
    first = lax.dynamic_slice_in_dim(load_currents, begin, 2, axis=1)
    second = lax.dynamic_slice_in_dim(load_currents, rows - 2 - begin, 2, axis=1)
    row_first = swap(first.reshape(-1, nodes), "row", 0)
    row_second = swap(second.reshape(-1, nodes), "row", 1)

    pay_rows = height + 2
    flat_load = load_currents.reshape(-1, nodes)
    (pay,) = call(
        functools.partial(sums_kernel, dims),
        [SMEM] + [VMEM] * 3,
        [shape((n_dev, pay_rows, 1, 128), F32)],
        [],
        20_000_000_000,
        4 if count <= 64 else 16,
    )(aggregate_map, block_types, aggregate_map, flat_load)
    gathered = lax.all_to_all(pay, ("row", "col"), 0, 0)
    (blocks,) = call(
        functools.partial(blocks_kernel, dims), [VMEM], [own], [], 1_000_000, 4
    )(flat_load)
    side_rows = (rows + 2) * 2 * sizings
    side = shape((side_rows, nodes), F32)
    first, second = call(
        functools.partial(sides_kernel, dims),
        [SMEM] + [VMEM] * 3,
        [side, side],
        [],
        40_000_000_000,
        4,
    )(info, blocks, row_first, row_second)
    col_first, col_second = swap(first, "col", 0), swap(second, "col", 1)
    stacked, low, row_sums = call(
        weights_kernel,
        [VMEM, VMEM, pl.BlockSpec(memory_space=pl.ANY)],
        [
            shape((kinds, 2 * nodes, 2 * nodes), BF16),
            shape((kinds, nodes, 2 * nodes), BF16),
            shape((kinds, nodes), F32),
        ],
        [],
        1_000_000,
        8,
    )(block_library, strap_conductance, first)

    big = pltpu.VMEM(((many + 1) * sizings, nodes), F32)
    coarse_shape = (n_col + 2, sizings, count)
    table = pltpu.VMEM(((count + 1) * sizings, nodes), F32)
    maps = ring_maps(rows, cols, count)
    longest = int(max(maps[1].sum(), maps[2].sum())) + (TILE - 1) * kinds + GROUP * TILE
    longest = -(-longest // 128) * 128
    inverses, cross, solved, plan, keys = call(
        functools.partial(coarse_kernel, dims, mesh_dims, kinds),
        [SMEM] + [VMEM] * 4,
        [
            shape((count, n_col * count), F32),
            shape((n_col, count, count), F32),
            shape(coarse_shape, F32),
            shape((8, longest), jnp.int32),
            shape((1, maps.shape[1]), jnp.int32),
        ],
        [],
        10_000_000_000,
        8 if count <= 64 else 48,
    )(info, jnp.asarray(maps), gathered, row_sums, strap_conductance)
    z, q, u, au, pay = call(
        functools.partial(middle_kernel, dims),
        [SMEM] * 4 + [VMEM] * 11,
        [own] * 4 + [shape((n_dev, 2 * height + 1, 1, 128), F32)],
        [big] * 7 + [table],
        1_000_000_000,
        20 if count <= 64 else 48,
    )(
        plan, info, aggregate_map, keys,
        solved, keys, blocks, row_first, row_second, col_first, col_second,
        stacked, low, row_sums, strap_conductance,
    )
    gathered = lax.all_to_all(pay, ("row", "col"), 0, 0)
    out = shape(load_currents.shape, F32)
    row_buffer = pltpu.VMEM((rows, sizings, cols, nodes), F32)
    return call(
        functools.partial(last_kernel, dims, mesh_dims),
        [SMEM] * 3 + [VMEM] * 11,
        [out, out],
        [big, pltpu.VMEM(coarse_shape, F32), table, row_buffer, row_buffer]
        + [pltpu.SemaphoreType.DMA((2, rows))],
        1_000_000_000,
        8 if count <= 64 else 32,
        out_specs=[pl.BlockSpec(memory_space=pl.ANY)] * 2,
    )(
        block_types, info, keys,
        gathered, keys, inverses, cross, z, q, u, au, blocks, row_sums, strap_conductance,
    )


def solution(mesh):
    placed = (P(None, "row", "col", None), P(), P(), P("row", "col"), P("row", "col"))
    return jax.shard_map(
        on_device,
        mesh=mesh,
        in_specs=placed,
        out_specs=(P(None, "row", "col", None), P(None, "row", "col", None)),
        check_vma=False,
    )
```
